128 devices in a mesh: head: 2 (over core), blk: 32 (over x_hi, y, z), seq: 2 (over x_lo).
Axes of the slice: x: 4 (x_hi: 2, x_lo: 2; x = x_hi * 2 + x_lo), y: 4, z: 4, core: 2. Of those that a mesh axis runs over, the one named last changes fastest.
Arguments:
- inputs: bfloat16 [2, 8192, 1600], P('seq', ('head', 'blk')), may hold values from -6 to 6
- segment_ids: int32 [2, 8192], P('seq'), may hold values from 0 to 11, as said below
- out_grad: bfloat16 [2, 8192, 1600], P('seq', ('head', 'blk')), may hold values from -6 to 6
- norm_gain: float32 [1600], replicated, may hold values from 0.5 to 1.5
- w_query: bfloat16 [1600, 1600], P(('blk', 'seq'), 'head'), may hold values from -0.15625 to 0.15625
- w_key: bfloat16 [1600, 320], P(('blk', 'seq'), 'head'), may hold values from -0.15625 to 0.15625
- w_value: bfloat16 [1600, 320], P(('blk', 'seq'), 'head'), may hold values from -0.15625 to 0.15625
- w_attn_out: bfloat16 [1600, 1600], P(('blk', 'seq'), 'head'), may hold values from -0.15625 to 0.15625
- w_mamba_in: bfloat16 [1600, 6400], P(('blk', 'seq'), 'head'), may hold values from -0.15625 to 0.15625
- conv_weight: float32 [4, 3200], replicated, may hold values from -3 to 3
- conv_bias: float32 [3200], replicated, may hold values from -3 to 3
- w_select: bfloat16 [3200, 132], P(('blk', 'seq'), 'head'), may hold values from -0.21875 to 0.21875
- w_step: bfloat16 [3200, 100], P(('blk', 'seq'), 'head'), may hold values from -0.625 to 0.625
- step_bias: float32 [3200], replicated, may hold values from -6 to -2
- log_decay: float32 [16, 3200], replicated, may hold values from -4.6 to 0
- skip_gain: float32 [3200], replicated, may hold values from 0.5 to 1.5
- w_mamba_out: bfloat16 [3200, 1600], P(('blk', 'seq'), 'head'), may hold values from -0.109375 to 0.109375
- attn_gain: float32 [1600], replicated, may hold values from 0.5 to 1.5
- mamba_gain: float32 [1600], replicated, may hold values from 0.5 to 1.5
- ffn_norm_gain: float32 [1600], replicated, may hold values from 0.5 to 1.5
- w_gate: bfloat16 [1600, 5504], P(('blk', 'seq'), 'head'), may hold values from -0.15625 to 0.15625
- w_up: bfloat16 [1600, 5504], P(('blk', 'seq'), 'head'), may hold values from -0.15625 to 0.15625
- w_down: bfloat16 [5504, 1600], P(('blk', 'seq'), 'head'), may hold values from -0.078125 to 0.078125
Outputs:
- output: bfloat16 [2, 8192, 1600], P('seq', ('head', 'blk'))
- input_grad: bfloat16 [2, 8192, 1600], P('seq', ('head', 'blk'))
- grad_norm_gain: float32 [1600], replicated
- grad_query: float32 [1600, 1600], P(('blk', 'seq'), 'head')
- grad_key: float32 [1600, 320], P(('blk', 'seq'), 'head')
- grad_value: float32 [1600, 320], P(('blk', 'seq'), 'head')
- grad_attn_out: float32 [1600, 1600], P(('blk', 'seq'), 'head')
- grad_mamba_in: float32 [1600, 6400], P(('blk', 'seq'), 'head')
- grad_conv_weight: float32 [4, 3200], replicated
- grad_conv_bias: float32 [3200], replicated
- grad_select: float32 [3200, 132], P(('blk', 'seq'), 'head')
- grad_step: float32 [3200, 100], P(('blk', 'seq'), 'head')
- grad_step_bias: float32 [3200], replicated
- grad_log_decay: float32 [16, 3200], replicated
- grad_skip_gain: float32 [3200], replicated
- grad_mamba_out: float32 [3200, 1600], P(('blk', 'seq'), 'head')
- grad_attn_gain: float32 [1600], replicated
- grad_mamba_gain: float32 [1600], replicated
- grad_ffn_norm_gain: float32 [1600], replicated
- grad_gate: float32 [1600, 5504], P(('blk', 'seq'), 'head')
- grad_up: float32 [1600, 5504], P(('blk', 'seq'), 'head')
- grad_down: float32 [5504, 1600], P(('blk', 'seq'), 'head')
The draws below stay inside these ranges and needn't reach their ends.
Inputs may be any that keep to these rules, and one draw needn't show every extreme that they name: `segment_ids`: segment numbers start at 0, never fall along a sequence and rise by at most 1 from one position to the next; every sequence holds exactly 12 documents, whose lengths differ widely, and the longest of them holds at least an eighth of the sequence's positions.
All inputs are finite; a program needn't handle non-finite values.
Results may differ from the reference program's by a relative error of at most 0.018.
Values may be sent and summed in bfloat16 or wider, within the bound.
No kernel may reach another device: no remote copies, remote signals or barrier semaphores. Data moves between devices by JAX's collectives and lax.ppermute only.
A program may use at most 576 MiB of HBM per device.

```python
import math
import jax
import jax.numpy as jnp
from jax import lax

D = 1600
HEADS = 25
KV_HEADS = 5
HEAD_DIM = 64
WINDOW = 1024
INNER = 3200
STATE = 16
CONV = 4
RANK = 100
FF = 5504
LENGTH = 8192
SEQS = 2


document_count = 12


def draw_segment_ids(key, part):
    key = jax.random.fold_in(key, 7)

    def one_sequence(index):
        seq_key = jax.random.fold_in(key, index)
        power_key, big_key = jax.random.split(seq_key)
        exponents = jax.random.randint(power_key, (document_count,), 0, 6, dtype=jnp.int32)
        weights = jnp.left_shift(jnp.ones((document_count,), jnp.int32), exponents)
        largest = jax.random.randint(big_key, (), 0, document_count, dtype=jnp.int32)
        weights = jnp.where(jnp.arange(document_count, dtype=jnp.int32) == largest, 64, weights).astype(jnp.int32)
        running = jnp.cumsum(weights).astype(jnp.int32)
        total = running[-1]
        cuts = jnp.arange(1, document_count, dtype=jnp.int32) + running[:-1] * (LENGTH - document_count) // total
        positions = jnp.arange(LENGTH, dtype=jnp.int32)
        return jnp.sum((positions[:, None] >= cuts[None, :]).astype(jnp.int32), axis=1).astype(jnp.int32)
    return jax.vmap(one_sequence)(jnp.arange(SEQS, dtype=jnp.int32))


def steps_of(own_key, dims, pieces, least, high):
    def one(dim, blocks):
        heights = jax.random.uniform(jax.random.fold_in(jax.random.fold_in(own_key, 6), dim), (blocks,), jnp.float32, least / len(pieces), high / len(pieces))
        return jnp.repeat(jnp.exp(heights), dims[dim] // blocks).reshape((-1,) + (1,) * (len(dims) - dim - 1))

    loudness = one(*pieces[0])
    for cut in pieces[1:]:
        loudness = loudness * one(*cut)
    return loudness


def centred(rng, dims, spread, most, pieces=(), kind=jnp.bfloat16):
    drawn = spread * jax.random.normal(rng, dims, jnp.float32)
    if pieces:
        drawn = drawn * steps_of(rng, dims, pieces, -0.22, 0.18)
    return jnp.clip(drawn, -most, most).astype(kind)


def setup_inputs(seed: int = 0) -> dict:
    key_list = jax.random.split(jax.random.key(seed), 24)
    inputs = centred(key_list[0], (SEQS, LENGTH, D), 1.0, 6.0, ((0, 2), (1, 64)))
    segment_ids = draw_segment_ids(jax.random.fold_in(key_list[23], 71), 0)
    out_grad = centred(key_list[2], (SEQS, LENGTH, D), 1.0, 6.0, ((0, 2), (1, 64)))
    norm_gain = jnp.clip(1.0 + 0.1 * jax.random.normal(key_list[3], (D,), jnp.float32), 0.5, 1.5)
    w_query = centred(key_list[4], (D, HEADS * HEAD_DIM), D ** -0.5, 0.15625, ((0, 64), (1, 2)))
    w_key = centred(key_list[5], (D, KV_HEADS * HEAD_DIM), D ** -0.5, 0.15625, ((0, 64), (1, 2)))
    w_value = centred(key_list[6], (D, KV_HEADS * HEAD_DIM), D ** -0.5, 0.15625, ((0, 64), (1, 2)))
    w_attn_out = centred(key_list[7], (HEADS * HEAD_DIM, D), (HEADS * HEAD_DIM) ** -0.5, 0.15625, ((0, 64), (1, 2)))
    w_mamba_in = centred(key_list[8], (D, 2 * INNER), D ** -0.5, 0.15625, ((0, 64), (1, 2)))
    conv_weight = centred(key_list[9], (CONV, INNER), CONV ** -0.5, 3.0, (), jnp.float32)
    conv_bias = centred(key_list[10], (INNER,), 0.5, 3.0, (), jnp.float32)
    w_select = centred(key_list[11], (INNER, RANK + 2 * STATE), (INNER // 4) ** -0.5, 0.21875, ((0, 64), (1, 2)))
    w_step = centred(key_list[12], (INNER, RANK), RANK ** -0.5, 0.625, ((0, 64), (1, 2)))
    step_bias = jnp.clip(jax.random.uniform(key_list[13], (INNER,), jnp.float32, -6.0, -2.0), -6.0, -2.0)
    log_decay = jnp.clip(jax.random.uniform(key_list[14], (STATE, INNER), jnp.float32, -4.6, 0.0), -4.6, 0.0)
    skip_gain = jnp.clip(jax.random.uniform(key_list[15], (INNER,), jnp.float32, 0.5, 1.5), 0.5, 1.5)
    w_mamba_out = centred(key_list[16], (INNER, D), INNER ** -0.5, 0.109375, ((0, 64), (1, 2)))
    attn_gain = jnp.clip(1.0 + 0.1 * jax.random.normal(key_list[17], (D,), jnp.float32), 0.5, 1.5)
    mamba_gain = jnp.clip(1.0 + 0.1 * jax.random.normal(key_list[18], (D,), jnp.float32), 0.5, 1.5)
    ffn_norm_gain = jnp.clip(1.0 + 0.1 * jax.random.normal(key_list[19], (D,), jnp.float32), 0.5, 1.5)
    w_gate = centred(key_list[20], (D, FF), D ** -0.5, 0.15625, ((0, 64), (1, 2)))
    w_up = centred(key_list[21], (D, FF), D ** -0.5, 0.15625, ((0, 64), (1, 2)))
    w_down = centred(key_list[22], (FF, D), FF ** -0.5, 0.078125, ((0, 64), (1, 2)))
    return {"inputs": inputs, "segment_ids": segment_ids, "out_grad": out_grad, "norm_gain": norm_gain, "w_query": w_query, "w_key": w_key, "w_value": w_value, "w_attn_out": w_attn_out, "w_mamba_in": w_mamba_in, "conv_weight": conv_weight, "conv_bias": conv_bias, "w_select": w_select, "w_step": w_step, "step_bias": step_bias, "log_decay": log_decay, "skip_gain": skip_gain, "w_mamba_out": w_mamba_out, "attn_gain": attn_gain, "mamba_gain": mamba_gain, "ffn_norm_gain": ffn_norm_gain, "w_gate": w_gate, "w_up": w_up, "w_down": w_down}


@jax.custom_vjp
def low(v):
    return lax.optimization_barrier(v.astype(jnp.bfloat16)).astype(jnp.float32)

@jax.custom_vjp
def low_back(v):
    return v

def low_keep(v):
    return (low(v), None)

def low_pass(kept, grad):
    return (grad,)

def back_keep(v):
    return (v, None)

def back_low(kept, grad):
    return (low(grad),)
low.defvjp(low_keep, low_pass)
low_back.defvjp(back_keep, back_low)
EPSILON = 1e-06
HIGHEST = lax.Precision.HIGHEST

def rms_scale(values, gain):
    return values * lax.rsqrt(lax.optimization_barrier(jnp.mean(values * values, axis=-1, keepdims=True)) + EPSILON) * gain

def matmul(left, right):
    return jnp.dot(left, right, precision=HIGHEST)

def attend(queries, keys, values, segments):
    block_rows = math.gcd(LENGTH, 512)
    group_size = HEADS // KV_HEADS
    score_scale = 1.0 / math.sqrt(HEAD_DIM)
    keys_pad = jnp.concatenate([jnp.zeros((WINDOW, KV_HEADS * HEAD_DIM), jnp.float32), keys], axis=0)
    values_pad = jnp.concatenate([jnp.zeros((WINDOW, KV_HEADS * HEAD_DIM), jnp.float32), values], axis=0)
    segments_pad = jnp.concatenate([jnp.full((WINDOW,), -1, jnp.int32), segments.astype(jnp.int32)])

    def one_block(start):
        rows_now = lax.dynamic_slice_in_dim(queries, start, block_rows, 0).reshape(block_rows, KV_HEADS, group_size, HEAD_DIM)
        near_keys = lax.dynamic_slice_in_dim(keys_pad, start, WINDOW + block_rows, 0).reshape(WINDOW + block_rows, KV_HEADS, HEAD_DIM)
        near_values = lax.dynamic_slice_in_dim(values_pad, start, WINDOW + block_rows, 0).reshape(WINDOW + block_rows, KV_HEADS, HEAD_DIM)
        query_segs = lax.dynamic_slice_in_dim(segments.astype(jnp.int32), start, block_rows)
        key_segs = lax.dynamic_slice_in_dim(segments_pad, start, WINDOW + block_rows)
        scores = low_back(jnp.einsum('qkgd,skd->kgqs', rows_now, near_keys, precision=HIGHEST) * score_scale)
        gaps = (WINDOW + jnp.arange(block_rows, dtype=jnp.int32))[:, None] - jnp.arange(WINDOW + block_rows, dtype=jnp.int32)[None, :]
        allowed = (gaps >= 0) & (gaps < WINDOW) & (query_segs[:, None] == key_segs[None, :])
        masked = jnp.where(allowed[None, None], scores, -1e+30)
        weights = jax.nn.softmax(masked, axis=-1)
        result = jnp.einsum('kgqs,skd->qkgd', low(weights), near_values, precision=HIGHEST)
        return result.reshape(block_rows, HEADS * HEAD_DIM)
    starts = jnp.arange(LENGTH // block_rows, dtype=jnp.int32) * block_rows
    return lax.map(jax.checkpoint(one_block), starts).reshape(LENGTH, HEADS * HEAD_DIM)

def selective(step_size, conved, in_mat, out_mat, decay_rate):
    block_rows = math.gcd(LENGTH, 64)

    def one_token(state, members):
        step_now, conv_now, in_now, out_now = members
        state = jnp.exp(step_now[None, :] * decay_rate) * state + in_now[:, None] * (step_now * conv_now)[None, :]
        return (state, lax.optimization_barrier(jnp.sum(out_now[:, None] * state, axis=0)))

    def one_block(state, members):
        return lax.scan(one_token, state, members)
    shaped = tuple((member.reshape(LENGTH // block_rows, block_rows, member.shape[-1]) for member in (step_size, conved, in_mat, out_mat)))
    start_state = jnp.zeros((STATE, INNER), jnp.float32)
    final_state, outputs = lax.scan(jax.checkpoint(one_block), start_state, shaped)
    return outputs.reshape(LENGTH, INNER)

def conv_silu(conv_in, conv_weight, conv_bias):
    padded = jnp.concatenate([jnp.zeros((CONV - 1, INNER), jnp.float32), conv_in], axis=0)
    total_sum = conv_bias
    for tap_index in range(CONV):
        total_sum = total_sum + conv_weight[tap_index] * padded[tap_index:tap_index + LENGTH]
    return jax.nn.silu(total_sum)

def forward(params, segment_ids):
    inputs, norm_gain, w_query, w_key, w_value, w_attn_out, w_mamba_in, conv_weight, conv_bias, w_select, w_step, step_bias, log_decay, skip_gain, w_mamba_out, attn_gain, mamba_gain, ffn_norm_gain, w_gate, w_up, w_down = params
    tokens = inputs.reshape(SEQS * LENGTH, D)
    normed = low(rms_scale(tokens, norm_gain))
    queries = low_back(low(matmul(normed, w_query)))
    keys = low_back(low(matmul(normed, w_key)))
    values = low_back(low(matmul(normed, w_value)))
    mixed_in = low_back(matmul(normed, w_mamba_in))
    conv_in = low(mixed_in[:, :INNER])
    gate_z = mixed_in[:, INNER:]
    conved = low(jnp.concatenate([conv_silu(conv_in[sequence * LENGTH:(sequence + 1) * LENGTH], conv_weight, conv_bias) for sequence in range(SEQS)], axis=0))
    selected = low_back(matmul(conved, w_select))
    step_raw = low(selected[:, :RANK])
    in_mat = selected[:, RANK:RANK + STATE]
    out_mat = selected[:, RANK + STATE:]
    step_pre = low_back(matmul(step_raw, w_step.T))
    step_size = jax.nn.softplus(step_pre + step_bias)
    decay_rate = -jnp.exp(log_decay)
    head_list = []
    scan_list = []
    for sequence in range(SEQS):
        first_row = sequence * LENGTH
        last_row = first_row + LENGTH
        head_list.append(attend(queries[first_row:last_row], keys[first_row:last_row], values[first_row:last_row], segment_ids[sequence]))
        scan_list.append(selective(step_size[first_row:last_row], conved[first_row:last_row], in_mat[first_row:last_row], out_mat[first_row:last_row], decay_rate))
    heads = low_back(low(jnp.concatenate(head_list, axis=0)))
    scan_out = jnp.concatenate(scan_list, axis=0)
    gated = low((scan_out + skip_gain * conved) * jax.nn.silu(gate_z))
    attn_out = low_back(matmul(heads, w_attn_out))
    mamba_out = low_back(matmul(gated, w_mamba_out))
    hidden_mid = tokens + 0.5 * (rms_scale(attn_out, attn_gain) + rms_scale(mamba_out, mamba_gain))
    normed_two = low(rms_scale(hidden_mid, ffn_norm_gain))
    gate_val = low_back(matmul(normed_two, w_gate))
    up_val = low_back(matmul(normed_two, w_up))
    act = low(jax.nn.silu(gate_val) * up_val)
    result = hidden_mid + matmul(act, w_down)
    return result.reshape(SEQS, LENGTH, D)

def reference(inputs, segment_ids, out_grad, norm_gain, w_query, w_key, w_value, w_attn_out, w_mamba_in, conv_weight, conv_bias, w_select, w_step, step_bias, log_decay, skip_gain, w_mamba_out, attn_gain, mamba_gain, ffn_norm_gain, w_gate, w_up, w_down):
    params = tuple((member.astype(jnp.float32) for member in (inputs, norm_gain, w_query, w_key, w_value, w_attn_out, w_mamba_in, conv_weight, conv_bias, w_select, w_step, step_bias, log_decay, skip_gain, w_mamba_out, attn_gain, mamba_gain, ffn_norm_gain, w_gate, w_up, w_down)))

    def closed(*members):
        return forward(members, segment_ids)
    output, back_fn = jax.vjp(closed, *params)
    grads = back_fn(out_grad.astype(jnp.float32))
    return (output.astype(jnp.bfloat16), grads[0].astype(jnp.bfloat16), grads[1], grads[2], grads[3], grads[4], grads[5], grads[6], grads[7], grads[8], grads[9], grads[10], grads[11], grads[12], grads[13], grads[14], grads[15], grads[16], grads[17], grads[18], grads[19], grads[20])
```

```python
import functools
import math

import jax
import jax.numpy as jnp
import numpy as np
from jax import lax
from jax.experimental import pallas as pl
from jax.experimental.pallas import tpu as pltpu
from jax.sharding import Mesh
from jax.sharding import PartitionSpec as P

HEADS = 25
KV_HEADS = 5
HEAD_DIM = 64
WINDOW = 1024
RANK = 100
X_RING = ("xh", "xl")
ROWS = ("head", "xh", "y")
EVERY = ("head", "xh", "y", "z", "xl")
Y_RING = "y"
Z_RING = "z"
BLK_SEQ = ("xh", "y", "z", "xl")
HEAD_BLK = ("head", "xh", "y", "z")
EPSILON = 1e-06
LOG2_E = 1.0 / math.log(2.0)
FF_PAD = 88


def received(a, axis, d):
    n = lax.axis_size(axis)
    return lax.ppermute(a, axis, [((i + d) % n, i) for i in range(n)])


def other_core(a):
    return received(a, "head", 1)


def shifted(a, distance, axis=HEAD_BLK):
    n = lax.axis_size(axis)
    return lax.ppermute(a, axis, [(i - distance, i) for i in range(n) if 0 <= i - distance < n])


def after(value, *others):
    return lax.optimization_barrier((value, *others))[0]


def dealt(blocks, axis):
    return lax.all_to_all(blocks, axis, 0, 0, tiled=True)


def shown(a, axis):
    return dealt(jnp.broadcast_to(a[None], (lax.axis_size(axis), *a.shape)), axis)


def summed(blocks, axis):
    return jnp.sum(dealt(blocks, axis).astype(jnp.float32), axis=0)


ORDER_A = (("y", "z"), X_RING)
ORDER_B = (("xh", "z", "xl"), Y_RING)
ORDER_C = (("xh", "y", "xl"), Z_RING)


def ring_pieces(a, axis):
    half = a.shape[0] // 2
    up, down = received(a, axis, 1), received(a, axis, -1)
    return [a, up, received(up[:half], axis, 1), received(down[half:], axis, -1), down]


def in_order(pieces, axis):
    own, up, far_low, far_high, down = pieces
    me = lax.axis_index(axis)
    out = jnp.zeros((4, *own.shape), own.dtype)
    out = lax.dynamic_update_index_in_dim(out, own, me, 0)
    out = lax.dynamic_update_index_in_dim(out, up, lax.rem(me + 1, 4), 0)
    out = lax.dynamic_update_index_in_dim(out, down, lax.rem(me + 3, 4), 0)
    far = lax.rem(me + 2, 4)
    out = lax.dynamic_update_slice(out, far_low[None], (far, 0, 0))
    out = lax.dynamic_update_slice(out, far_high[None], (far, far_low.shape[0], 0))
    return out.reshape(4 * own.shape[0], own.shape[1])


def ring_whole(a, axis):
    return jnp.concatenate([a] + [received(a, axis, j) for j in (1, 2, 3)], axis=0)


def ring_in_order(a, axis):
    me = lax.axis_index(axis)
    out = jnp.zeros((4, *a.shape), a.dtype)
    for j, part in enumerate([a] + [received(a, axis, j) for j in (1, 2, 3)]):
        out = lax.dynamic_update_index_in_dim(out, part, lax.rem(me + j, 4), 0)
    return out.reshape(4 * a.shape[0], a.shape[1])


def plane(shard, order):
    return shown(shard, order[0]).reshape(16 * shard.shape[0], shard.shape[1])


def ring_sum(pieces, axis):
    own, up, far_low, far_high, down = pieces
    half = far_low.shape[0]
    low = own.dtype
    from_down, from_up = received(far_low, axis, -1), received(far_high, axis, 1)
    to_up = jnp.concatenate(
        [(up[:half].astype(jnp.float32) + from_down.astype(jnp.float32)).astype(low), up[half:]]
    )
    to_down = jnp.concatenate(
        [down[:half], (down[half:].astype(jnp.float32) + from_up.astype(jnp.float32)).astype(low)]
    )
    return (
        own.astype(jnp.float32)
        + received(to_up, axis, -1).astype(jnp.float32)
        + received(to_down, axis, 1).astype(jnp.float32)
    )


def ring_sum_whole(whole, axis):
    rows = whole.shape[0] // 4
    total = whole[:rows].astype(jnp.float32)
    for j in (1, 2, 3):
        total = total + received(whole[j * rows : (j + 1) * rows], axis, -j).astype(jnp.float32)
    return total


def plane_sum(whole, order, rows):
    return summed(to_low(whole).reshape(16, rows, whole.shape[1]), order[0])


def turned_pieces(whole, axis):
    rows = whole.shape[0] // 4
    blocks = whole.reshape(4, rows, whole.shape[1])
    me = lax.axis_index(axis)

    def block(j):
        return lax.dynamic_index_in_dim(blocks, lax.rem(me + j, 4), 0, keepdims=False)

    far = block(2)
    return [block(0), block(1), far[: rows // 2], far[rows // 2 :], block(3)]


def ring_sum_in_order(whole, axis):
    rows = whole.shape[0] // 4
    blocks = whole.reshape(4, rows, whole.shape[1])
    me = lax.axis_index(axis)
    total = 0.0
    for j in range(4):
        block = lax.dynamic_index_in_dim(blocks, lax.rem(me + j, 4), 0, keepdims=False)
        total = total + (received(block, axis, -j) if j else block).astype(jnp.float32)
    return total


def picker(order, rows):
    ring, inside = np.indices((4, 16 * rows))
    turned = lax.rem(lax.axis_index(order[1]) + jnp.asarray(ring, jnp.int32), 4)
    block, row = inside // rows, jnp.asarray(inside % rows, jnp.int32)
    if order is ORDER_A:
        xh, y, z, xl = turned // 2, block // 4, block % 4, turned % 2
    elif order is ORDER_B:
        xh, y, z, xl = block // 8, turned, block // 2 % 4, block % 2
    else:
        xh, y, z, xl = block // 8, block // 2 % 4, turned, block % 2
    return ((((xh * 4 + y) * 4 + z) * 2 + xl) * rows + row).reshape(-1)


def ff_picker(rows):
    y, x, z, row = (jnp.asarray(j, jnp.int32) for j in np.indices((4, 4, 4, rows)))
    y = lax.rem(lax.axis_index(Y_RING) + y, 4)
    x = lax.rem(lax.axis_index(X_RING) + x, 4)
    return (((((x // 2) * 4 + y) * 4 + z) * 2 + x % 2) * rows + row).reshape(-1)


def one_hot(index, rows):
    return (jnp.arange(rows, dtype=jnp.int32)[:, None] == index[None, :]).astype(jnp.bfloat16)


def piece_bounds(total):
    k = total // 8
    return [(0, 2 * k), (2 * k, 4 * k), (4 * k, 5 * k), (5 * k, 6 * k), (6 * k, 8 * k)]


def by_pieces(left, pieces):
    total = 0.0
    for (start, stop), piece in zip(piece_bounds(left.shape[1]), pieces):
        total = total + product(left[:, start:stop], piece)
    return total


def by_pieces_nt(left, pieces):
    return jnp.concatenate([product_nt(left, piece) for piece in pieces], axis=1)


def grad_pieces(left, right):
    return [to_low(product_tn(left[:, start:stop], right)) for start, stop in piece_bounds(left.shape[1])]


def to_channels(a):
    lead, width = a.shape[:-1], a.shape[-1]
    return lax.optimization_barrier(
        jnp.swapaxes(a.reshape(*lead, 2, 16, 2, width // 64), -3, -2).reshape(*lead, width)
    )


def from_channels(a):
    lead, width = a.shape[:-1], a.shape[-1]
    a = lax.optimization_barrier(a)
    return jnp.swapaxes(a.reshape(*lead, 2, 2, 16, width // 64), -3, -2).reshape(*lead, width)


def join_columns(mine, got):
    first = lax.axis_index("head") == 0
    return jnp.concatenate([jnp.where(first, mine, got), jnp.where(first, got, mine)], axis=1)


def own_tokens(both):
    rows = both.shape[0] // 2
    return join_columns(both[:rows], other_core(both[rows:]))


def own_columns(a):
    first = lax.axis_index("head") == 0
    low, high = jnp.split(a, 2, axis=1)
    mine, theirs = jnp.where(first, low, high), jnp.where(first, high, low)
    return jnp.concatenate([mine, other_core(theirs)], axis=0)


def both_tokens(a):
    return jnp.concatenate([a, other_core(a)], axis=0)


def sum_cores(both):
    rows = both.shape[0] // 2
    return both[:rows] + other_core(to_low(both[rows:])).astype(jnp.float32)


def chain_kernel(reverse, packed_ref, rate_ref, out_ref):
    rate = rate_ref[...] * LOG2_E
    count, states = packed_ref.shape[0], rate.shape[0]

    def one(k, state):
        p = count - 1 - k if reverse else k
        out_ref[p] = state
        packed = packed_ref[p].astype(jnp.float32)
        total = packed[states : states + 1] + packed[states + 1 : states + 2]
        return jnp.exp2(total * rate) * state + packed[:states]

    lax.fori_loop(0, count, one, jnp.zeros(rate.shape, jnp.float32))


def chain_carry(total_step, state, decay_rate, reverse):
    count = lax.axis_size(HEAD_BLK)
    states, channels = state.shape
    high = lax.reduce_precision(total_step, 8, 7)
    packed = jnp.concatenate([state, high[None], (total_step - high)[None]]).astype(jnp.bfloat16)

    def tiles(a):
        padded = jnp.pad(a, ((0, 0), (0, count * 128 - channels)))
        return padded.reshape(a.shape[0], count, 128).transpose(1, 0, 2)

    rate = lax.dynamic_index_in_dim(tiles(decay_rate), lax.axis_index(HEAD_BLK), 0, keepdims=False)
    chained = pl.pallas_call(
        functools.partial(chain_kernel, reverse),
        out_shape=jax.ShapeDtypeStruct((count, states, 128), jnp.float32),
    )(dealt(tiles(packed), HEAD_BLK), rate)
    got = dealt(to_low(chained), HEAD_BLK)[: channels // 128]
    return got.transpose(1, 0, 2).reshape(states, channels).astype(jnp.float32)


def sum_all(values):
    count = lax.axis_size(EVERY)
    lines = values.reshape(-1, 128)
    each = -(-lines.shape[0] // count)
    padded = jnp.pad(lines, ((0, count * each - lines.shape[0]), (0, 0)))
    mine = summed(padded.reshape(count, each, 128), EVERY)
    return shown(mine, EVERY).reshape(-1, 128)[: lines.shape[0]].reshape(values.shape)


def rms_scale(values, gain):
    return values * lax.rsqrt(jnp.mean(values * values, axis=-1, keepdims=True) + EPSILON) * gain


def to_low(values):
    return values.astype(jnp.bfloat16)


def product(left, right):
    return jnp.dot(left, right, preferred_element_type=jnp.float32)


def product_tn(left, right):
    return lax.dot_general(
        left, right, (((0,), (0,)), ((), ())), preferred_element_type=jnp.float32
    )


def product_nt(left, right):
    return lax.dot_general(
        left, right, (((1,), (1,)), ((), ())), preferred_element_type=jnp.float32
    )


def chain_combine(earlier, later):
    return (earlier[0] * later[0], later[0] * earlier[1] + later[1])


def conv_silu(padded, conv_weight, conv_bias):
    tap_count = conv_weight.shape[0]
    length = padded.shape[0] - tap_count + 1
    total_sum = conv_bias
    for tap_index in range(tap_count):
        total_sum = total_sum + conv_weight[tap_index] * padded[tap_index : tap_index + length]
    return jax.nn.silu(total_sum)


def rate_piece(step_pre, step_bias, log_decay):
    return (jax.nn.softplus(step_pre + step_bias), -jnp.exp(log_decay))


def gate_piece(scan_out, conv_values, gate_z, skip_gain):
    return (scan_out + skip_gain * conv_values) * jax.nn.silu(gate_z)


def merge_piece(tokens, attn_out, mamba_out, attn_gain, mamba_gain):
    return tokens + 0.5 * (rms_scale(attn_out, attn_gain) + rms_scale(mamba_out, mamba_gain))


def swiglu(gate_val, up_val):
    return jax.nn.silu(gate_val) * up_val


def group_scores(queries, window_keys, allowed, group_index, group_size, score_scale):
    query_part = queries[
        :, group_index * group_size * HEAD_DIM : (group_index + 1) * group_size * HEAD_DIM
    ].reshape(queries.shape[0], group_size, HEAD_DIM)
    key_part = window_keys[:, group_index * HEAD_DIM : (group_index + 1) * HEAD_DIM]
    raw_scores = (
        jnp.einsum("qgd,sd->gqs", query_part, key_part, preferred_element_type=jnp.float32)
        * score_scale
    )
    return (jnp.where(allowed[None], raw_scores, -1e30), query_part, key_part)


SCAN_TILE = 640


def scan_state_kernel(step_ref, drive_ref, in_ref, rate_ref, end_ref):
    rate = rate_ref[...] * LOG2_E
    width = rate.shape[1]

    def eight(k, state):
        base = pl.multiple_of(k * 8, 8)
        step, drive = step_ref[pl.ds(base, 8), :], drive_ref[pl.ds(base, 8), :]
        for i in range(8):
            decay = jnp.exp2(step[i : i + 1] * rate)
            in_now = jnp.tile(in_ref[base + i], (1, width // 128))
            state = decay * state + in_now * drive[i : i + 1]
        return state

    end_ref[...] = lax.fori_loop(0, step_ref.shape[0] // 8, eight, jnp.zeros(rate.shape, jnp.float32))


def scan_full_kernel(step_ref, drive_ref, in_ref, out_ref, rate_ref, start_ref, y_ref):
    rate = rate_ref[...] * LOG2_E
    width = rate.shape[1]

    def eight(k, state):
        base = pl.multiple_of(k * 8, 8)
        step, drive = step_ref[pl.ds(base, 8), :], drive_ref[pl.ds(base, 8), :]
        rows = []
        for i in range(8):
            decay = jnp.exp2(step[i : i + 1] * rate)
            in_now = jnp.tile(in_ref[base + i], (1, width // 128))
            out_now = jnp.tile(out_ref[base + i], (1, width // 128))
            state = decay * state + in_now * drive[i : i + 1]
            rows.append(jnp.sum(out_now * state, axis=0, keepdims=True))
        y_ref[pl.ds(base, 8), :] = jnp.concatenate(rows, axis=0)
        return state

    lax.fori_loop(0, step_ref.shape[0] // 8, eight, start_ref[...])


def adjoint_state_kernel(step_ref, d_scan_ref, out_ref, rate_ref, d_start_ref):
    rate = rate_ref[...] * LOG2_E
    width = rate.shape[1]
    blocks = step_ref.shape[0] // 8

    def eight(k, carry):
        base = pl.multiple_of((blocks - 1 - k) * 8, 8)
        step, d_scan = step_ref[pl.ds(base, 8), :], d_scan_ref[pl.ds(base, 8), :]
        for i in range(7, -1, -1):
            out_now = jnp.tile(out_ref[base + i], (1, width // 128))
            carry = jnp.exp2(step[i : i + 1] * rate) * (out_now * d_scan[i : i + 1] + carry)
        return carry

    d_start_ref[...] = lax.fori_loop(0, blocks, eight, jnp.zeros(rate.shape, jnp.float32))


def scan_back_kernel(
    step_ref,
    conv_ref,
    d_scan_ref,
    in_ref,
    out_ref,
    rate_ref,
    start_ref,
    d_end_ref,
    d_step_ref,
    d_conv_ref,
    d_rate_ref,
    d_in_ref,
    d_out_ref,
    states_ref,
    decays_ref,
):
    true_rate = rate_ref[...]
    rate = true_rate * LOG2_E
    width = rate.shape[1]
    tiles = width // 128
    blocks = step_ref.shape[0] // 8

    @pl.when(pl.program_id(0) == 0)
    def _():
        d_in_ref[...] = jnp.zeros(d_in_ref.shape, jnp.float32)
        d_out_ref[...] = jnp.zeros(d_out_ref.shape, jnp.float32)

    def folded(a):
        total = a[:, :128]
        for j in range(1, tiles):
            total = total + a[:, j * 128 : (j + 1) * 128]
        return total

    states_ref[0] = start_ref[...]

    def forward(k, state):
        base = pl.multiple_of(k * 8, 8)
        step, conv = step_ref[pl.ds(base, 8), :], conv_ref[pl.ds(base, 8), :]
        d_scan = d_scan_ref[pl.ds(base, 8), :]
        drive = step * conv
        for i in range(8):
            decay = jnp.exp2(step[i : i + 1] * rate)
            in_now = jnp.tile(in_ref[base + i], (1, tiles))
            state = decay * state + in_now * drive[i : i + 1]
            decays_ref[base + i] = decay
            states_ref[base + i + 1] = state
            d_out_ref[base + i] += folded(d_scan[i : i + 1] * state)
        return state

    lax.fori_loop(0, blocks, forward, start_ref[...])

    def backward(k, carried):
        carry, d_rate = carried
        base = pl.multiple_of((blocks - 1 - k) * 8, 8)
        step, conv = step_ref[pl.ds(base, 8), :], conv_ref[pl.ds(base, 8), :]
        d_scan = d_scan_ref[pl.ds(base, 8), :]
        drive = step * conv
        through_rate, through_drive = [], []
        for i in range(7, -1, -1):
            in_now = jnp.tile(in_ref[base + i], (1, tiles))
            out_now = jnp.tile(out_ref[base + i], (1, tiles))
            adjoint = out_now * d_scan[i : i + 1] + carry
            carry = decays_ref[base + i] * adjoint
            before = carry * states_ref[base + i]
            d_rate = d_rate + before * step[i : i + 1]
            through_rate.append(jnp.sum(true_rate * before, axis=0, keepdims=True))
            through_drive.append(jnp.sum(adjoint * in_now, axis=0, keepdims=True))
            d_in_ref[base + i] += folded(adjoint * drive[i : i + 1])
        by_rate = jnp.concatenate(through_rate[::-1], axis=0)
        by_drive = jnp.concatenate(through_drive[::-1], axis=0)
        d_step_ref[pl.ds(base, 8), :] = by_rate + by_drive * conv
        d_conv_ref[pl.ds(base, 8), :] = by_drive * step
        return carry, d_rate

    zero = jnp.zeros(rate.shape, jnp.float32)
    d_rate_ref[...] = lax.fori_loop(0, blocks, backward, (d_end_ref[...], zero))[1]


def scan_specs(rows, states):
    tokens = pl.BlockSpec((rows, SCAN_TILE), lambda i: (0, i))
    maps = pl.BlockSpec((rows, states, 128), lambda i: (0, 0, 0))
    state = pl.BlockSpec((states, SCAN_TILE), lambda i: (0, i))
    return tokens, maps, state


def scan_call(kernel, operands, in_kinds, outs, out_kinds, scratch=(), flops=8, exps=1):
    rows, channels = operands[0].shape
    states = 16
    kinds = dict(zip("tms", scan_specs(rows, states)))
    shapes = {"t": (rows, channels), "m": (rows, states, 128), "s": (states, channels)}
    work = rows * states * channels
    return pl.pallas_call(
        kernel,
        grid=(channels // SCAN_TILE,),
        in_specs=[kinds[k] for k in in_kinds],
        out_specs=[kinds[k] for k in out_kinds],
        out_shape=[jax.ShapeDtypeStruct(shapes[k], jnp.float32) for k in out_kinds],
        scratch_shapes=scratch,
        compiler_params=pltpu.CompilerParams(
            dimension_semantics=("arbitrary",), vmem_limit_bytes=(36 if scratch else 16) * 2**20
        ),
        cost_estimate=pl.CostEstimate(
            flops=work * flops, bytes_accessed=4 * rows * channels * 4, transcendentals=work * exps
        ),
    )(*operands)


def lanes(a):
    return jnp.broadcast_to(a[:, :, None], (*a.shape, 128))


def scan_state(step_size, drive, in_lanes, decay_rate):
    return scan_call(scan_state_kernel, (step_size, drive, in_lanes, decay_rate), "ttms", 1, "s")[0]


def scan_full(step_size, drive, in_lanes, out_lanes, decay_rate, state_in):
    operands = (step_size, drive, in_lanes, out_lanes, decay_rate, state_in)
    return scan_call(scan_full_kernel, operands, "ttmmss", 1, "t")[0]


def adjoint_state(step_size, d_scan, out_lanes, decay_rate):
    return scan_call(adjoint_state_kernel, (step_size, d_scan, out_lanes, decay_rate), "ttms", 1, "s")[0]


def scan_back(step_size, conv_values, d_scan, in_lanes, out_lanes, decay_rate, state_in, d_end):
    rows, states = step_size.shape[0], decay_rate.shape[0]
    scratch = (
        pltpu.VMEM((rows + 1, states, SCAN_TILE), jnp.float32),
        pltpu.VMEM((rows, states, SCAN_TILE), jnp.float32),
    )
    operands = (step_size, conv_values, d_scan, in_lanes, out_lanes, decay_rate, state_in, d_end)
    d_step, d_conv, d_rate, d_in, d_out = scan_call(
        scan_back_kernel, operands, "tttmmsss", 5, "ttsmm", scratch, flops=24
    )
    return d_step, d_conv, d_rate, jnp.sum(d_in, axis=-1), jnp.sum(d_out, axis=-1)


def shards(
    inputs,
    segment_ids,
    out_grad,
    norm_gain,
    w_query,
    w_key,
    w_value,
    w_attn_out,
    w_mamba_in,
    conv_weight,
    conv_bias,
    w_select,
    w_step,
    step_bias,
    log_decay,
    skip_gain,
    w_mamba_out,
    attn_gain,
    mamba_gain,
    ffn_norm_gain,
    w_gate,
    w_up,
    w_down,
):
    rows_dev, width = inputs.shape[1:]
    inner = conv_weight.shape[1]
    edge_count = conv_weight.shape[0] - 1
    rank_width = RANK
    state_width = log_decay.shape[0]
    reach_blocks = WINDOW // rows_dev
    group_size = HEADS // KV_HEADS
    score_scale = 1.0 / math.sqrt(HEAD_DIM)
    position = lax.axis_index(HEAD_BLK)
    core = lax.axis_index("head")
    first_core = core == 0
    tokens = inputs[0].astype(jnp.float32)

    conv_weight, conv_bias, step_bias, log_decay, skip_gain = (
        to_channels(v) for v in (conv_weight, conv_bias, step_bias, log_decay, skip_gain)
    )

    d_rows = w_query.shape[0]
    c_rows = w_select.shape[0]
    sel_half, step_half = w_select.shape[1], w_step.shape[1]
    mamba_in = to_channels(w_mamba_in)
    cut_a, cut_b = 1024, 2176
    plane_b = plane(mamba_in[:, cut_a:cut_b], ORDER_B)
    in_b = ring_pieces(plane_b, ORDER_B[1])
    plane_a = plane(after(mamba_in[:, :cut_a], plane_b), ORDER_A)
    in_a = ring_pieces(plane_a, ORDER_A[1])
    plane_c = plane(after(mamba_in[:, cut_b:], plane_a), ORDER_C)
    in_c = ring_pieces(plane_c, ORDER_C[1])
    select_step = jnp.pad(
        jnp.concatenate([w_select, w_step], axis=1), ((0, 0), (0, 128 - sel_half - step_half))
    )
    select_mine = shown(after(select_step, plane_c), ("xh", "xl", "y", "z")).reshape(inner, 128)
    select_got = other_core(select_mine)
    select_full = join_columns(select_mine[:, :sel_half], select_got[:, :sel_half])
    step_full = join_columns(
        select_mine[:, sel_half : sel_half + step_half], select_got[:, sel_half : sel_half + step_half]
    )

    plane_out_a = plane(after(w_mamba_out, select_mine), ORDER_A)
    mamba_out_a = in_order(ring_pieces(plane_out_a, ORDER_A[1]), ORDER_A[1])
    qkv_shard = jnp.concatenate([w_query, w_key, w_value], axis=1)
    plane_qkv = plane(after(qkv_shard, plane_out_a), ORDER_C)
    qkv_c = ring_pieces(plane_qkv, ORDER_C[1])
    plane_out_b = plane(after(w_attn_out, plane_qkv), ORDER_B)
    attn_out_b = ring_pieces(plane_out_b, ORDER_B[1])

    ff_rows = w_down.shape[0]

    def to_units(w):
        split = w.reshape(d_rows, 4, 4, 2, ff_rows).transpose(2, 0, 3, 1, 4)
        return jnp.pad(split, ((0, 0),) * 4 + ((0, FF_PAD - ff_rows),)).reshape(4, d_rows, 8 * FF_PAD)

    def from_units(g):
        split = g.reshape(4, d_rows, 2, 4, FF_PAD)[..., :ff_rows]
        return split.transpose(1, 3, 0, 2, 4).reshape(d_rows, 32 * ff_rows)

    units = 8 * FF_PAD
    gate_up = jnp.concatenate([to_units(w_gate), to_units(w_up)], axis=2)
    gate_up = dealt(after(gate_up, plane_out_b), Z_RING).reshape(4 * d_rows, 2 * units)
    gate_up = ring_pieces(ring_whole(gate_up, X_RING), Y_RING)
    down_cols = jnp.pad(after(w_down, plane_c), ((0, FF_PAD - ff_rows), (0, 0)))
    down_cols = in_order(ring_pieces(ring_in_order(down_cols, Y_RING), X_RING), X_RING)
    down_low, down_high = down_cols[:units], down_cols[units:]
    down_mine = jnp.where(first_core, down_low, down_high)
    down_theirs = jnp.where(first_core, down_high, down_low)
    down = join_columns(down_mine, other_core(down_theirs))

    def group_tokens(a):
        return both_tokens(ring_whole(a, Z_RING))

    def group_sum(both):
        return ring_sum_whole(to_low(sum_cores(both)), Z_RING)

    grad_out = out_grad[0]
    grad_out_group = group_tokens(after(grad_out, plane_c))

    pick_a, pick_b, pick_c = (
        one_hot(picker(order, d_rows), width) for order in (ORDER_A, ORDER_B, ORDER_C)
    )
    pick_ff = one_hot(ff_picker(d_rows), width)

    def permuted(a, hot):
        return to_low(product(a, hot))

    normed, norm_back = jax.vjp(rms_scale, tokens, norm_gain)
    normed_low = to_low(normed)
    normed_chip = both_tokens(normed_low)
    normed_a, normed_b, normed_c = (permuted(normed_chip, hot) for hot in (pick_a, pick_b, pick_c))

    mixed_half = jnp.concatenate(
        [by_pieces(normed_a, in_a), by_pieces(normed_b, in_b), by_pieces(normed_c, in_c)], axis=1
    )
    mixed_mine = mixed_half[:rows_dev]
    mixed_got = other_core(to_low(mixed_half[rows_dev:]))
    conv_in = jnp.where(first_core, to_low(mixed_mine), mixed_got)
    gate_z = jnp.where(first_core, mixed_got.astype(jnp.float32), mixed_mine)

    qkv_half = to_low(by_pieces(normed_c, qkv_c))
    q_cols, k_cols = w_query.shape[1], w_key.shape[1]
    qkv_mine, qkv_got = qkv_half[:rows_dev], other_core(qkv_half[rows_dev:])
    queries = join_columns(qkv_mine[:, :q_cols], qkv_got[:, :q_cols])
    keys_low = join_columns(qkv_mine[:, q_cols : q_cols + k_cols], qkv_got[:, q_cols : q_cols + k_cols])
    values_low = join_columns(qkv_mine[:, q_cols + k_cols :], qkv_got[:, q_cols + k_cols :])

    edge_rows = shifted(conv_in[rows_dev - edge_count :], 1)
    key_value = jnp.concatenate([keys_low, values_low], axis=1)
    along_z = lax.axis_index(Z_RING)
    kv_cols = KV_HEADS * HEAD_DIM
    row = ring_in_order(key_value, Z_RING).reshape(4, rows_dev, 2 * kv_cols)
    window = jnp.concatenate([shifted(row, 2, ROWS), shifted(row, 1, ROWS), row])
    window = lax.dynamic_slice_in_dim(window, along_z, reach_blocks + 1).reshape(-1, key_value.shape[1])
    window_keys, window_values = window[:, :kv_cols], window[:, kv_cols:]

    padded_in = jnp.concatenate([edge_rows, conv_in], axis=0).astype(jnp.float32)
    conved, conv_back = jax.vjp(conv_silu, padded_in, conv_weight, conv_bias)
    conved_low = to_low(conved)
    conv_values = conved_low.astype(jnp.float32)
    selected = product(conved_low, select_full)
    step_raw = to_low(selected[:, :rank_width])
    in_mat = selected[:, rank_width : rank_width + state_width]
    out_mat = selected[:, rank_width + state_width :]
    step_pre = product_nt(step_raw, step_full)
    (step_size, decay_rate), rate_back = jax.vjp(rate_piece, step_pre, step_bias, log_decay)
    total_step = jnp.sum(step_size, axis=0)
    drive = step_size * conv_values
    in_lanes, out_lanes = lanes(in_mat), lanes(out_mat)
    end_state = scan_state(step_size, drive, in_lanes, decay_rate)
    state_in = chain_carry(total_step, end_state, decay_rate, False)
    scan_out = scan_full(step_size, drive, in_lanes, out_lanes, decay_rate, state_in)
    gated, gate_back = jax.vjp(gate_piece, scan_out, conv_values, gate_z, skip_gain)
    gated_low = to_low(gated)

    span_keys = (reach_blocks + 1) * rows_dev
    segment_row = segment_ids[0]
    padded_segs = jnp.concatenate(
        [jnp.full((reach_blocks * rows_dev,), -1, jnp.int32), segment_row]
    )
    key_segs = lax.dynamic_slice_in_dim(padded_segs, position * rows_dev, span_keys)
    query_segs = lax.dynamic_slice_in_dim(segment_row, position * rows_dev, rows_dev)
    gaps = (reach_blocks * rows_dev + jnp.arange(rows_dev, dtype=jnp.int32))[:, None] - jnp.arange(
        span_keys, dtype=jnp.int32
    )[None, :]
    allowed = (gaps >= 0) & (gaps < WINDOW) & (query_segs[:, None] == key_segs[None, :])
    head_outputs = []
    log_totals = []
    for group_index in range(KV_HEADS):
        scores, query_part, key_part = group_scores(
            queries, window_keys, allowed, group_index, group_size, score_scale
        )
        row_max = jnp.max(scores, axis=-1, keepdims=True)
        exp_scores = jnp.exp(scores - row_max)
        row_total = jnp.sum(exp_scores, axis=-1, keepdims=True)
        log_totals.append(row_max + jnp.log(row_total))
        weights_low = to_low(exp_scores / row_total)
        value_part = window_values[:, group_index * HEAD_DIM : (group_index + 1) * HEAD_DIM]
        head_outputs.append(
            jnp.einsum(
                "gqs,sd->qgd", weights_low, value_part, preferred_element_type=jnp.float32
            ).reshape(rows_dev, group_size * HEAD_DIM)
        )
    heads_low = to_low(jnp.concatenate(head_outputs, axis=1))

    heads_b = both_tokens(permuted(heads_low, pick_b))
    gated_chip = both_tokens(gated_low)
    branch_out = jnp.concatenate([by_pieces(heads_b, attn_out_b), product(gated_chip, mamba_out_a)], axis=1)
    half_width = width // 2
    out_mine, out_got = branch_out[:rows_dev], other_core(branch_out[rows_dev:])
    attn_out = join_columns(out_mine[:, :half_width], out_got[:, :half_width])
    mamba_out = join_columns(out_mine[:, half_width:], out_got[:, half_width:])
    hidden_mid, merge_back = jax.vjp(
        merge_piece, tokens, attn_out, mamba_out, attn_gain, mamba_gain
    )
    normed_two, norm_two_back = jax.vjp(rms_scale, hidden_mid, ffn_norm_gain)
    normed_two_ff = group_tokens(permuted(to_low(normed_two), pick_ff))
    gate_up_val = by_pieces(normed_two_ff, gate_up)
    act_val, act_back = jax.vjp(swiglu, gate_up_val[:, :units], gate_up_val[:, units:])
    act_low = to_low(act_val)
    d_act = product_nt(grad_out_group, down)
    d_gate, d_up = act_back(d_act)
    d_gate_up = jnp.concatenate([to_low(d_gate), to_low(d_up)], axis=1)
    d_normed_two = group_sum(by_pieces_nt(d_gate_up, gate_up))
    grad_gate_up = grad_pieces(normed_two_ff, d_gate_up)
    grad_down = to_low(product_tn(act_low, grad_out_group))
    output = to_low(hidden_mid + group_sum(product(act_low, down)))[None]

    gate_up_sum = ring_sum_whole(to_low(ring_sum(grad_gate_up, Y_RING)), X_RING)
    gate_up_sum = dealt(to_low(gate_up_sum).reshape(4, d_rows, 2 * units), Z_RING).astype(jnp.float32)
    grad_gate, grad_up = from_units(gate_up_sum[..., :units]), from_units(gate_up_sum[..., units:])
    down_l, down_r = jnp.split(grad_down, 2, axis=1)
    down_mine = jnp.where(first_core, down_l, down_r)
    down_got = other_core(jnp.where(first_core, down_r, down_l))
    grad_down = jnp.concatenate(
        [jnp.where(first_core, down_mine, down_got), jnp.where(first_core, down_got, down_mine)], axis=0
    )
    grad_down = to_low(ring_sum(turned_pieces(grad_down, X_RING), X_RING))
    grad_down = ring_sum_in_order(grad_down, Y_RING)[:ff_rows]

    def unpermuted(a, hot):
        high = lax.reduce_precision(a, 8, 7)
        return product_nt(to_low(high), hot) + product_nt(to_low(a - high), hot)

    d_mid_norm, grad_ffn_norm = norm_two_back(unpermuted(d_normed_two, pick_ff))
    d_mid = grad_out.astype(jnp.float32) + d_mid_norm
    d_tokens_res, d_attn_out, d_mamba_out, grad_attn_gain, grad_mamba_gain = merge_back(d_mid)
    d_attn_low, d_mamba_low = to_low(d_attn_out), to_low(d_mamba_out)
    d_branch = jnp.concatenate(
        [d_attn_low[:, :half_width], d_mamba_low[:, :half_width], d_attn_low[:, half_width:], d_mamba_low[:, half_width:]],
        axis=1,
    )
    d_branch_half = own_columns(d_branch)
    d_attn_half, d_mamba_half = d_branch_half[:, :half_width], d_branch_half[:, half_width:]
    d_gated = sum_cores(product_nt(d_mamba_half, mamba_out_a))
    d_heads_b = sum_cores(by_pieces_nt(d_attn_half, attn_out_b))
    d_heads = to_low(product_nt(to_low(d_heads_b), pick_b))
    grad_attn_out = plane_sum(ring_sum(grad_pieces(heads_b, d_attn_half), ORDER_B[1]), ORDER_B, d_rows)
    grad_mamba_out = turned_pieces(to_low(product_tn(gated_chip, d_mamba_half)), ORDER_A[1])
    grad_mamba_out = plane_sum(ring_sum(grad_mamba_out, ORDER_A[1]), ORDER_A, c_rows)

    query_grads = []
    key_grads = []
    value_grads = []
    for group_index in range(KV_HEADS):
        scores, query_part, key_part = group_scores(
            queries, window_keys, allowed, group_index, group_size, score_scale
        )
        weights_now = jnp.exp(scores - log_totals[group_index])
        weights_low = to_low(weights_now)
        value_part = window_values[:, group_index * HEAD_DIM : (group_index + 1) * HEAD_DIM]
        head_grad = d_heads[
            :, group_index * group_size * HEAD_DIM : (group_index + 1) * group_size * HEAD_DIM
        ].reshape(rows_dev, group_size, HEAD_DIM)
        d_weights = jnp.einsum(
            "qgd,sd->gqs", head_grad, value_part, preferred_element_type=jnp.float32
        )
        d_scores = to_low(
            weights_now * (d_weights - jnp.sum(weights_now * d_weights, axis=-1, keepdims=True))
        )
        query_grads.append(
            jnp.einsum(
                "gqs,sd->qgd", d_scores, key_part, preferred_element_type=jnp.float32
            ).reshape(rows_dev, group_size * HEAD_DIM)
            * score_scale
        )
        key_grads.append(
            jnp.einsum("gqs,qgd->sd", d_scores, query_part, preferred_element_type=jnp.float32)
            * score_scale
        )
        value_grads.append(
            jnp.einsum("gqs,qgd->sd", weights_low, head_grad, preferred_element_type=jnp.float32)
        )
    d_queries = to_low(jnp.concatenate(query_grads, axis=1))
    d_window = jnp.concatenate(key_grads + value_grads, axis=1)
    d_rows_z = jnp.zeros((12, rows_dev, d_window.shape[1]), jnp.bfloat16)
    d_rows_z = lax.dynamic_update_slice_in_dim(
        d_rows_z, to_low(d_window).reshape(reach_blocks + 1, rows_dev, -1), along_z, 0
    )
    d_row = (
        d_rows_z[8:].astype(jnp.float32)
        + shifted(d_rows_z[4:8], -1, ROWS).astype(jnp.float32)
        + shifted(d_rows_z[:4], -2, ROWS).astype(jnp.float32)
    )
    d_key_value = ring_sum_in_order(to_low(d_row).reshape(4 * rows_dev, 2 * kv_cols), Z_RING)
    d_keys, d_values = to_low(d_key_value[:, :kv_cols]), to_low(d_key_value[:, kv_cols:])

    d_scan, d_conv_gate, d_gate_z, grad_skip = gate_back(d_gated)
    d_state_in = adjoint_state(step_size, d_scan, out_lanes, decay_rate)
    d_end = chain_carry(total_step, d_state_in, decay_rate, True)
    d_step, d_conv_scan, d_rate, d_in_mat, d_out_mat = scan_back(
        step_size, conv_values, d_scan, in_lanes, out_lanes, decay_rate, state_in, d_end
    )
    d_step_pre, grad_step_bias, grad_log_decay = rate_back((d_step, d_rate))
    d_step_low = to_low(d_step_pre)
    grad_step_w = product_tn(d_step_low, step_raw)
    d_step_raw = product(d_step_low, step_full)
    d_selected = to_low(jnp.concatenate([d_step_raw, d_in_mat, d_out_mat], axis=1))
    grad_select = product_tn(conved_low, d_selected)
    d_conved = product_nt(d_selected, select_full) + d_conv_gate + d_conv_scan
    d_padded, grad_conv_w, grad_conv_b = conv_back(d_conved)
    edge_back = shifted(to_low(d_padded[:edge_count]), -1).astype(jnp.float32)
    d_conv_in = d_padded[edge_count:] + jnp.concatenate(
        [jnp.zeros((rows_dev - edge_count, inner), jnp.float32), edge_back], axis=0
    )
    d_mixed_half = own_columns(to_low(jnp.concatenate([d_conv_in, d_gate_z], axis=1)))
    kv_half = kv_cols // 2
    d_qkv_half = own_columns(
        jnp.concatenate(
            [
                d_queries[:, : q_cols],
                d_keys[:, :kv_half],
                d_values[:, :kv_half],
                d_queries[:, q_cols :],
                d_keys[:, kv_half:],
                d_values[:, kv_half:],
            ],
            axis=1,
        )
    )
    d_mixed_a, d_mixed_b = d_mixed_half[:, :cut_a], d_mixed_half[:, cut_a:cut_b]
    d_mixed_c = jnp.concatenate([d_mixed_half[:, cut_b:], d_qkv_half], axis=1)

    both_halves = [
        jnp.pad(
            jnp.concatenate([sel, stp], axis=1), ((0, 0), (0, 128 - sel_half - step_half))
        )
        for sel, stp in zip(jnp.split(grad_select, 2, axis=1), jnp.split(grad_step_w, 2, axis=1))
    ]
    select_mine = jnp.where(first_core, both_halves[0], both_halves[1])
    select_theirs = jnp.where(first_core, both_halves[1], both_halves[0])
    select_sum = to_low(select_mine + other_core(to_low(select_theirs)).astype(jnp.float32))
    select_sum = summed(select_sum.reshape(64, c_rows, 128), ("xh", "xl", "y", "z"))
    ring_a = ring_sum(grad_pieces(normed_a, d_mixed_a), ORDER_A[1])
    ring_b = ring_sum(grad_pieces(normed_b, d_mixed_b), ORDER_B[1])
    ring_c = ring_sum(grad_pieces(normed_c, d_mixed_c), ORDER_C[1])
    sum_a = plane_sum(ring_a, ORDER_A, d_rows)
    sum_b = plane_sum(ring_b, ORDER_B, d_rows)
    sum_c = plane_sum(ring_c, ORDER_C, d_rows)
    mixed_c = inner - cut_b
    grad_mamba_in = from_channels(
        jnp.concatenate([sum_a, sum_b, sum_c[:, :mixed_c]], axis=1)
    )
    grad_query = sum_c[:, mixed_c : mixed_c + q_cols]
    grad_key = sum_c[:, mixed_c + q_cols : mixed_c + q_cols + k_cols]
    grad_value = sum_c[:, mixed_c + q_cols + k_cols :]
    grad_select, grad_step = select_sum[:, :sel_half], select_sum[:, sel_half : sel_half + step_half]

    d_normed_c = by_pieces_nt(d_mixed_c[:, :mixed_c], in_c) + by_pieces_nt(d_qkv_half, qkv_c)
    d_normed = (
        product_nt(to_low(by_pieces_nt(d_mixed_a, in_a)), pick_a)
        + product_nt(to_low(by_pieces_nt(d_mixed_b, in_b)), pick_b)
        + product_nt(to_low(d_normed_c), pick_c)
    )
    d_tokens_norm, grad_norm = norm_back(sum_cores(d_normed))
    input_grad = to_low(d_tokens_res + d_tokens_norm)[None]

    smalls = (
        grad_norm,
        grad_conv_w,
        grad_conv_b,
        grad_step_bias,
        grad_log_decay,
        grad_skip,
        grad_attn_gain,
        grad_mamba_gain,
        grad_ffn_norm,
    )
    channel_rows = [a.reshape(-1, inner) for a in smalls[1:6]]
    gains = jnp.concatenate([smalls[0], *smalls[6:]]).reshape(-1, inner)
    totals = sum_all(jnp.concatenate([gains, *channel_rows]))
    gain_sums = totals[: gains.shape[0]].reshape(4, width)
    at, channel_sums = gains.shape[0], []
    for a in channel_rows:
        channel_sums.append(from_channels(totals[at : at + a.shape[0]]))
        at += a.shape[0]
    totals = [
        gain_sums[0],
        channel_sums[0],
        *(channel_sums[k][0] for k in (1, 2)),
        channel_sums[3],
        channel_sums[4][0],
        *gain_sums[1:],
    ]
    return (
        output,
        input_grad,
        totals[0],
        grad_query,
        grad_key,
        grad_value,
        grad_attn_out,
        grad_mamba_in,
        totals[1],
        totals[2],
        grad_select,
        grad_step,
        totals[3],
        totals[4],
        totals[5],
        grad_mamba_out,
        totals[6],
        totals[7],
        totals[8],
        grad_gate,
        grad_up,
        grad_down,
    )


def solution(mesh):
    torus = Mesh(
        mesh.devices.reshape(mesh.shape["head"], 2, 4, 4, mesh.shape["seq"]),
        ("head", "xh", "y", "z", "xl"),
    )
    weight = P(BLK_SEQ, "head")
    rows = P("xl", HEAD_BLK, None)
    in_specs = (rows, P("xl", None), rows, P()) + (weight,) * 5
    in_specs += (P(), P(), weight, weight, P(), P(), P(), weight, P(), P(), P()) + (weight,) * 3
    out_specs = (rows, rows, P()) + (weight,) * 5
    out_specs += (P(), P(), weight, weight, P(), P(), P(), weight, P(), P(), P()) + (weight,) * 3
    return jax.shard_map(
        shards, mesh=torus, in_specs=in_specs, out_specs=out_specs, check_vma=False
    )
```

```python
import functools
import math

import jax
import jax.numpy as jnp
import numpy as np
from jax import lax
from jax.experimental import pallas as pl
from jax.experimental.pallas import tpu as pltpu
from jax.sharding import Mesh
from jax.sharding import PartitionSpec as P

HEADS = 25
KV_HEADS = 5
HEAD_DIM = 64
WINDOW = 1024
RANK = 100
X_RING = ("xh", "xl")
ROWS = ("head", "xh", "y")
EVERY = ("head", "xh", "y", "z", "xl")
Y_RING = "y"
Z_RING = "z"
BLK_SEQ = ("xh", "y", "z", "xl")
HEAD_BLK = ("head", "xh", "y", "z")
EPSILON = 1e-06
LOG2_E = 1.0 / math.log(2.0)
FF_PAD = 88
WIDTH = HEADS * HEAD_DIM
LANES = -(-WIDTH // 128) * 128


def received(a, axis, d):
    n = lax.axis_size(axis)
    return lax.ppermute(a, axis, [((i + d) % n, i) for i in range(n)])


def other_core(a):
    return received(a, "head", 1)


def shifted(a, distance, axis=HEAD_BLK):
    n = lax.axis_size(axis)
    return lax.ppermute(a, axis, [(i - distance, i) for i in range(n) if 0 <= i - distance < n])


def after(value, *others):
    return lax.optimization_barrier((value, *others))[0]


def dealt(blocks, axis):
    return lax.all_to_all(blocks, axis, 0, 0, tiled=True)


def shown(a, axis):
    return dealt(jnp.broadcast_to(a[None], (lax.axis_size(axis), *a.shape)), axis)


def summed(blocks, axis):
    return jnp.sum(dealt(blocks, axis).astype(jnp.float32), axis=0)


ORDER_A = (("y", "z"), X_RING)
ORDER_B = (("xh", "z", "xl"), Y_RING)
ORDER_C = (("xh", "y", "xl"), Z_RING)
ORDERS = (ORDER_A, ORDER_B, ORDER_C)


def together(values):
    return lax.optimization_barrier(tuple(values))


def ring_pieces(a, axis):
    half = a.shape[0] // 2
    up, down = received(a, axis, 1), received(a, axis, -1)
    return [a, up, received(up[:half], axis, 1), received(down[half:], axis, -1), down]


def ring_whole(a, axis):
    return jnp.concatenate([a] + [received(a, axis, j) for j in (1, 2, 3)], axis=0)


def ring_in_order(a, axis):
    me = lax.axis_index(axis)
    out = jnp.zeros((4, *a.shape), a.dtype)
    for j, part in enumerate([a] + [received(a, axis, j) for j in (1, 2, 3)]):
        out = lax.dynamic_update_index_in_dim(out, part, lax.rem(me + j, 4), 0)
    return out.reshape(4 * a.shape[0], a.shape[1])


def gather_planes(shards, orders, last=()):
    planes = []
    for a, order in zip(shards, orders):
        planes.append(shown(after(a, *last), order[0]).reshape(16 * a.shape[0], a.shape[1]))
        last = planes[-1:]
    return planes


def ring_sum(pieces, axis):
    own, up, far_low, far_high, down = pieces
    half = far_low.shape[0]
    low = own.dtype
    from_down, from_up = received(far_low, axis, -1), received(far_high, axis, 1)
    to_up = jnp.concatenate(
        [(up[:half].astype(jnp.float32) + from_down.astype(jnp.float32)).astype(low), up[half:]]
    )
    to_down = jnp.concatenate(
        [down[:half], (down[half:].astype(jnp.float32) + from_up.astype(jnp.float32)).astype(low)]
    )
    return (
        own.astype(jnp.float32)
        + received(to_up, axis, -1).astype(jnp.float32)
        + received(to_down, axis, 1).astype(jnp.float32)
    )


def ring_sum_whole(whole, axis):
    rows = whole.shape[0] // 4
    total = whole[:rows].astype(jnp.float32)
    for j in (1, 2, 3):
        total = total + received(whole[j * rows : (j + 1) * rows], axis, -j).astype(jnp.float32)
    return total


def sum_rings(grads, orders):
    return [to_low(ring_sum(a, order[1])) for a, order in zip(grads, orders)]


def sum_planes(rings, orders):
    return [summed(a.reshape(16, a.shape[0] // 16, a.shape[1]), order[0]) for a, order in zip(rings, orders)]


def ring_sum_in_order(whole, axis):
    rows = whole.shape[0] // 4
    blocks = whole.reshape(4, rows, whole.shape[1])
    me = lax.axis_index(axis)
    total = 0.0
    for j in range(4):
        block = lax.dynamic_index_in_dim(blocks, lax.rem(me + j, 4), 0, keepdims=False)
        total = total + (received(block, axis, -j) if j else block).astype(jnp.float32)
    return total


def padded_index(index):
    return jnp.pad(index, (0, LANES - WIDTH), constant_values=-1)


def picker(order, rows, stride=None, offset=0):
    stride = stride or rows
    ring, inside = np.indices((4, 16 * rows))
    turned = lax.rem(lax.axis_index(order[1]) + jnp.asarray(ring, jnp.int32), 4)
    block, row = inside // rows, jnp.asarray(inside % rows, jnp.int32)
    if order is ORDER_A:
        xh, y, z, xl = turned // 2, block // 4, block % 4, turned % 2
    elif order is ORDER_B:
        xh, y, z, xl = block // 8, turned, block // 2 % 4, block % 2
    else:
        xh, y, z, xl = block // 8, block // 2 % 4, turned, block % 2
    return padded_index(((((xh * 4 + y) * 4 + z) * 2 + xl) * stride + offset + row).reshape(-1))


def ff_picker(rows):
    xh, y, xl, z, row = np.indices((2, 4, 2, 4, rows))
    index = (((((xh * 4 + y) * 4 + z) * 2 + xl) * rows + row)).reshape(16, 4 * rows)
    return jnp.asarray(np.pad(index, ((0, 0), (0, LANES // 16 - 4 * rows)), constant_values=-1).reshape(-1), jnp.int32)


def gathered(a, axes):
    return lax.all_gather(a, axes).reshape(-1, a.shape[1])


def scattered(a, axes):
    blocks = a.reshape(lax.axis_size(axes), -1, a.shape[1])
    return lax.optimization_barrier(lax.psum_scatter(blocks, axes, scatter_dimension=0))


HALVES = (WIDTH // 4, WIDTH // 4, WIDTH // 8, WIDTH // 8, WIDTH // 4)


def bounds(sizes):
    stops = np.cumsum(sizes)
    return [(int(stop - size), int(stop)) for size, stop in zip(sizes, stops)]


def rows_of(pieces):
    return bounds([a.shape[0] for a in pieces])


def dot_nn(a, b):
    return jnp.dot(a, b, preferred_element_type=jnp.float32)


def dot_nt(a, b):
    return lax.dot_general(a, b, (((1,), (1,)), ((), ())), preferred_element_type=jnp.float32)


def dot_tn(a, b):
    return lax.dot_general(a, b, (((0,), (0,)), ((), ())), preferred_element_type=jnp.float32)


def whole_call(kernel, operands, outs, flops):
    sizes = sum(a.size * a.dtype.itemsize for a in (*operands, *outs))
    return pl.pallas_call(
        kernel,
        out_shape=outs,
        in_specs=[pl.BlockSpec(memory_space=pltpu.VMEM)] * len(operands),
        out_specs=[pl.BlockSpec(memory_space=pltpu.VMEM)] * len(outs),
        compiler_params=pltpu.CompilerParams(vmem_limit_bytes=40 * 2**20),
        cost_estimate=pl.CostEstimate(flops=flops, bytes_accessed=sizes, transcendentals=0),
    )(*operands)


def out_array(rows, cols, low=True):
    return jax.ShapeDtypeStruct((rows, cols), jnp.bfloat16 if low else jnp.float32)


def clear_rest(ref, start):
    if start < ref.shape[1]:
        ref[:, start:] = jnp.zeros((ref.shape[0], ref.shape[1] - start), ref.dtype)


def nn_kernel(windows, *refs):
    count = len(windows)
    lefts, pieces, y_ref = refs[:count], refs[count:-1], refs[-1]
    width = windows[0][1] - windows[0][0]
    for at in range(0, width, 512):
        stop = min(at + 512, width)
        total = 0.0
        for left, (low, _) in zip(lefts, windows):
            for (start, end), piece in zip(rows_of(pieces), pieces):
                total = total + dot_nn(left[:, start:end], piece[:, low + at : low + stop])
        y_ref[:, at:stop] = total.astype(y_ref.dtype)
    clear_rest(y_ref, width)


def by_pieces(lefts, pieces, windows, low=True):
    rows, width = lefts[0].shape[0], windows[0][1] - windows[0][0]
    flops = 2 * rows * width * sum(a.shape[1] for a in lefts)
    return whole_call(
        functools.partial(nn_kernel, windows), (*lefts, *pieces), [out_array(rows, -(-width // 128) * 128 if low else width, low)], flops
    )[0]


def nt_kernel(windows, *refs):
    count = len(windows)
    grads, pieces, outs = refs[:count], refs[count:-count], refs[-count:]
    for grad, (low, high), out in zip(grads, windows, outs):
        for (start, end), piece in zip(rows_of(pieces), pieces):
            out[:, start:end] = dot_nt(grad[:, : high - low], piece[:, low:high]).astype(out.dtype)
        clear_rest(out, rows_of(pieces)[-1][1])


def by_pieces_nt(grads, pieces, windows):
    rows, depth = grads[0].shape[0], sum(a.shape[0] for a in pieces)
    flops = 2 * rows * depth * sum(a.shape[1] for a in grads)
    return whole_call(
        functools.partial(nt_kernel, windows), (*grads, *pieces), [out_array(rows, -(-depth // 128) * 128)] * len(grads), flops
    )


def tn_kernel(sizes, right, *refs):
    lefts, outs = refs[: -len(sizes)], refs[-len(sizes) :]
    width = right.shape[1]
    for k, left in enumerate(lefts):
        for (start, end), out in zip(bounds(sizes), outs):
            out[:, k * width : (k + 1) * width] = dot_tn(left[:, start:end], right[...]).astype(out.dtype)


def grad_pieces(lefts, right, sizes):
    outs = [out_array(size, right.shape[1] * len(lefts)) for size in sizes]
    flops = 2 * right.size * sum(sizes) * len(lefts)
    return whole_call(functools.partial(tn_kernel, sizes), (right, *lefts), outs, flops)


def feed_kernel(x_ref, g_ref, up_ref, down_ref, act_ref, d_ref, y_ref, dx_ref):
    units = down_ref.shape[0]
    both = dot_nn(x_ref[...], up_ref[...])
    gate, up = both[:, :units], both[:, units:]
    sig = 1.0 / (1.0 + jnp.exp(-gate))
    silu = gate * sig
    act = (silu * up).astype(jnp.bfloat16)
    act_ref[...] = act
    y_ref[:, :WIDTH] = dot_nn(act, down_ref[...]).astype(y_ref.dtype)
    clear_rest(y_ref, WIDTH)
    d_act = dot_nt(g_ref[:, :WIDTH], down_ref[...])
    d_ref[:, :units] = (d_act * up * (sig * (1.0 + gate * (1.0 - sig)))).astype(d_ref.dtype)
    d_ref[:, units:] = (d_act * silu).astype(d_ref.dtype)
    dx_ref[...] = dot_nt(d_ref[...], up_ref[...]).astype(dx_ref.dtype)


def feed_forward(x, g, gate_up, down):
    tokens, width = x.shape
    units = down.shape[0]
    block = 256

    def rows(cols):
        return pl.BlockSpec((block, cols), lambda i: (i, 0))

    def fixed(a):
        return pl.BlockSpec(a.shape, lambda i: (0, 0))

    return pl.pallas_call(
        feed_kernel,
        grid=(tokens // block,),
        in_specs=[rows(width), rows(width), fixed(gate_up), fixed(down)],
        out_specs=[rows(units), rows(2 * units), rows(width), rows(width)],
        out_shape=[out_array(tokens, c) for c in (units, 2 * units, width, width)],
        compiler_params=pltpu.CompilerParams(
            dimension_semantics=("arbitrary",), vmem_limit_bytes=48 * 2**20
        ),
        cost_estimate=pl.CostEstimate(
            flops=2 * tokens * width * units * 6, bytes_accessed=2 * tokens * (4 * width + 3 * units), transcendentals=tokens * units
        ),
    )(x, g, gate_up, down)


def feed_grads_kernel(x_ref, d_ref, act_ref, g_ref, up_ref, down_ref):
    up_ref[...] = dot_tn(x_ref[...], d_ref[...]).astype(up_ref.dtype)
    down_ref[...] = dot_tn(act_ref[...], g_ref[:, :WIDTH]).astype(down_ref.dtype)


def feed_grads(x, d, act, g):
    outs = [out_array(x.shape[1], d.shape[1]), out_array(act.shape[1], WIDTH)]
    flops = 2 * x.shape[0] * x.shape[1] * (d.shape[1] + act.shape[1])
    return whole_call(feed_grads_kernel, (x, d, act, g), outs, flops)


def one_hot(index_ref, start, stop):
    width = index_ref.shape[1]
    rows = lax.broadcasted_iota(jnp.int32, (stop - start, width), 0) + start
    return jnp.where(rows == index_ref[...], 1.0, 0.0).astype(jnp.bfloat16)


def turn_kernel(count, *refs):
    lefts, indices, outs = refs[:count], refs[count : 2 * count], refs[2 * count :]
    for left, index, out in zip(lefts, indices, outs):
        total = 0.0
        for start in range(0, left.shape[1], 400):
            total = total + dot_nn(left[:, start : start + 400], one_hot(index, start, start + 400))
        out[...] = total.astype(out.dtype)


def turned(lefts, indices):
    outs = [out_array(a.shape[0], index.shape[0]) for a, index in zip(lefts, indices)]
    rows = [index.reshape(1, -1) for index in indices]
    flops = sum(2 * a.size * a.shape[1] for a in lefts)
    return whole_call(functools.partial(turn_kernel, len(lefts)), (*lefts, *rows), outs, flops)


def turn_back_kernel(count, *refs):
    lefts, indices, outs = refs[:count], refs[count : 2 * count], refs[2 * count :]
    for start in range(0, outs[0].shape[1], 400):
        total = 0.0
        for k, (left, index) in enumerate(zip(lefts, indices)):
            hot = one_hot(index, start, start + 400)
            if left.dtype == jnp.float32:
                high = left[...].astype(jnp.bfloat16)
                rest = (left[...] - high.astype(jnp.float32)).astype(jnp.bfloat16)
                part = dot_nt(high, hot) + dot_nt(rest, hot)
            else:
                part = dot_nt(left[...], hot)
            if len(outs) > 1:
                outs[k][:, start : start + 400] = part.astype(outs[k].dtype)
            total = total + part
        if len(outs) == 1:
            outs[0][:, start : start + 400] = total.astype(outs[0].dtype)


def turned_back(lefts, indices, low, summed=False, width=WIDTH):
    rows = lefts[0].shape[0]
    outs = [out_array(rows, width, low)] * (1 if summed else len(lefts))
    hots = [index.reshape(1, -1) for index in indices]
    flops = sum(2 * a.size * width for a in lefts)
    return whole_call(functools.partial(turn_back_kernel, len(lefts)), (*lefts, *hots), outs, flops)


def join_columns(mine, got):
    first = lax.axis_index("head") == 0
    return jnp.concatenate([jnp.where(first, mine, got), jnp.where(first, got, mine)], axis=1)


def own_tokens(both):
    rows = both.shape[0] // 2
    return join_columns(both[:rows], other_core(both[rows:]))


def own_columns(a):
    first = lax.axis_index("head") == 0
    low, high = jnp.split(a, 2, axis=1)
    mine, theirs = jnp.where(first, low, high), jnp.where(first, high, low)
    return jnp.concatenate([mine, other_core(theirs)], axis=0)


def both_tokens(a):
    return jnp.concatenate([a, other_core(a)], axis=0)


def sum_cores(both):
    rows = both.shape[0] // 2
    return both[:rows].astype(jnp.float32) + other_core(to_low(both[rows:])).astype(jnp.float32)


def chain_kernel(reverse, packed_ref, rate_ref, out_ref):
    rate = rate_ref[...] * LOG2_E
    count, states = packed_ref.shape[0], rate.shape[0]

    def one(k, state):
        p = count - 1 - k if reverse else k
        out_ref[p] = state
        packed = packed_ref[p].astype(jnp.float32)
        total = packed[states : states + 1] + packed[states + 1 : states + 2]
        return jnp.exp2(total * rate) * state + packed[:states]

    lax.fori_loop(0, count, one, jnp.zeros(rate.shape, jnp.float32))


def chain_carry(total_step, state, decay_rate, reverse, others=()):
    count = lax.axis_size(HEAD_BLK)
    states, channels = state.shape
    high = lax.reduce_precision(total_step, 8, 7)
    packed = jnp.concatenate([state, high[None], (total_step - high)[None]]).astype(jnp.bfloat16)

    def tiles(a):
        padded = jnp.pad(a, ((0, 0), (0, count * 128 - channels)))
        return padded.reshape(a.shape[0], count, 128).transpose(1, 0, 2)

    rate = lax.dynamic_index_in_dim(tiles(decay_rate), lax.axis_index(HEAD_BLK), 0, keepdims=False)
    chained = pl.pallas_call(
        functools.partial(chain_kernel, reverse),
        out_shape=jax.ShapeDtypeStruct((count, states, 128), jnp.float32),
    )(dealt(tiles(packed), HEAD_BLK), rate)
    got = dealt(after(to_low(chained), *others), HEAD_BLK)[: channels // 128]
    return got.transpose(1, 0, 2).reshape(states, channels).astype(jnp.float32)


def sum_all(values, owned):
    count = lax.axis_size(EVERY)
    lines = values.reshape(-1, 128)
    each = -(-lines.shape[0] // count)
    padded = jnp.pad(lines, ((0, count * each - lines.shape[0]), (0, 0))).reshape(count, each, 128)
    mine = summed(jnp.concatenate([to_low(owned), to_low(padded)], axis=1), EVERY)
    all_lines = shown(mine[owned.shape[1] :], EVERY).reshape(-1, 128)
    return all_lines[: lines.shape[0]].reshape(values.shape), mine[: owned.shape[1]]


def rms_scale(values, gain):
    return values * lax.rsqrt(jnp.mean(values * values, axis=-1, keepdims=True) + EPSILON) * gain


def to_low(values):
    return values.astype(jnp.bfloat16)


def product(left, right):
    return jnp.dot(left, right, preferred_element_type=jnp.float32)


def product_tn(left, right):
    return lax.dot_general(
        left, right, (((0,), (0,)), ((), ())), preferred_element_type=jnp.float32
    )


def product_nt(left, right):
    return lax.dot_general(
        left, right, (((1,), (1,)), ((), ())), preferred_element_type=jnp.float32
    )


def chain_combine(earlier, later):
    return (earlier[0] * later[0], later[0] * earlier[1] + later[1])


def conv_silu(padded, conv_weight, conv_bias):
    tap_count = conv_weight.shape[0]
    length = padded.shape[0] - tap_count + 1
    total_sum = conv_bias
    for tap_index in range(tap_count):
        total_sum = total_sum + conv_weight[tap_index] * padded[tap_index : tap_index + length]
    return jax.nn.silu(total_sum)


def rate_piece(step_pre, step_bias, log_decay):
    return (jax.nn.softplus(step_pre + step_bias), -jnp.exp(log_decay))


def gate_piece(scan_out, conv_values, gate_z, skip_gain):
    return (scan_out + skip_gain * conv_values) * jax.nn.silu(gate_z)


def merge_piece(tokens, attn_out, mamba_out, attn_gain, mamba_gain):
    return tokens + 0.5 * (rms_scale(attn_out, attn_gain) + rms_scale(mamba_out, mamba_gain))


def swiglu(gate_val, up_val):
    return jax.nn.silu(gate_val) * up_val


SCAN_TILE = 640


def scan_state_kernel(step_ref, drive_ref, in_ref, rate_ref, end_ref):
    rate = rate_ref[...] * LOG2_E
    width = rate.shape[1]

    def eight(k, state):
        base = pl.multiple_of(k * 8, 8)
        step, drive = step_ref[pl.ds(base, 8), :], drive_ref[pl.ds(base, 8), :]
        for i in range(8):
            decay = jnp.exp2(step[i : i + 1] * rate)
            in_now = jnp.tile(in_ref[base + i], (1, width // 128))
            state = decay * state + in_now * drive[i : i + 1]
        return state

    end_ref[...] = lax.fori_loop(0, step_ref.shape[0] // 8, eight, jnp.zeros(rate.shape, jnp.float32))


def scan_full_kernel(step_ref, drive_ref, in_ref, out_ref, rate_ref, start_ref, y_ref):
    rate = rate_ref[...] * LOG2_E
    width = rate.shape[1]

    def eight(k, state):
        base = pl.multiple_of(k * 8, 8)
        step, drive = step_ref[pl.ds(base, 8), :], drive_ref[pl.ds(base, 8), :]
        rows = []
        for i in range(8):
            decay = jnp.exp2(step[i : i + 1] * rate)
            in_now = jnp.tile(in_ref[base + i], (1, width // 128))
            out_now = jnp.tile(out_ref[base + i], (1, width // 128))
            state = decay * state + in_now * drive[i : i + 1]
            rows.append(jnp.sum(out_now * state, axis=0, keepdims=True))
        y_ref[pl.ds(base, 8), :] = jnp.concatenate(rows, axis=0)
        return state

    lax.fori_loop(0, step_ref.shape[0] // 8, eight, start_ref[...])


def adjoint_state_kernel(step_ref, d_scan_ref, out_ref, rate_ref, d_start_ref):
    rate = rate_ref[...] * LOG2_E
    width = rate.shape[1]
    blocks = step_ref.shape[0] // 8

    def eight(k, carry):
        base = pl.multiple_of((blocks - 1 - k) * 8, 8)
        step, d_scan = step_ref[pl.ds(base, 8), :], d_scan_ref[pl.ds(base, 8), :]
        for i in range(7, -1, -1):
            out_now = jnp.tile(out_ref[base + i], (1, width // 128))
            carry = jnp.exp2(step[i : i + 1] * rate) * (out_now * d_scan[i : i + 1] + carry)
        return carry

    d_start_ref[...] = lax.fori_loop(0, blocks, eight, jnp.zeros(rate.shape, jnp.float32))


def scan_back_kernel(
    step_ref,
    conv_ref,
    d_scan_ref,
    in_ref,
    out_ref,
    rate_ref,
    start_ref,
    d_end_ref,
    d_step_ref,
    d_conv_ref,
    d_rate_ref,
    d_in_ref,
    d_out_ref,
    states_ref,
    decays_ref,
):
    true_rate = rate_ref[...]
    rate = true_rate * LOG2_E
    width = rate.shape[1]
    tiles = width // 128
    blocks = step_ref.shape[0] // 8

    @pl.when(pl.program_id(0) == 0)
    def _():
        d_in_ref[...] = jnp.zeros(d_in_ref.shape, jnp.float32)
        d_out_ref[...] = jnp.zeros(d_out_ref.shape, jnp.float32)

    def folded(a):
        total = a[:, :128]
        for j in range(1, tiles):
            total = total + a[:, j * 128 : (j + 1) * 128]
        return total

    states_ref[0] = start_ref[...]

    def forward(k, state):
        base = pl.multiple_of(k * 8, 8)
        step, conv = step_ref[pl.ds(base, 8), :], conv_ref[pl.ds(base, 8), :]
        d_scan = d_scan_ref[pl.ds(base, 8), :]
        drive = step * conv
        for i in range(8):
            decay = jnp.exp2(step[i : i + 1] * rate)
            in_now = jnp.tile(in_ref[base + i], (1, tiles))
            state = decay * state + in_now * drive[i : i + 1]
            decays_ref[base + i] = decay
            states_ref[base + i + 1] = state
            d_out_ref[base + i] += folded(d_scan[i : i + 1] * state)
        return state

    lax.fori_loop(0, blocks, forward, start_ref[...])

    def backward(k, carried):
        carry, d_rate = carried
        base = pl.multiple_of((blocks - 1 - k) * 8, 8)
        step, conv = step_ref[pl.ds(base, 8), :], conv_ref[pl.ds(base, 8), :]
        d_scan = d_scan_ref[pl.ds(base, 8), :]
        drive = step * conv
        through_rate, through_drive = [], []
        for i in range(7, -1, -1):
            in_now = jnp.tile(in_ref[base + i], (1, tiles))
            out_now = jnp.tile(out_ref[base + i], (1, tiles))
            adjoint = out_now * d_scan[i : i + 1] + carry
            carry = decays_ref[base + i] * adjoint
            before = carry * states_ref[base + i]
            d_rate = d_rate + before * step[i : i + 1]
            through_rate.append(jnp.sum(true_rate * before, axis=0, keepdims=True))
            through_drive.append(jnp.sum(adjoint * in_now, axis=0, keepdims=True))
            d_in_ref[base + i] += folded(adjoint * drive[i : i + 1])
        by_rate = jnp.concatenate(through_rate[::-1], axis=0)
        by_drive = jnp.concatenate(through_drive[::-1], axis=0)
        d_step_ref[pl.ds(base, 8), :] = by_rate + by_drive * conv
        d_conv_ref[pl.ds(base, 8), :] = by_drive * step
        return carry, d_rate

    zero = jnp.zeros(rate.shape, jnp.float32)
    d_rate_ref[...] = lax.fori_loop(0, blocks, backward, (d_end_ref[...], zero))[1]


def scan_specs(rows, states):
    tokens = pl.BlockSpec((rows, SCAN_TILE), lambda i: (0, i))
    maps = pl.BlockSpec((rows, states, 128), lambda i: (0, 0, 0))
    state = pl.BlockSpec((states, SCAN_TILE), lambda i: (0, i))
    return tokens, maps, state


def scan_call(kernel, operands, in_kinds, outs, out_kinds, scratch=(), flops=8, exps=1):
    rows, channels = operands[0].shape
    states = 16
    kinds = dict(zip("tms", scan_specs(rows, states)))
    shapes = {"t": (rows, channels), "m": (rows, states, 128), "s": (states, channels)}
    work = rows * states * channels
    return pl.pallas_call(
        kernel,
        grid=(channels // SCAN_TILE,),
        in_specs=[kinds[k] for k in in_kinds],
        out_specs=[kinds[k] for k in out_kinds],
        out_shape=[jax.ShapeDtypeStruct(shapes[k], jnp.float32) for k in out_kinds],
        scratch_shapes=scratch,
        compiler_params=pltpu.CompilerParams(
            dimension_semantics=("arbitrary",), vmem_limit_bytes=(36 if scratch else 16) * 2**20
        ),
        cost_estimate=pl.CostEstimate(
            flops=work * flops, bytes_accessed=4 * rows * channels * 4, transcendentals=work * exps
        ),
    )(*operands)


def lanes(a):
    return jnp.broadcast_to(a[:, :, None], (*a.shape, 128))


def scan_state(step_size, drive, in_lanes, decay_rate):
    return scan_call(scan_state_kernel, (step_size, drive, in_lanes, decay_rate), "ttms", 1, "s")[0]


def scan_full(step_size, drive, in_lanes, out_lanes, decay_rate, state_in):
    operands = (step_size, drive, in_lanes, out_lanes, decay_rate, state_in)
    return scan_call(scan_full_kernel, operands, "ttmmss", 1, "t")[0]


def adjoint_state(step_size, d_scan, out_lanes, decay_rate):
    return scan_call(adjoint_state_kernel, (step_size, d_scan, out_lanes, decay_rate), "ttms", 1, "s")[0]


def scan_back(step_size, conv_values, d_scan, in_lanes, out_lanes, decay_rate, state_in, d_end):
    rows, states = step_size.shape[0], decay_rate.shape[0]
    scratch = (
        pltpu.VMEM((rows + 1, states, SCAN_TILE), jnp.float32),
        pltpu.VMEM((rows, states, SCAN_TILE), jnp.float32),
    )
    operands = (step_size, conv_values, d_scan, in_lanes, out_lanes, decay_rate, state_in, d_end)
    d_step, d_conv, d_rate, d_in, d_out = scan_call(
        scan_back_kernel, operands, "tttmmsss", 5, "ttsmm", scratch, flops=24
    )
    return d_step, d_conv, d_rate, jnp.sum(d_in, axis=-1), jnp.sum(d_out, axis=-1)


SCORE_SCALE = 1.0 / math.sqrt(HEAD_DIM)
GROUP = HEADS // KV_HEADS


def attend_kernel(q_ref, window_ref, bias_ref, out_ref, total_ref):
    keys, values = window_ref[:, :HEAD_DIM], window_ref[:, HEAD_DIM:]
    for h in range(GROUP):
        lanes = slice(h * HEAD_DIM, (h + 1) * HEAD_DIM)
        scores = dot_nt(q_ref[0, :, lanes], keys) * SCORE_SCALE + bias_ref[...]
        top = jnp.max(scores, axis=1, keepdims=True)
        weights = jnp.exp(scores - top)
        total = jnp.sum(weights, axis=1, keepdims=True)
        low = (weights * (1.0 / total)).astype(jnp.bfloat16)
        out_ref[0, :, lanes] = dot_nn(low, values).astype(out_ref.dtype)
        total_ref[0, :, h : h + 1] = top + jnp.log(total)


def attend_back_kernel(q_ref, window_ref, bias_ref, total_ref, d_ref, dq_ref, d_window_ref):
    keys, values = window_ref[:, :HEAD_DIM], window_ref[:, HEAD_DIM:]
    d_keys = d_values = 0.0
    for h in range(GROUP):
        lanes = slice(h * HEAD_DIM, (h + 1) * HEAD_DIM)
        queries, d_heads = q_ref[0, :, lanes], d_ref[0, :, lanes]
        weights = jnp.exp(dot_nt(keys, queries) * SCORE_SCALE + bias_ref[...] - total_ref[0, h : h + 1, :])
        d_weights = dot_nt(values, d_heads)
        through = jnp.sum(weights * d_weights, axis=0, keepdims=True)
        d_scores = (weights * (d_weights - through)).astype(jnp.bfloat16)
        d_values = d_values + dot_nn(weights.astype(jnp.bfloat16), d_heads)
        d_keys = d_keys + dot_nn(d_scores, queries)
        dq_ref[0, :, lanes] = (dot_tn(d_scores, keys) * SCORE_SCALE).astype(dq_ref.dtype)
    d_window_ref[:, :HEAD_DIM] = (d_keys * SCORE_SCALE).astype(d_window_ref.dtype)
    d_window_ref[:, HEAD_DIM:] = d_values.astype(d_window_ref.dtype)


def attend_call(kernel, operands, kinds, outs, out_kinds, rows, span, products):
    groups = pl.BlockSpec((1, rows, GROUP * HEAD_DIM), lambda i: (i, 0, 0))
    window = pl.BlockSpec((span, 2 * HEAD_DIM), lambda i: (0, i))
    specs = {"q": groups, "w": window}
    for a in (*operands, *outs):
        specs[a.shape] = pl.BlockSpec(a.shape, lambda i: (0, 0)) if len(a.shape) == 2 else pl.BlockSpec((1, *a.shape[1:]), lambda i: (i, 0, 0))
    return pl.pallas_call(
        kernel,
        grid=(KV_HEADS,),
        in_specs=[specs[k if k in specs else a.shape] for k, a in zip(kinds, operands)],
        out_specs=[specs[k if k in specs else a.shape] for k, a in zip(out_kinds, outs)],
        out_shape=outs,
        compiler_params=pltpu.CompilerParams(
            dimension_semantics=("arbitrary",), vmem_limit_bytes=24 * 2**20
        ),
        cost_estimate=pl.CostEstimate(
            flops=2 * products * HEADS * rows * span * HEAD_DIM, bytes_accessed=4 * rows * span, transcendentals=HEADS * rows * span
        ),
    )(*operands)


def by_groups(a):
    return a.reshape(a.shape[0], KV_HEADS, GROUP * HEAD_DIM).transpose(1, 0, 2)


def from_groups(a):
    return a.transpose(1, 0, 2).reshape(a.shape[1], HEADS * HEAD_DIM)


def attend(queries, window, bias):
    rows, span = queries.shape[1], window.shape[0]
    outs = [
        jax.ShapeDtypeStruct(queries.shape, jnp.bfloat16),
        jax.ShapeDtypeStruct((KV_HEADS, rows, 8), jnp.float32),
    ]
    return attend_call(attend_kernel, (queries, window, bias), "qwb", outs, "qt", rows, span, 2)


def attend_back(queries, window, bias_t, totals, d_heads):
    rows, span = queries.shape[1], window.shape[0]
    outs = [
        jax.ShapeDtypeStruct(queries.shape, jnp.bfloat16),
        jax.ShapeDtypeStruct(window.shape, jnp.bfloat16),
    ]
    operands = (queries, window, bias_t, totals.transpose(0, 2, 1), d_heads)
    return attend_call(attend_back_kernel, operands, "qwbtq", outs, "qw", rows, span, 5)


def shards(
    inputs,
    segment_ids,
    out_grad,
    norm_gain,
    w_query,
    w_key,
    w_value,
    w_attn_out,
    w_mamba_in,
    conv_weight,
    conv_bias,
    w_select,
    w_step,
    step_bias,
    log_decay,
    skip_gain,
    w_mamba_out,
    attn_gain,
    mamba_gain,
    ffn_norm_gain,
    w_gate,
    w_up,
    w_down,
):
    rows_dev, width = inputs.shape[1:]
    inner = conv_weight.shape[1]
    edge_count = conv_weight.shape[0] - 1
    rank_width = RANK
    state_width = log_decay.shape[0]
    reach_blocks = WINDOW // rows_dev
    group_size = HEADS // KV_HEADS
    score_scale = 1.0 / math.sqrt(HEAD_DIM)
    position = lax.axis_index(HEAD_BLK)
    core = lax.axis_index("head")
    first_core = core == 0
    tokens = inputs[0].astype(jnp.float32)

    d_rows = w_query.shape[0]
    c_rows = w_select.shape[0]
    sel_half, step_half = w_select.shape[1], w_step.shape[1]
    mamba_in = w_mamba_in
    cut_a, cut_b = 1408, 2816
    mixed_c = inner - cut_b
    planes = gather_planes(
        (
            mamba_in[:, :cut_a],
            mamba_in[:, cut_a:cut_b],
            jnp.concatenate([mamba_in[:, cut_b:], w_query, w_key, w_value], axis=1),
        ),
        ORDERS,
    )
    parts = [ring_pieces(a, order[1]) for a, order in zip(planes, ORDERS)]
    half_width = width // 2
    windows_in = [(0, a[0].shape[1]) for a in parts]
    windows_out_a, window_out_b = ((0, half_width), (half_width, 2 * half_width)), (0, half_width)
    select_step = jnp.pad(
        jnp.concatenate([w_select, w_step], axis=1), ((0, 0), (0, 128 - sel_half - step_half))
    )
    select_mine = shown(after(select_step, planes[2]), BLK_SEQ).reshape(inner, 128)
    select_got = other_core(select_mine)
    select_full = join_columns(select_mine[:, :sel_half], select_got[:, :sel_half])
    step_full = join_columns(
        select_mine[:, sel_half : sel_half + step_half], select_got[:, sel_half : sel_half + step_half]
    )

    out_shards = (jnp.concatenate([w_mamba_out[:d_rows], w_mamba_out[d_rows:]], axis=1), w_attn_out)

    ff_rows = w_down.shape[0]

    def to_units(w):
        split = w.reshape(d_rows, 4, 4, 2, ff_rows).transpose(2, 0, 1, 3, 4)
        return jnp.pad(split, ((0, 0),) * 4 + ((0, FF_PAD - ff_rows),)).reshape(4, d_rows, 8 * FF_PAD)

    def from_units(g):
        split = g.reshape(4, d_rows, 4, 2, FF_PAD)[..., :ff_rows]
        return split.transpose(1, 2, 0, 3, 4).reshape(d_rows, 32 * ff_rows)

    units = 8 * FF_PAD
    gate_up = jnp.concatenate([to_units(w_gate), to_units(w_up)], axis=2)
    gate_up_dealt = dealt(after(gate_up, select_mine), Z_RING).reshape(4 * d_rows, 2 * units)
    gate_up = gathered(jnp.pad(gate_up_dealt, ((0, LANES // 16 - 4 * d_rows), (0, 0))), ("xh", "y", "xl"))

    here = lax.axis_index("xh") == core
    down = jnp.pad(w_down, ((0, FF_PAD - ff_rows), (0, 0)))
    down = join_columns(down, other_core(down))
    down = jnp.where(here, down, received(down, "xh", 1))
    down_shard = down
    down = gathered(down, ("y", "xl"))

    out_planes = gather_planes(out_shards, ORDERS[:2], (gate_up_dealt,))

    def group_tokens(a):
        return both_tokens(ring_whole(a, Z_RING))

    def group_sum(both):
        return ring_sum_whole(to_low(sum_cores(both)), Z_RING)

    grad_out = out_grad[0]

    pick_a, pick_b, pick_c = (picker(order, d_rows) for order in ORDERS)
    pick_ff = ff_picker(d_rows)
    pick_out = [picker(ORDER_A, d_rows, c_rows, k * d_rows) for k in (0, 1)]

    normed, norm_back = jax.vjp(rms_scale, tokens, norm_gain)
    normed_chip = both_tokens(to_low(normed))
    normed_a, normed_b, normed_c = turned((normed_chip,) * 3, (pick_a, pick_b, pick_c))
    normed_c = after(normed_c, out_planes[0], down_shard)

    q_cols, k_cols = w_query.shape[1], w_key.shape[1]
    projected = [
        by_pieces((left,), pieces, (window,))
        for left, pieces, window in zip((normed_a, normed_b, normed_c), parts, windows_in)
    ]
    mixed_mine = jnp.concatenate([a[:rows_dev] for a in projected], axis=1)
    mixed_got = other_core(jnp.concatenate([a[rows_dev:] for a in projected], axis=1))
    conv_in = jnp.where(first_core, mixed_mine[:, :inner], mixed_got[:, :inner])
    gate_z = jnp.where(first_core, mixed_got[:, :inner], mixed_mine[:, :inner]).astype(jnp.float32)
    qkv_cols = q_cols + 2 * k_cols
    qkv_mine, qkv_got = (a[:, inner : inner + qkv_cols] for a in (mixed_mine, mixed_got))
    queries = join_columns(qkv_mine[:, :q_cols], qkv_got[:, :q_cols])
    keys_low = join_columns(qkv_mine[:, q_cols : q_cols + k_cols], qkv_got[:, q_cols : q_cols + k_cols])
    values_low = join_columns(qkv_mine[:, q_cols + k_cols :], qkv_got[:, q_cols + k_cols :])
    key_value = jnp.stack([a.reshape(rows_dev, KV_HEADS, HEAD_DIM) for a in (keys_low, values_low)], axis=2)
    key_value = key_value.reshape(rows_dev, 2 * KV_HEADS * HEAD_DIM)

    mamba_out_a, attn_out_b = (
        ring_pieces(after(a, conv_in), order[1]) for a, order in zip(out_planes, ORDERS)
    )
    grad_out_group = group_tokens(jnp.pad(after(grad_out, conv_in), ((0, 0), (0, LANES - width))))

    kv_cols = KV_HEADS * HEAD_DIM
    window = jnp.concatenate([shifted(key_value, d) for d in range(reach_blocks, 0, -1)] + [key_value], axis=0)
    edge_rows = after(shifted(conv_in[rows_dev - edge_count :], 1), out_planes[1])

    padded_in = jnp.concatenate([edge_rows, conv_in], axis=0).astype(jnp.float32)
    conved, conv_back = jax.vjp(conv_silu, padded_in, conv_weight, conv_bias)
    conved_low = to_low(conved)
    conv_values = conved_low.astype(jnp.float32)
    selected = product(conved_low, select_full)
    step_raw = to_low(selected[:, :rank_width])
    in_mat = selected[:, rank_width : rank_width + state_width]
    out_mat = selected[:, rank_width + state_width :]
    step_pre = product_nt(step_raw, step_full)
    (step_size, decay_rate), rate_back = jax.vjp(rate_piece, step_pre, step_bias, log_decay)
    total_step = jnp.sum(step_size, axis=0)
    drive = after(step_size * conv_values, window)
    in_lanes, out_lanes = lanes(in_mat), lanes(out_mat)
    end_state = scan_state(step_size, drive, in_lanes, decay_rate)
    queries = after(queries, end_state)
    state_in = chain_carry(total_step, end_state, decay_rate, False)
    scan_out = scan_full(step_size, drive, in_lanes, out_lanes, decay_rate, state_in)
    gated, gate_back = jax.vjp(gate_piece, scan_out, conv_values, gate_z, skip_gain)
    gated_low = after(to_low(gated), grad_out_group)

    span_keys = (reach_blocks + 1) * rows_dev
    segment_row = segment_ids[0]
    padded_segs = jnp.concatenate(
        [jnp.full((reach_blocks * rows_dev,), -1, jnp.int32), segment_row]
    )
    key_segs = lax.dynamic_slice_in_dim(padded_segs, position * rows_dev, span_keys)
    query_segs = lax.dynamic_slice_in_dim(segment_row, position * rows_dev, rows_dev)
    gaps = (reach_blocks * rows_dev + jnp.arange(rows_dev, dtype=jnp.int32))[:, None] - jnp.arange(
        span_keys, dtype=jnp.int32
    )[None, :]
    allowed = (gaps >= 0) & (gaps < WINDOW) & (query_segs[:, None] == key_segs[None, :])
    queries_by_group = by_groups(queries)
    heads_by_group, score_totals = attend(queries_by_group, window, jnp.where(allowed, 0.0, -1e30))
    heads_low = from_groups(heads_by_group)

    heads_b, *gated_a = (
        both_tokens(a) for a in turned((heads_low, gated_low, gated_low), (pick_b, *pick_out))
    )
    branch_out = jnp.concatenate(
        [
            by_pieces((heads_b,), attn_out_b, (window_out_b,), False),
            by_pieces(gated_a, mamba_out_a, windows_out_a, False),
        ],
        axis=1,
    )
    out_mine, out_got = branch_out[:rows_dev], other_core(branch_out[rows_dev:])
    attn_out = join_columns(out_mine[:, :half_width], out_got[:, :half_width])
    mamba_out = join_columns(out_mine[:, half_width:], out_got[:, half_width:])
    hidden_mid, merge_back = jax.vjp(
        merge_piece, tokens, attn_out, mamba_out, attn_gain, mamba_gain
    )
    normed_two, norm_two_back = jax.vjp(rms_scale, hidden_mid, ffn_norm_gain)
    normed_two_ff = group_tokens(turned((to_low(normed_two),), (pick_ff,))[0])
    act_low, d_gate_up, down_part, d_part = feed_forward(normed_two_ff, grad_out_group, gate_up, down)
    d_cores = to_low(sum_cores(d_part))
    d_normed_two = ring_sum_whole(d_cores, Z_RING)
    act_low, d_gate_up = together((act_low, d_gate_up, d_cores))[:2]
    grad_gate_up, grad_down = feed_grads(normed_two_ff, d_gate_up, act_low, grad_out_group)

    gate_up_sum = scattered(grad_gate_up, ("xh", "y", "xl"))[: 4 * d_rows].reshape(4, d_rows, 2 * units)
    gate_up_sum = dealt(gate_up_sum, Z_RING).astype(jnp.float32)
    grad_gate, grad_up = from_units(gate_up_sum[..., :units]), from_units(gate_up_sum[..., units:])
    grad_down = scattered(grad_down, ("y", "xl")).astype(jnp.float32)
    grad_down = grad_down + received(to_low(grad_down), "xh", 1).astype(jnp.float32)
    down_l, down_r = grad_down[:ff_rows, :half_width], grad_down[:ff_rows, half_width:]
    down_got = other_core(to_low(jnp.where(first_core, down_r, down_l))).astype(jnp.float32)
    grad_down = jnp.where(here, jnp.where(first_core, down_l, down_r), down_got)

    d_mid_norm, grad_ffn_norm = norm_two_back(turned_back((d_normed_two,), (pick_ff,), False)[0])
    d_mid = grad_out.astype(jnp.float32) + d_mid_norm
    d_tokens_res, d_attn_out, d_mamba_out, grad_attn_gain, grad_mamba_gain = merge_back(d_mid)
    d_attn_low, d_mamba_low = to_low(d_attn_out), to_low(d_mamba_out)
    d_branch = jnp.concatenate(
        [d_attn_low[:, :half_width], d_mamba_low[:, :half_width], d_attn_low[:, half_width:], d_mamba_low[:, half_width:]],
        axis=1,
    )
    d_branch_half = own_columns(d_branch)
    d_attn_half, d_mamba_half = d_branch_half[:, :half_width], d_branch_half[:, half_width:]
    d_gated_a = by_pieces_nt((d_mamba_half, d_mamba_half), mamba_out_a, windows_out_a)
    d_heads_b = by_pieces_nt((d_attn_half,), attn_out_b, (window_out_b,))
    d_branch = to_low(sum_cores(jnp.concatenate([*d_gated_a, *d_heads_b], axis=1)))
    d_gated_a, d_heads_b = [d_branch[:, k * LANES : (k + 1) * LANES] for k in (0, 1)], d_branch[:, 2 * LANES :]
    d_gated = turned_back(d_gated_a, pick_out, False, True, inner)[0]
    d_heads = turned_back((d_heads_b,), (pick_b,), True)[0]

    d_scan, d_conv_gate, d_gate_z, grad_skip = gate_back(d_gated)
    d_state_in = adjoint_state(step_size, d_scan, out_lanes, decay_rate)
    d_heads, d_attn_half, d_mamba_half, down_part = together(
        (d_heads, d_attn_half, d_mamba_half, down_part, d_state_in)
    )[:4]
    output = to_low(hidden_mid + group_sum(down_part)[:, :width])[None]

    d_queries, d_window = attend_back(
        queries_by_group, window, jnp.where(allowed.T, 0.0, -1e30), score_totals, by_groups(d_heads)
    )
    d_queries = from_groups(d_queries)
    d_key_value = d_window[reach_blocks * rows_dev :].astype(jnp.float32)
    for d in range(1, reach_blocks + 1):
        piece = d_window[(reach_blocks - d) * rows_dev : (reach_blocks - d + 1) * rows_dev]
        d_key_value = d_key_value + shifted(piece, -d).astype(jnp.float32)
    d_key_value = to_low(d_key_value).reshape(rows_dev, KV_HEADS, 2, HEAD_DIM)
    d_keys, d_values = (d_key_value[:, :, k].reshape(rows_dev, kv_cols) for k in (0, 1))

    kv_half = kv_cols // 2
    d_qkv_half = own_columns(
        jnp.concatenate(
            [
                d_queries[:, :q_cols],
                d_keys[:, :kv_half],
                d_values[:, :kv_half],
                d_queries[:, q_cols:],
                d_keys[:, kv_half:],
                d_values[:, kv_half:],
            ],
            axis=1,
        )
    )
    rings = sum_rings(
        (grad_pieces(gated_a, d_mamba_half, HALVES), grad_pieces((heads_b,), d_attn_half, HALVES)), ORDERS[:2]
    )

    d_end = chain_carry(total_step, d_state_in, decay_rate, True, rings)
    d_step, d_conv_scan, d_rate, d_in_mat, d_out_mat = scan_back(
        step_size, conv_values, d_scan, in_lanes, out_lanes, decay_rate, state_in, d_end
    )
    d_step_pre, grad_step_bias, grad_log_decay = rate_back((d_step, d_rate))
    d_step_low = to_low(d_step_pre)
    grad_step_w = product_tn(d_step_low, step_raw)
    d_step_raw = product(d_step_low, step_full)
    d_selected = to_low(jnp.concatenate([d_step_raw, d_in_mat, d_out_mat], axis=1))
    grad_select = product_tn(conved_low, d_selected)
    d_conved = product_nt(d_selected, select_full) + d_conv_gate + d_conv_scan
    d_padded, grad_conv_w, grad_conv_b = conv_back(d_conved)
    edge_back = shifted(to_low(d_padded[:edge_count]), -1).astype(jnp.float32)
    d_conv_in = d_padded[edge_count:] + jnp.concatenate(
        [jnp.zeros((rows_dev - edge_count, inner), jnp.float32), edge_back], axis=0
    )
    d_conv_in = after(d_conv_in, gate_up_sum)
    d_mixed_half = own_columns(to_low(jnp.concatenate([d_conv_in, d_gate_z], axis=1)))
    d_mixed_a, d_mixed_b, d_mixed_c = (
        d_mixed_half[:, :cut_a],
        d_mixed_half[:, cut_a:cut_b],
        jnp.concatenate([d_mixed_half[:, cut_b:], d_qkv_half], axis=1),
    )

    ring_a, ring_b, ring_c = sum_rings(
        [
            grad_pieces((left,), grad, HALVES)
            for left, grad in ((normed_a, d_mixed_a), (normed_b, d_mixed_b), (normed_c, d_mixed_c))
        ],
        ORDERS,
    )
    sum_a, sum_b, sum_c = sum_planes(
        [jnp.concatenate([ring_a, rings[0]], axis=1), jnp.concatenate([ring_b, rings[1]], axis=1), ring_c], ORDERS
    )
    sum_a, out_sum_a = sum_a[:, :cut_a], sum_a[:, cut_a:]
    sum_b, grad_attn_out = sum_b[:, : cut_b - cut_a], sum_b[:, cut_b - cut_a :]
    grad_mamba_out = jnp.concatenate([out_sum_a[:, :half_width], out_sum_a[:, half_width:]], axis=0)
    grad_mamba_in = jnp.concatenate([sum_a, sum_b, sum_c[:, :mixed_c]], axis=1)
    grad_qkv = sum_c[:, mixed_c:]
    grad_query = grad_qkv[:, :q_cols]
    grad_key, grad_value = grad_qkv[:, q_cols : q_cols + k_cols], grad_qkv[:, q_cols + k_cols :]

    d_normed = turned_back(
        [
            by_pieces_nt((grad,), pieces, (window,))[0]
            for grad, pieces, window in zip((d_mixed_a, d_mixed_b, d_mixed_c), parts, windows_in)
        ],
        (pick_a, pick_b, pick_c),
        False,
        True,
    )[0]
    d_tokens_norm, grad_norm = norm_back(sum_cores(d_normed))
    input_grad = to_low(d_tokens_res + d_tokens_norm)[None]

    smalls = (
        grad_norm,
        grad_conv_w,
        grad_conv_b,
        grad_step_bias,
        grad_log_decay,
        grad_skip,
        grad_attn_gain,
        grad_mamba_gain,
        grad_ffn_norm,
    )
    channel_rows = [a.reshape(-1, inner) for a in smalls[1:6]]
    gains = jnp.concatenate([smalls[0], *smalls[6:]]).reshape(-1, inner)
    select_rows = jnp.stack(
        [
            jnp.pad(jnp.concatenate([sel, stp], axis=1), ((0, 0), (0, 128 - sel_half - step_half)))
            for sel, stp in zip(jnp.split(grad_select, 2, axis=1), jnp.split(grad_step_w, 2, axis=1))
        ]
    )
    select_rows = select_rows.reshape(128, c_rows, 128)
    totals, select_sum = sum_all(jnp.concatenate([gains, *channel_rows]), select_rows)
    grad_select, grad_step = select_sum[:, :sel_half], select_sum[:, sel_half : sel_half + step_half]
    gain_sums = totals[: gains.shape[0]].reshape(4, width)
    at, channel_sums = gains.shape[0], []
    for a in channel_rows:
        channel_sums.append(totals[at : at + a.shape[0]])
        at += a.shape[0]
    totals = [
        gain_sums[0],
        channel_sums[0],
        *(channel_sums[k][0] for k in (1, 2)),
        channel_sums[3],
        channel_sums[4][0],
        *gain_sums[1:],
    ]
    return (
        output,
        input_grad,
        totals[0],
        grad_query,
        grad_key,
        grad_value,
        grad_attn_out,
        grad_mamba_in,
        totals[1],
        totals[2],
        grad_select,
        grad_step,
        totals[3],
        totals[4],
        totals[5],
        grad_mamba_out,
        totals[6],
        totals[7],
        totals[8],
        grad_gate,
        grad_up,
        grad_down,
    )


def solution(mesh):
    torus = Mesh(
        mesh.devices.reshape(mesh.shape["head"], 2, 4, 4, mesh.shape["seq"]),
        ("head", "xh", "y", "z", "xl"),
    )
    weight = P(BLK_SEQ, "head")
    rows = P("xl", HEAD_BLK, None)
    in_specs = (rows, P("xl", None), rows, P()) + (weight,) * 5
    in_specs += (P(), P(), weight, weight, P(), P(), P(), weight, P(), P(), P()) + (weight,) * 3
    out_specs = (rows, rows, P()) + (weight,) * 5
    out_specs += (P(), P(), weight, weight, P(), P(), P(), weight, P(), P(), P()) + (weight,) * 3
    return jax.shard_map(
        shards, mesh=torus, in_specs=in_specs, out_specs=out_specs, check_vma=False
    )
```

```python
import functools
import math

import jax
import jax.numpy as jnp
import numpy as np
from jax import lax
from jax.experimental import pallas as pl
from jax.experimental.pallas import tpu as pltpu
from jax.sharding import Mesh
from jax.sharding import PartitionSpec as P

HEADS = 25
KV_HEADS = 5
HEAD_DIM = 64
WINDOW = 1024
RANK = 100
X_RING = ("xh", "xl")
ROWS = ("head", "xh", "y")
EVERY = ("head", "xh", "y", "z", "xl")
Y_RING = "y"
Z_RING = "z"
BLK_SEQ = ("xh", "y", "z", "xl")
HEAD_BLK = ("head", "xh", "y", "z")
EPSILON = 1e-06
LOG2_E = 1.0 / math.log(2.0)
FF_PAD = 88
WIDTH = HEADS * HEAD_DIM
LANES = -(-WIDTH // 128) * 128


def received(a, axis, d):
    n = lax.axis_size(axis)
    return lax.ppermute(a, axis, [((i + d) % n, i) for i in range(n)])


def other_core(a):
    return received(a, "head", 1)


def shifted(a, distance, axis=HEAD_BLK):
    n = lax.axis_size(axis)
    return lax.ppermute(a, axis, [(i - distance, i) for i in range(n) if 0 <= i - distance < n])


def after(value, *others):
    return lax.optimization_barrier((value, *others))[0]


def dealt(blocks, axis):
    return lax.all_to_all(blocks, axis, 0, 0, tiled=True)


def shown(a, axis):
    return dealt(jnp.broadcast_to(a[None], (lax.axis_size(axis), *a.shape)), axis)


def summed(blocks, axis):
    return jnp.sum(dealt(blocks, axis).astype(jnp.float32), axis=0)


ORDER_A = (("y", "z"), X_RING)
ORDER_B = (("xh", "z", "xl"), Y_RING)
ORDER_C = (("xh", "y", "xl"), Z_RING)
ORDERS = (ORDER_A, ORDER_B, ORDER_C)


def together(values):
    return lax.optimization_barrier(tuple(values))


def ring_pieces(a, axis):
    half = a.shape[0] // 2
    up, down = received(a, axis, 1), received(a, axis, -1)
    return [a, up, received(up[:half], axis, 1), received(down[half:], axis, -1), down]


def ring_whole(a, axis):
    return jnp.concatenate([a] + [received(a, axis, j) for j in (1, 2, 3)], axis=0)


def ring_in_order(a, axis):
    me = lax.axis_index(axis)
    out = jnp.zeros((4, *a.shape), a.dtype)
    for j, part in enumerate([a] + [received(a, axis, j) for j in (1, 2, 3)]):
        out = lax.dynamic_update_index_in_dim(out, part, lax.rem(me + j, 4), 0)
    return out.reshape(4 * a.shape[0], a.shape[1])


def gather_planes(shards, orders, last=()):
    planes = []
    for a, order in zip(shards, orders):
        planes.append(shown(after(a, *last), order[0]).reshape(16 * a.shape[0], a.shape[1]))
        last = planes[-1:]
    return planes


def ring_sum(pieces, axis):
    own, up, far_low, far_high, down = pieces
    half = far_low.shape[0]
    low = own.dtype
    from_down, from_up = received(far_low, axis, -1), received(far_high, axis, 1)
    to_up = jnp.concatenate(
        [(up[:half].astype(jnp.float32) + from_down.astype(jnp.float32)).astype(low), up[half:]]
    )
    to_down = jnp.concatenate(
        [down[:half], (down[half:].astype(jnp.float32) + from_up.astype(jnp.float32)).astype(low)]
    )
    return (
        own.astype(jnp.float32)
        + received(to_up, axis, -1).astype(jnp.float32)
        + received(to_down, axis, 1).astype(jnp.float32)
    )


def ring_sum_whole(whole, axis):
    rows = whole.shape[0] // 4
    total = whole[:rows].astype(jnp.float32)
    for j in (1, 2, 3):
        total = total + received(whole[j * rows : (j + 1) * rows], axis, -j).astype(jnp.float32)
    return total


def sum_rings(grads, orders):
    return [to_low(ring_sum(a, order[1])) for a, order in zip(grads, orders)]


def sum_planes(rings, orders):
    return [summed(a.reshape(16, a.shape[0] // 16, a.shape[1]), order[0]) for a, order in zip(rings, orders)]


def ring_sum_in_order(whole, axis):
    rows = whole.shape[0] // 4
    blocks = whole.reshape(4, rows, whole.shape[1])
    me = lax.axis_index(axis)
    total = 0.0
    for j in range(4):
        block = lax.dynamic_index_in_dim(blocks, lax.rem(me + j, 4), 0, keepdims=False)
        total = total + (received(block, axis, -j) if j else block).astype(jnp.float32)
    return total


def padded_index(index):
    return jnp.pad(index, (0, LANES - WIDTH), constant_values=-1)


def picker(order, rows, stride=None, offset=0):
    stride = stride or rows
    ring, inside = np.indices((4, 16 * rows))
    turned = lax.rem(lax.axis_index(order[1]) + jnp.asarray(ring, jnp.int32), 4)
    block, row = inside // rows, jnp.asarray(inside % rows, jnp.int32)
    if order is ORDER_A:
        xh, y, z, xl = turned // 2, block // 4, block % 4, turned % 2
    elif order is ORDER_B:
        xh, y, z, xl = block // 8, turned, block // 2 % 4, block % 2
    else:
        xh, y, z, xl = block // 8, block // 2 % 4, turned, block % 2
    return padded_index(((((xh * 4 + y) * 4 + z) * 2 + xl) * stride + offset + row).reshape(-1))


def ff_picker(rows):
    xh, y, xl, z, row = np.indices((2, 4, 2, 4, rows))
    index = (((((xh * 4 + y) * 4 + z) * 2 + xl) * rows + row)).reshape(16, 4 * rows)
    return jnp.asarray(np.pad(index, ((0, 0), (0, LANES // 16 - 4 * rows)), constant_values=-1).reshape(-1), jnp.int32)


def gathered(a, axes):
    return lax.all_gather(a, axes).reshape(-1, a.shape[1])


def scattered(a, axes):
    blocks = a.reshape(lax.axis_size(axes), -1, a.shape[1])
    return lax.optimization_barrier(lax.psum_scatter(blocks, axes, scatter_dimension=0))


HALVES = (WIDTH // 4, WIDTH // 4, WIDTH // 8, WIDTH // 8, WIDTH // 4)


def bounds(sizes):
    stops = np.cumsum(sizes)
    return [(int(stop - size), int(stop)) for size, stop in zip(sizes, stops)]


def rows_of(pieces):
    return bounds([a.shape[0] for a in pieces])


def dot_nn(a, b):
    return jnp.dot(a, b, preferred_element_type=jnp.float32)


def dot_nt(a, b):
    return lax.dot_general(a, b, (((1,), (1,)), ((), ())), preferred_element_type=jnp.float32)


def dot_tn(a, b):
    return lax.dot_general(a, b, (((0,), (0,)), ((), ())), preferred_element_type=jnp.float32)


def whole_call(kernel, operands, outs, flops):
    sizes = sum(a.size * a.dtype.itemsize for a in (*operands, *outs))
    return pl.pallas_call(
        kernel,
        out_shape=outs,
        in_specs=[pl.BlockSpec(memory_space=pltpu.VMEM)] * len(operands),
        out_specs=[pl.BlockSpec(memory_space=pltpu.VMEM)] * len(outs),
        compiler_params=pltpu.CompilerParams(vmem_limit_bytes=40 * 2**20),
        cost_estimate=pl.CostEstimate(flops=flops, bytes_accessed=sizes, transcendentals=0),
    )(*operands)


def out_array(rows, cols, low=True):
    return jax.ShapeDtypeStruct((rows, cols), jnp.bfloat16 if low else jnp.float32)


def clear_rest(ref, start):
    if start < ref.shape[1]:
        ref[:, start:] = jnp.zeros((ref.shape[0], ref.shape[1] - start), ref.dtype)


def nn_kernel(windows, *refs):
    count = len(windows)
    lefts, pieces, y_ref = refs[:count], refs[count:-1], refs[-1]
    width = windows[0][1] - windows[0][0]
    for at in range(0, width, 512):
        stop = min(at + 512, width)
        total = 0.0
        for left, (low, _) in zip(lefts, windows):
            for (start, end), piece in zip(rows_of(pieces), pieces):
                total = total + dot_nn(left[:, start:end], piece[:, low + at : low + stop])
        y_ref[:, at:stop] = total.astype(y_ref.dtype)
    clear_rest(y_ref, width)


def by_pieces(lefts, pieces, windows, low=True):
    rows, width = lefts[0].shape[0], windows[0][1] - windows[0][0]
    flops = 2 * rows * width * sum(a.shape[1] for a in lefts)
    return whole_call(
        functools.partial(nn_kernel, windows), (*lefts, *pieces), [out_array(rows, -(-width // 128) * 128 if low else width, low)], flops
    )[0]


def nt_kernel(windows, *refs):
    count = len(windows)
    grads, pieces, outs = refs[:count], refs[count:-count], refs[-count:]
    for grad, (low, high), out in zip(grads, windows, outs):
        for (start, end), piece in zip(rows_of(pieces), pieces):
            out[:, start:end] = dot_nt(grad[:, : high - low], piece[:, low:high]).astype(out.dtype)
        clear_rest(out, rows_of(pieces)[-1][1])


def by_pieces_nt(grads, pieces, windows):
    rows, depth = grads[0].shape[0], sum(a.shape[0] for a in pieces)
    flops = 2 * rows * depth * sum(a.shape[1] for a in grads)
    return whole_call(
        functools.partial(nt_kernel, windows), (*grads, *pieces), [out_array(rows, -(-depth // 128) * 128)] * len(grads), flops
    )


def tn_kernel(sizes, right, *refs):
    lefts, outs = refs[: -len(sizes)], refs[-len(sizes) :]
    width = right.shape[1]
    for k, left in enumerate(lefts):
        for (start, end), out in zip(bounds(sizes), outs):
            out[:, k * width : (k + 1) * width] = dot_tn(left[:, start:end], right[...]).astype(out.dtype)


def grad_pieces(lefts, right, sizes):
    outs = [out_array(size, right.shape[1] * len(lefts)) for size in sizes]
    flops = 2 * right.size * sum(sizes) * len(lefts)
    return whole_call(functools.partial(tn_kernel, sizes), (right, *lefts), outs, flops)


def feed_kernel(x_ref, g_ref, up_ref, down_ref, act_ref, d_ref, y_ref, dx_ref):
    units = down_ref.shape[0]
    both = dot_nn(x_ref[...], up_ref[...])
    gate, up = both[:, :units], both[:, units:]
    sig = 1.0 / (1.0 + jnp.exp(-gate))
    silu = gate * sig
    act = (silu * up).astype(jnp.bfloat16)
    act_ref[...] = act
    y_ref[:, :WIDTH] = dot_nn(act, down_ref[...]).astype(y_ref.dtype)
    clear_rest(y_ref, WIDTH)
    d_act = dot_nt(g_ref[:, :WIDTH], down_ref[...])
    d_ref[:, :units] = (d_act * up * (sig * (1.0 + gate * (1.0 - sig)))).astype(d_ref.dtype)
    d_ref[:, units:] = (d_act * silu).astype(d_ref.dtype)
    dx_ref[...] = dot_nt(d_ref[...], up_ref[...]).astype(dx_ref.dtype)


def feed_forward(x, g, gate_up, down):
    tokens, width = x.shape
    units = down.shape[0]
    block = 256

    def rows(cols):
        return pl.BlockSpec((block, cols), lambda i: (i, 0))

    def fixed(a):
        return pl.BlockSpec(a.shape, lambda i: (0, 0))

    return pl.pallas_call(
        feed_kernel,
        grid=(tokens // block,),
        in_specs=[rows(width), rows(width), fixed(gate_up), fixed(down)],
        out_specs=[rows(units), rows(2 * units), rows(width), rows(width)],
        out_shape=[out_array(tokens, c) for c in (units, 2 * units, width, width)],
        compiler_params=pltpu.CompilerParams(
            dimension_semantics=("arbitrary",), vmem_limit_bytes=48 * 2**20
        ),
        cost_estimate=pl.CostEstimate(
            flops=2 * tokens * width * units * 6, bytes_accessed=2 * tokens * (4 * width + 3 * units), transcendentals=tokens * units
        ),
    )(x, g, gate_up, down)


def feed_grads_kernel(x_ref, d_ref, act_ref, g_ref, up_ref, down_ref):
    up_ref[...] = dot_tn(x_ref[...], d_ref[...]).astype(up_ref.dtype)
    down_ref[...] = dot_tn(act_ref[...], g_ref[:, :WIDTH]).astype(down_ref.dtype)


def feed_grads(x, d, act, g):
    outs = [out_array(x.shape[1], d.shape[1]), out_array(act.shape[1], WIDTH)]
    flops = 2 * x.shape[0] * x.shape[1] * (d.shape[1] + act.shape[1])
    return whole_call(feed_grads_kernel, (x, d, act, g), outs, flops)


def one_hot(index_ref, start, stop):
    width = index_ref.shape[1]
    rows = lax.broadcasted_iota(jnp.int32, (stop - start, width), 0) + start
    return jnp.where(rows == index_ref[...], 1.0, 0.0).astype(jnp.bfloat16)


def turn_kernel(count, *refs):
    lefts, indices, outs = refs[:count], refs[count : 2 * count], refs[2 * count :]
    for left, index, out in zip(lefts, indices, outs):
        total = 0.0
        for start in range(0, left.shape[1], 400):
            total = total + dot_nn(left[:, start : start + 400], one_hot(index, start, start + 400))
        out[...] = total.astype(out.dtype)


def turned(lefts, indices):
    outs = [out_array(a.shape[0], index.shape[0]) for a, index in zip(lefts, indices)]
    rows = [index.reshape(1, -1) for index in indices]
    flops = sum(2 * a.size * a.shape[1] for a in lefts)
    return whole_call(functools.partial(turn_kernel, len(lefts)), (*lefts, *rows), outs, flops)


def turn_back_kernel(count, *refs):
    lefts, indices, outs = refs[:count], refs[count : 2 * count], refs[2 * count :]
    for start in range(0, outs[0].shape[1], 400):
        total = 0.0
        for k, (left, index) in enumerate(zip(lefts, indices)):
            hot = one_hot(index, start, start + 400)
            if left.dtype == jnp.float32:
                high = left[...].astype(jnp.bfloat16)
                rest = (left[...] - high.astype(jnp.float32)).astype(jnp.bfloat16)
                part = dot_nt(high, hot) + dot_nt(rest, hot)
            else:
                part = dot_nt(left[...], hot)
            if len(outs) > 1:
                outs[k][:, start : start + 400] = part.astype(outs[k].dtype)
            total = total + part
        if len(outs) == 1:
            outs[0][:, start : start + 400] = total.astype(outs[0].dtype)


def turned_back(lefts, indices, low, summed=False, width=WIDTH):
    rows = lefts[0].shape[0]
    outs = [out_array(rows, width, low)] * (1 if summed else len(lefts))
    hots = [index.reshape(1, -1) for index in indices]
    flops = sum(2 * a.size * width for a in lefts)
    return whole_call(functools.partial(turn_back_kernel, len(lefts)), (*lefts, *hots), outs, flops)


def join_columns(mine, got):
    first = lax.axis_index("head") == 0
    return jnp.concatenate([jnp.where(first, mine, got), jnp.where(first, got, mine)], axis=1)


def own_tokens(both):
    rows = both.shape[0] // 2
    return join_columns(both[:rows], other_core(both[rows:]))


def own_columns(a):
    first = lax.axis_index("head") == 0
    low, high = jnp.split(a, 2, axis=1)
    mine, theirs = jnp.where(first, low, high), jnp.where(first, high, low)
    return jnp.concatenate([mine, other_core(theirs)], axis=0)


def both_tokens(a):
    return jnp.concatenate([a, other_core(a)], axis=0)


def sum_cores(both):
    rows = both.shape[0] // 2
    return both[:rows].astype(jnp.float32) + other_core(to_low(both[rows:])).astype(jnp.float32)


def chain_kernel(reverse, packed_ref, rate_ref, out_ref):
    rate = rate_ref[...] * LOG2_E
    count, states = packed_ref.shape[0], rate.shape[0]

    def one(k, state):
        p = count - 1 - k if reverse else k
        out_ref[p] = state
        packed = packed_ref[p].astype(jnp.float32)
        total = packed[states : states + 1] + packed[states + 1 : states + 2]
        return jnp.exp2(total * rate) * state + packed[:states]

    lax.fori_loop(0, count, one, jnp.zeros(rate.shape, jnp.float32))


def chain_carry(total_step, state, decay_rate, reverse):
    count = lax.axis_size(HEAD_BLK)
    states, channels = state.shape
    high = lax.reduce_precision(total_step, 8, 7)
    packed = jnp.concatenate([state, high[None], (total_step - high)[None]]).astype(jnp.bfloat16)

    def tiles(a):
        padded = jnp.pad(a, ((0, 0), (0, count * 128 - channels)))
        return padded.reshape(a.shape[0], count, 128).transpose(1, 0, 2)

    rate = lax.dynamic_index_in_dim(tiles(decay_rate), lax.axis_index(HEAD_BLK), 0, keepdims=False)
    chained = pl.pallas_call(
        functools.partial(chain_kernel, reverse),
        out_shape=jax.ShapeDtypeStruct((count, states, 128), jnp.float32),
    )(dealt(tiles(packed), HEAD_BLK), rate)
    got = dealt(to_low(chained), HEAD_BLK)[: channels // 128]
    return got.transpose(1, 0, 2).reshape(states, channels).astype(jnp.float32)


def sum_all(values, owned):
    count = lax.axis_size(EVERY)
    lines = values.reshape(-1, 128)
    each = -(-lines.shape[0] // count)
    padded = jnp.pad(lines, ((0, count * each - lines.shape[0]), (0, 0))).reshape(count, each, 128)
    mine = summed(jnp.concatenate([to_low(owned), to_low(padded)], axis=1), EVERY)
    all_lines = shown(mine[owned.shape[1] :], EVERY).reshape(-1, 128)
    return all_lines[: lines.shape[0]].reshape(values.shape), mine[: owned.shape[1]]


def rms_scale(values, gain):
    return values * lax.rsqrt(jnp.mean(values * values, axis=-1, keepdims=True) + EPSILON) * gain


def to_low(values):
    return values.astype(jnp.bfloat16)


def product(left, right):
    return jnp.dot(left, right, preferred_element_type=jnp.float32)


def product_tn(left, right):
    return lax.dot_general(
        left, right, (((0,), (0,)), ((), ())), preferred_element_type=jnp.float32
    )


def product_nt(left, right):
    return lax.dot_general(
        left, right, (((1,), (1,)), ((), ())), preferred_element_type=jnp.float32
    )


def chain_combine(earlier, later):
    return (earlier[0] * later[0], later[0] * earlier[1] + later[1])


def conv_silu(padded, conv_weight, conv_bias):
    tap_count = conv_weight.shape[0]
    length = padded.shape[0] - tap_count + 1
    total_sum = conv_bias
    for tap_index in range(tap_count):
        total_sum = total_sum + conv_weight[tap_index] * padded[tap_index : tap_index + length]
    return jax.nn.silu(total_sum)


def rate_piece(step_pre, step_bias, log_decay):
    return (jax.nn.softplus(step_pre + step_bias), -jnp.exp(log_decay))


def gate_piece(scan_out, conv_values, gate_z, skip_gain):
    return (scan_out + skip_gain * conv_values) * jax.nn.silu(gate_z)


def merge_piece(tokens, attn_out, mamba_out, attn_gain, mamba_gain):
    return tokens + 0.5 * (rms_scale(attn_out, attn_gain) + rms_scale(mamba_out, mamba_gain))


def swiglu(gate_val, up_val):
    return jax.nn.silu(gate_val) * up_val


SCAN_TILE = 640


def scan_state_kernel(step_ref, drive_ref, in_ref, rate_ref, end_ref):
    rate = rate_ref[...] * LOG2_E
    width = rate.shape[1]

    def eight(k, state):
        base = pl.multiple_of(k * 8, 8)
        step, drive = step_ref[pl.ds(base, 8), :], drive_ref[pl.ds(base, 8), :]
        for i in range(8):
            decay = jnp.exp2(step[i : i + 1] * rate)
            in_now = jnp.tile(in_ref[base + i], (1, width // 128))
            state = decay * state + in_now * drive[i : i + 1]
        return state

    end_ref[...] = lax.fori_loop(0, step_ref.shape[0] // 8, eight, jnp.zeros(rate.shape, jnp.float32))


def scan_full_kernel(step_ref, drive_ref, in_ref, out_ref, rate_ref, start_ref, y_ref):
    rate = rate_ref[...] * LOG2_E
    width = rate.shape[1]

    def eight(k, state):
        base = pl.multiple_of(k * 8, 8)
        step, drive = step_ref[pl.ds(base, 8), :], drive_ref[pl.ds(base, 8), :]
        rows = []
        for i in range(8):
            decay = jnp.exp2(step[i : i + 1] * rate)
            in_now = jnp.tile(in_ref[base + i], (1, width // 128))
            out_now = jnp.tile(out_ref[base + i], (1, width // 128))
            state = decay * state + in_now * drive[i : i + 1]
            rows.append(jnp.sum(out_now * state, axis=0, keepdims=True))
        y_ref[pl.ds(base, 8), :] = jnp.concatenate(rows, axis=0)
        return state

    lax.fori_loop(0, step_ref.shape[0] // 8, eight, start_ref[...])


def adjoint_state_kernel(step_ref, d_scan_ref, out_ref, rate_ref, d_start_ref):
    rate = rate_ref[...] * LOG2_E
    width = rate.shape[1]
    blocks = step_ref.shape[0] // 8

    def eight(k, carry):
        base = pl.multiple_of((blocks - 1 - k) * 8, 8)
        step, d_scan = step_ref[pl.ds(base, 8), :], d_scan_ref[pl.ds(base, 8), :]
        for i in range(7, -1, -1):
            out_now = jnp.tile(out_ref[base + i], (1, width // 128))
            carry = jnp.exp2(step[i : i + 1] * rate) * (out_now * d_scan[i : i + 1] + carry)
        return carry

    d_start_ref[...] = lax.fori_loop(0, blocks, eight, jnp.zeros(rate.shape, jnp.float32))


def scan_back_kernel(
    step_ref,
    conv_ref,
    d_scan_ref,
    in_ref,
    out_ref,
    rate_ref,
    start_ref,
    d_end_ref,
    d_step_ref,
    d_conv_ref,
    d_rate_ref,
    d_in_ref,
    d_out_ref,
    states_ref,
    decays_ref,
):
    true_rate = rate_ref[...]
    rate = true_rate * LOG2_E
    width = rate.shape[1]
    tiles = width // 128
    blocks = step_ref.shape[0] // 8

    @pl.when(pl.program_id(0) == 0)
    def _():
        d_in_ref[...] = jnp.zeros(d_in_ref.shape, jnp.float32)
        d_out_ref[...] = jnp.zeros(d_out_ref.shape, jnp.float32)

    def folded(a):
        total = a[:, :128]
        for j in range(1, tiles):
            total = total + a[:, j * 128 : (j + 1) * 128]
        return total

    states_ref[0] = start_ref[...]

    def forward(k, state):
        base = pl.multiple_of(k * 8, 8)
        step, conv = step_ref[pl.ds(base, 8), :], conv_ref[pl.ds(base, 8), :]
        d_scan = d_scan_ref[pl.ds(base, 8), :]
        drive = step * conv
        for i in range(8):
            decay = jnp.exp2(step[i : i + 1] * rate)
            in_now = jnp.tile(in_ref[base + i], (1, tiles))
            state = decay * state + in_now * drive[i : i + 1]
            decays_ref[base + i] = decay
            states_ref[base + i + 1] = state
            d_out_ref[base + i] += folded(d_scan[i : i + 1] * state)
        return state

    lax.fori_loop(0, blocks, forward, start_ref[...])

    def backward(k, carried):
        carry, d_rate = carried
        base = pl.multiple_of((blocks - 1 - k) * 8, 8)
        step, conv = step_ref[pl.ds(base, 8), :], conv_ref[pl.ds(base, 8), :]
        d_scan = d_scan_ref[pl.ds(base, 8), :]
        drive = step * conv
        through_rate, through_drive = [], []
        for i in range(7, -1, -1):
            in_now = jnp.tile(in_ref[base + i], (1, tiles))
            out_now = jnp.tile(out_ref[base + i], (1, tiles))
            adjoint = out_now * d_scan[i : i + 1] + carry
            carry = decays_ref[base + i] * adjoint
            before = carry * states_ref[base + i]
            d_rate = d_rate + before * step[i : i + 1]
            through_rate.append(jnp.sum(true_rate * before, axis=0, keepdims=True))
            through_drive.append(jnp.sum(adjoint * in_now, axis=0, keepdims=True))
            d_in_ref[base + i] += folded(adjoint * drive[i : i + 1])
        by_rate = jnp.concatenate(through_rate[::-1], axis=0)
        by_drive = jnp.concatenate(through_drive[::-1], axis=0)
        d_step_ref[pl.ds(base, 8), :] = by_rate + by_drive * conv
        d_conv_ref[pl.ds(base, 8), :] = by_drive * step
        return carry, d_rate

    zero = jnp.zeros(rate.shape, jnp.float32)
    d_rate_ref[...] = lax.fori_loop(0, blocks, backward, (d_end_ref[...], zero))[1]


def scan_specs(rows, states):
    tokens = pl.BlockSpec((rows, SCAN_TILE), lambda i: (0, i))
    maps = pl.BlockSpec((rows, states, 128), lambda i: (0, 0, 0))
    state = pl.BlockSpec((states, SCAN_TILE), lambda i: (0, i))
    return tokens, maps, state


def scan_call(kernel, operands, in_kinds, outs, out_kinds, scratch=(), flops=8, exps=1):
    rows, channels = operands[0].shape
    states = 16
    kinds = dict(zip("tms", scan_specs(rows, states)))
    shapes = {"t": (rows, channels), "m": (rows, states, 128), "s": (states, channels)}
    work = rows * states * channels
    return pl.pallas_call(
        kernel,
        grid=(channels // SCAN_TILE,),
        in_specs=[kinds[k] for k in in_kinds],
        out_specs=[kinds[k] for k in out_kinds],
        out_shape=[jax.ShapeDtypeStruct(shapes[k], jnp.float32) for k in out_kinds],
        scratch_shapes=scratch,
        compiler_params=pltpu.CompilerParams(
            dimension_semantics=("arbitrary",), vmem_limit_bytes=(36 if scratch else 16) * 2**20
        ),
        cost_estimate=pl.CostEstimate(
            flops=work * flops, bytes_accessed=4 * rows * channels * 4, transcendentals=work * exps
        ),
    )(*operands)


def lanes(a):
    return jnp.broadcast_to(a[:, :, None], (*a.shape, 128))


def scan_state(step_size, drive, in_lanes, decay_rate):
    return scan_call(scan_state_kernel, (step_size, drive, in_lanes, decay_rate), "ttms", 1, "s")[0]


def scan_full(step_size, drive, in_lanes, out_lanes, decay_rate, state_in):
    operands = (step_size, drive, in_lanes, out_lanes, decay_rate, state_in)
    return scan_call(scan_full_kernel, operands, "ttmmss", 1, "t")[0]


def adjoint_state(step_size, d_scan, out_lanes, decay_rate):
    return scan_call(adjoint_state_kernel, (step_size, d_scan, out_lanes, decay_rate), "ttms", 1, "s")[0]


def scan_back(step_size, conv_values, d_scan, in_lanes, out_lanes, decay_rate, state_in, d_end):
    rows, states = step_size.shape[0], decay_rate.shape[0]
    scratch = (
        pltpu.VMEM((rows + 1, states, SCAN_TILE), jnp.float32),
        pltpu.VMEM((rows, states, SCAN_TILE), jnp.float32),
    )
    operands = (step_size, conv_values, d_scan, in_lanes, out_lanes, decay_rate, state_in, d_end)
    d_step, d_conv, d_rate, d_in, d_out = scan_call(
        scan_back_kernel, operands, "tttmmsss", 5, "ttsmm", scratch, flops=24
    )
    return d_step, d_conv, d_rate, jnp.sum(d_in, axis=-1), jnp.sum(d_out, axis=-1)


SCORE_SCALE = 1.0 / math.sqrt(HEAD_DIM)
GROUP = HEADS // KV_HEADS


def attend_kernel(q_ref, window_ref, bias_ref, out_ref, total_ref):
    keys, values = window_ref[:, :HEAD_DIM], window_ref[:, HEAD_DIM:]
    for h in range(GROUP):
        lanes = slice(h * HEAD_DIM, (h + 1) * HEAD_DIM)
        scores = dot_nt(q_ref[0, :, lanes], keys) * SCORE_SCALE + bias_ref[...]
        top = jnp.max(scores, axis=1, keepdims=True)
        weights = jnp.exp(scores - top)
        total = jnp.sum(weights, axis=1, keepdims=True)
        low = (weights * (1.0 / total)).astype(jnp.bfloat16)
        out_ref[0, :, lanes] = dot_nn(low, values).astype(out_ref.dtype)
        total_ref[0, :, h : h + 1] = top + jnp.log(total)


def attend_back_kernel(q_ref, window_ref, bias_ref, total_ref, d_ref, dq_ref, d_window_ref):
    keys, values = window_ref[:, :HEAD_DIM], window_ref[:, HEAD_DIM:]
    d_keys = d_values = 0.0
    for h in range(GROUP):
        lanes = slice(h * HEAD_DIM, (h + 1) * HEAD_DIM)
        queries, d_heads = q_ref[0, :, lanes], d_ref[0, :, lanes]
        weights = jnp.exp(dot_nt(keys, queries) * SCORE_SCALE + bias_ref[...] - total_ref[0, h : h + 1, :])
        d_weights = dot_nt(values, d_heads)
        through = jnp.sum(weights * d_weights, axis=0, keepdims=True)
        d_scores = (weights * (d_weights - through)).astype(jnp.bfloat16)
        d_values = d_values + dot_nn(weights.astype(jnp.bfloat16), d_heads)
        d_keys = d_keys + dot_nn(d_scores, queries)
        dq_ref[0, :, lanes] = (dot_tn(d_scores, keys) * SCORE_SCALE).astype(dq_ref.dtype)
    d_window_ref[:, :HEAD_DIM] = (d_keys * SCORE_SCALE).astype(d_window_ref.dtype)
    d_window_ref[:, HEAD_DIM:] = d_values.astype(d_window_ref.dtype)


def attend_call(kernel, operands, kinds, outs, out_kinds, rows, span, products):
    groups = pl.BlockSpec((1, rows, GROUP * HEAD_DIM), lambda i: (i, 0, 0))
    window = pl.BlockSpec((span, 2 * HEAD_DIM), lambda i: (0, i))
    specs = {"q": groups, "w": window}
    for a in (*operands, *outs):
        specs[a.shape] = pl.BlockSpec(a.shape, lambda i: (0, 0)) if len(a.shape) == 2 else pl.BlockSpec((1, *a.shape[1:]), lambda i: (i, 0, 0))
    return pl.pallas_call(
        kernel,
        grid=(KV_HEADS,),
        in_specs=[specs[k if k in specs else a.shape] for k, a in zip(kinds, operands)],
        out_specs=[specs[k if k in specs else a.shape] for k, a in zip(out_kinds, outs)],
        out_shape=outs,
        compiler_params=pltpu.CompilerParams(
            dimension_semantics=("arbitrary",), vmem_limit_bytes=24 * 2**20
        ),
        cost_estimate=pl.CostEstimate(
            flops=2 * products * HEADS * rows * span * HEAD_DIM, bytes_accessed=4 * rows * span, transcendentals=HEADS * rows * span
        ),
    )(*operands)


def by_groups(a):
    return a.reshape(a.shape[0], KV_HEADS, GROUP * HEAD_DIM).transpose(1, 0, 2)


def from_groups(a):
    return a.transpose(1, 0, 2).reshape(a.shape[1], HEADS * HEAD_DIM)


def attend(queries, window, bias):
    rows, span = queries.shape[1], window.shape[0]
    outs = [
        jax.ShapeDtypeStruct(queries.shape, jnp.bfloat16),
        jax.ShapeDtypeStruct((KV_HEADS, rows, 8), jnp.float32),
    ]
    return attend_call(attend_kernel, (queries, window, bias), "qwb", outs, "qt", rows, span, 2)


def attend_back(queries, window, bias_t, totals, d_heads):
    rows, span = queries.shape[1], window.shape[0]
    outs = [
        jax.ShapeDtypeStruct(queries.shape, jnp.bfloat16),
        jax.ShapeDtypeStruct(window.shape, jnp.bfloat16),
    ]
    operands = (queries, window, bias_t, totals.transpose(0, 2, 1), d_heads)
    return attend_call(attend_back_kernel, operands, "qwbtq", outs, "qw", rows, span, 5)


def shards(
    inputs,
    segment_ids,
    out_grad,
    norm_gain,
    w_query,
    w_key,
    w_value,
    w_attn_out,
    w_mamba_in,
    conv_weight,
    conv_bias,
    w_select,
    w_step,
    step_bias,
    log_decay,
    skip_gain,
    w_mamba_out,
    attn_gain,
    mamba_gain,
    ffn_norm_gain,
    w_gate,
    w_up,
    w_down,
):
    rows_dev, width = inputs.shape[1:]
    inner = conv_weight.shape[1]
    edge_count = conv_weight.shape[0] - 1
    rank_width = RANK
    state_width = log_decay.shape[0]
    reach_blocks = WINDOW // rows_dev
    group_size = HEADS // KV_HEADS
    score_scale = 1.0 / math.sqrt(HEAD_DIM)
    position = lax.axis_index(HEAD_BLK)
    core = lax.axis_index("head")
    first_core = core == 0
    tokens = inputs[0].astype(jnp.float32)

    d_rows = w_query.shape[0]
    c_rows = w_select.shape[0]
    sel_half, step_half = w_select.shape[1], w_step.shape[1]
    mamba_in = w_mamba_in
    cut_a, cut_b = 1408, 2816
    mixed_c = inner - cut_b
    planes = gather_planes(
        (
            mamba_in[:, :cut_a],
            mamba_in[:, cut_a:cut_b],
            jnp.concatenate([mamba_in[:, cut_b:], w_query, w_key, w_value], axis=1),
        ),
        ORDERS,
    )
    parts = [ring_pieces(a, order[1]) for a, order in zip(planes, ORDERS)]
    half_width = width // 2
    windows_in = [(0, a[0].shape[1]) for a in parts]
    windows_out_a, window_out_b = ((0, half_width), (half_width, 2 * half_width)), (0, half_width)
    select_step = jnp.pad(
        jnp.concatenate([w_select, w_step], axis=1), ((0, 0), (0, 128 - sel_half - step_half))
    )
    select_mine = shown(after(select_step, planes[2]), BLK_SEQ).reshape(inner, 128)
    select_got = other_core(select_mine)
    select_full = join_columns(select_mine[:, :sel_half], select_got[:, :sel_half])
    step_full = join_columns(
        select_mine[:, sel_half : sel_half + step_half], select_got[:, sel_half : sel_half + step_half]
    )

    out_shards = (jnp.concatenate([w_mamba_out[:d_rows], w_mamba_out[d_rows:]], axis=1), w_attn_out)
    out_planes = [
        gathered(after(out_shards[0], planes[0]), ORDER_A[0]),
        *gather_planes(out_shards[1:], ORDERS[1:2], (select_mine,)),
    ]

    ff_rows = w_down.shape[0]

    def to_units(w):
        split = w.reshape(d_rows, 4, 4, 2, ff_rows).transpose(2, 0, 1, 3, 4)
        return jnp.pad(split, ((0, 0),) * 4 + ((0, FF_PAD - ff_rows),)).reshape(4, d_rows, 8 * FF_PAD)

    def from_units(g):
        split = g.reshape(4, d_rows, 4, 2, FF_PAD)[..., :ff_rows]
        return split.transpose(1, 2, 0, 3, 4).reshape(d_rows, 32 * ff_rows)

    units = 8 * FF_PAD
    gate_up = jnp.concatenate([to_units(w_gate), to_units(w_up)], axis=2)
    gate_up_dealt = dealt(after(gate_up, out_planes[1]), Z_RING).reshape(4 * d_rows, 2 * units)
    gate_up = gathered(jnp.pad(gate_up_dealt, ((0, LANES // 16 - 4 * d_rows), (0, 0))), ("xh", "y", "xl"))

    here = lax.axis_index("xh") == core
    down = jnp.pad(w_down, ((0, FF_PAD - ff_rows), (0, 0)))
    down = join_columns(down, other_core(down))
    down = jnp.where(here, down, received(down, "xh", 1))
    down_shard = down
    down = gathered(down, ("y", "xl"))

    def group_tokens(a):
        return both_tokens(ring_whole(a, Z_RING))

    def group_sum(both):
        return ring_sum_whole(to_low(sum_cores(both)), Z_RING)

    grad_out = out_grad[0]

    pick_a, pick_b, pick_c = (picker(order, d_rows) for order in ORDERS)
    pick_ff = ff_picker(d_rows)
    pick_out = [picker(ORDER_A, d_rows, c_rows, k * d_rows) for k in (0, 1)]

    normed, norm_back = jax.vjp(rms_scale, tokens, norm_gain)
    normed_chip = both_tokens(to_low(normed))
    normed_a, normed_b, normed_c = turned((normed_chip,) * 3, (pick_a, pick_b, pick_c))
    normed_c = after(normed_c, gate_up_dealt, down_shard)

    q_cols, k_cols = w_query.shape[1], w_key.shape[1]
    projected = [
        by_pieces((left,), pieces, (window,))
        for left, pieces, window in zip((normed_a, normed_b, normed_c), parts, windows_in)
    ]
    mixed_mine = jnp.concatenate([a[:rows_dev] for a in projected], axis=1)
    mixed_got = other_core(jnp.concatenate([a[rows_dev:] for a in projected], axis=1))
    conv_in = jnp.where(first_core, mixed_mine[:, :inner], mixed_got[:, :inner])
    gate_z = jnp.where(first_core, mixed_got[:, :inner], mixed_mine[:, :inner]).astype(jnp.float32)
    qkv_cols = q_cols + 2 * k_cols
    qkv_mine, qkv_got = (a[:, inner : inner + qkv_cols] for a in (mixed_mine, mixed_got))
    queries = join_columns(qkv_mine[:, :q_cols], qkv_got[:, :q_cols])
    keys_low = join_columns(qkv_mine[:, q_cols : q_cols + k_cols], qkv_got[:, q_cols : q_cols + k_cols])
    values_low = join_columns(qkv_mine[:, q_cols + k_cols :], qkv_got[:, q_cols + k_cols :])
    key_value = jnp.stack([a.reshape(rows_dev, KV_HEADS, HEAD_DIM) for a in (keys_low, values_low)], axis=2)
    key_value = key_value.reshape(rows_dev, 2 * KV_HEADS * HEAD_DIM)

    mamba_out_a, attn_out_b = (
        ring_pieces(after(a, conv_in), order[1]) for a, order in zip(out_planes, ORDERS)
    )
    grad_out_group = group_tokens(jnp.pad(after(grad_out, conv_in), ((0, 0), (0, LANES - width))))

    along_z = lax.axis_index(Z_RING)
    kv_cols = KV_HEADS * HEAD_DIM
    row = ring_in_order(key_value, Z_RING).reshape(4, rows_dev, 2 * kv_cols)
    edge_rows = after(shifted(conv_in[rows_dev - edge_count :], 1), row)
    window = jnp.concatenate([shifted(row, 2, ROWS), shifted(row, 1, ROWS), row])
    window = lax.dynamic_slice_in_dim(window, along_z, reach_blocks + 1).reshape(-1, key_value.shape[1])

    padded_in = jnp.concatenate([edge_rows, conv_in], axis=0).astype(jnp.float32)
    conved, conv_back = jax.vjp(conv_silu, padded_in, conv_weight, conv_bias)
    conved_low = to_low(conved)
    conv_values = conved_low.astype(jnp.float32)
    selected = product(conved_low, select_full)
    step_raw = to_low(selected[:, :rank_width])
    in_mat = selected[:, rank_width : rank_width + state_width]
    out_mat = selected[:, rank_width + state_width :]
    step_pre = product_nt(step_raw, step_full)
    (step_size, decay_rate), rate_back = jax.vjp(rate_piece, step_pre, step_bias, log_decay)
    total_step = jnp.sum(step_size, axis=0)
    drive = step_size * conv_values
    in_lanes, out_lanes = lanes(in_mat), lanes(out_mat)
    end_state = scan_state(step_size, drive, in_lanes, decay_rate)
    queries = after(queries, end_state)
    state_in = chain_carry(total_step, end_state, decay_rate, False)
    scan_out = scan_full(step_size, drive, in_lanes, out_lanes, decay_rate, state_in)
    gated, gate_back = jax.vjp(gate_piece, scan_out, conv_values, gate_z, skip_gain)
    gated_low = after(to_low(gated), grad_out_group)

    span_keys = (reach_blocks + 1) * rows_dev
    segment_row = segment_ids[0]
    padded_segs = jnp.concatenate(
        [jnp.full((reach_blocks * rows_dev,), -1, jnp.int32), segment_row]
    )
    key_segs = lax.dynamic_slice_in_dim(padded_segs, position * rows_dev, span_keys)
    query_segs = lax.dynamic_slice_in_dim(segment_row, position * rows_dev, rows_dev)
    gaps = (reach_blocks * rows_dev + jnp.arange(rows_dev, dtype=jnp.int32))[:, None] - jnp.arange(
        span_keys, dtype=jnp.int32
    )[None, :]
    allowed = (gaps >= 0) & (gaps < WINDOW) & (query_segs[:, None] == key_segs[None, :])
    queries_by_group = by_groups(queries)
    heads_by_group, score_totals = attend(queries_by_group, window, jnp.where(allowed, 0.0, -1e30))
    heads_low = from_groups(heads_by_group)

    heads_b, *gated_a = (
        both_tokens(a) for a in turned((heads_low, gated_low, gated_low), (pick_b, *pick_out))
    )
    branch_out = jnp.concatenate(
        [
            by_pieces((heads_b,), attn_out_b, (window_out_b,), False),
            by_pieces(gated_a, mamba_out_a, windows_out_a, False),
        ],
        axis=1,
    )
    out_mine, out_got = branch_out[:rows_dev], other_core(branch_out[rows_dev:])
    attn_out = join_columns(out_mine[:, :half_width], out_got[:, :half_width])
    mamba_out = join_columns(out_mine[:, half_width:], out_got[:, half_width:])
    hidden_mid, merge_back = jax.vjp(
        merge_piece, tokens, attn_out, mamba_out, attn_gain, mamba_gain
    )
    normed_two, norm_two_back = jax.vjp(rms_scale, hidden_mid, ffn_norm_gain)
    normed_two_ff = group_tokens(turned((to_low(normed_two),), (pick_ff,))[0])
    act_low, d_gate_up, down_part, d_part = feed_forward(normed_two_ff, grad_out_group, gate_up, down)
    d_cores = to_low(sum_cores(d_part))
    d_normed_two = ring_sum_whole(d_cores, Z_RING)
    act_low, d_gate_up = together((act_low, d_gate_up, d_cores))[:2]
    grad_gate_up, grad_down = feed_grads(normed_two_ff, d_gate_up, act_low, grad_out_group)

    gate_up_sum = scattered(grad_gate_up, ("xh", "y", "xl"))[: 4 * d_rows].reshape(4, d_rows, 2 * units)
    gate_up_sum = dealt(gate_up_sum, Z_RING).astype(jnp.float32)
    grad_gate, grad_up = from_units(gate_up_sum[..., :units]), from_units(gate_up_sum[..., units:])
    grad_down = scattered(grad_down, ("y", "xl")).astype(jnp.float32)
    grad_down = grad_down + received(to_low(grad_down), "xh", 1).astype(jnp.float32)
    down_l, down_r = grad_down[:ff_rows, :half_width], grad_down[:ff_rows, half_width:]
    down_got = other_core(to_low(jnp.where(first_core, down_r, down_l))).astype(jnp.float32)
    grad_down = jnp.where(here, jnp.where(first_core, down_l, down_r), down_got)

    d_mid_norm, grad_ffn_norm = norm_two_back(turned_back((d_normed_two,), (pick_ff,), False)[0])
    d_mid = grad_out.astype(jnp.float32) + d_mid_norm
    d_tokens_res, d_attn_out, d_mamba_out, grad_attn_gain, grad_mamba_gain = merge_back(d_mid)
    d_attn_low, d_mamba_low = to_low(d_attn_out), to_low(d_mamba_out)
    d_branch = jnp.concatenate(
        [d_attn_low[:, :half_width], d_mamba_low[:, :half_width], d_attn_low[:, half_width:], d_mamba_low[:, half_width:]],
        axis=1,
    )
    d_branch_half = own_columns(d_branch)
    d_attn_half, d_mamba_half = d_branch_half[:, :half_width], d_branch_half[:, half_width:]
    d_gated_a = by_pieces_nt((d_mamba_half, d_mamba_half), mamba_out_a, windows_out_a)
    d_heads_b = by_pieces_nt((d_attn_half,), attn_out_b, (window_out_b,))
    d_branch = to_low(sum_cores(jnp.concatenate([*d_gated_a, *d_heads_b], axis=1)))
    d_gated_a, d_heads_b = [d_branch[:, k * LANES : (k + 1) * LANES] for k in (0, 1)], d_branch[:, 2 * LANES :]
    d_gated = turned_back(d_gated_a, pick_out, False, True, inner)[0]
    d_heads = turned_back((d_heads_b,), (pick_b,), True)[0]

    d_scan, d_conv_gate, d_gate_z, grad_skip = gate_back(d_gated)
    d_state_in = adjoint_state(step_size, d_scan, out_lanes, decay_rate)
    d_heads, d_attn_half, d_mamba_half, down_part = together(
        (d_heads, d_attn_half, d_mamba_half, down_part, d_state_in)
    )[:4]
    output = to_low(hidden_mid + group_sum(down_part)[:, :width])[None]

    d_queries, d_window = attend_back(
        queries_by_group, window, jnp.where(allowed.T, 0.0, -1e30), score_totals, by_groups(d_heads)
    )
    d_queries = from_groups(d_queries)
    d_rows_z = jnp.zeros((12, rows_dev, d_window.shape[1]), jnp.bfloat16)
    d_rows_z = lax.dynamic_update_slice_in_dim(
        d_rows_z, d_window.reshape(reach_blocks + 1, rows_dev, -1), along_z, 0
    )
    d_row = (
        d_rows_z[8:].astype(jnp.float32)
        + shifted(d_rows_z[4:8], -1, ROWS).astype(jnp.float32)
        + shifted(d_rows_z[:4], -2, ROWS).astype(jnp.float32)
    )
    d_key_value = ring_sum_in_order(to_low(d_row).reshape(4 * rows_dev, 2 * kv_cols), Z_RING)
    d_key_value = to_low(d_key_value).reshape(rows_dev, KV_HEADS, 2, HEAD_DIM)
    d_keys, d_values = (d_key_value[:, :, k].reshape(rows_dev, kv_cols) for k in (0, 1))

    kv_half = kv_cols // 2
    d_qkv_half = own_columns(
        jnp.concatenate(
            [
                d_queries[:, :q_cols],
                d_keys[:, :kv_half],
                d_values[:, :kv_half],
                d_queries[:, q_cols:],
                d_keys[:, kv_half:],
                d_values[:, kv_half:],
            ],
            axis=1,
        )
    )
    rings = sum_rings(
        (grad_pieces(gated_a, d_mamba_half, HALVES), grad_pieces((heads_b,), d_attn_half, HALVES)), ORDERS[:2]
    )

    d_end = chain_carry(total_step, d_state_in, decay_rate, True)
    d_step, d_conv_scan, d_rate, d_in_mat, d_out_mat = scan_back(
        step_size, conv_values, d_scan, in_lanes, out_lanes, decay_rate, state_in, d_end
    )
    d_step_pre, grad_step_bias, grad_log_decay = rate_back((d_step, d_rate))
    d_step_low = to_low(d_step_pre)
    grad_step_w = product_tn(d_step_low, step_raw)
    d_step_raw = product(d_step_low, step_full)
    d_selected = to_low(jnp.concatenate([d_step_raw, d_in_mat, d_out_mat], axis=1))
    grad_select = product_tn(conved_low, d_selected)
    d_conved = product_nt(d_selected, select_full) + d_conv_gate + d_conv_scan
    d_padded, grad_conv_w, grad_conv_b = conv_back(d_conved)
    edge_back = shifted(to_low(d_padded[:edge_count]), -1).astype(jnp.float32)
    d_conv_in = d_padded[edge_count:] + jnp.concatenate(
        [jnp.zeros((rows_dev - edge_count, inner), jnp.float32), edge_back], axis=0
    )
    d_mixed_half = own_columns(to_low(jnp.concatenate([d_conv_in, d_gate_z], axis=1)))
    d_mixed_a, d_mixed_b, d_mixed_c = (
        d_mixed_half[:, :cut_a],
        d_mixed_half[:, cut_a:cut_b],
        jnp.concatenate([d_mixed_half[:, cut_b:], d_qkv_half], axis=1),
    )

    pieces = [
        grad_pieces((left,), grad, HALVES)
        for left, grad in ((normed_a, d_mixed_a), (normed_b, d_mixed_b), (normed_c, d_mixed_c))
    ]
    d_mixed_a, d_mixed_b, d_mixed_c = together((d_mixed_a, d_mixed_b, d_mixed_c, *(p[0] for p in pieces)))[:3]
    ring_a, ring_b, ring_c = sum_rings(pieces, ORDERS)
    d_normed = turned_back(
        [
            by_pieces_nt((grad,), pieces, (window,))[0]
            for grad, pieces, window in zip((d_mixed_a, d_mixed_b, d_mixed_c), parts, windows_in)
        ],
        (pick_a, pick_b, pick_c),
        False,
        True,
    )[0]
    d_tokens_norm, grad_norm = norm_back(sum_cores(d_normed))
    input_grad = to_low(d_tokens_res + d_tokens_norm)[None]

    smalls = (
        grad_norm,
        grad_conv_w,
        grad_conv_b,
        grad_step_bias,
        grad_log_decay,
        grad_skip,
        grad_attn_gain,
        grad_mamba_gain,
        grad_ffn_norm,
    )
    channel_rows = [a.reshape(-1, inner) for a in smalls[1:6]]
    gains = jnp.concatenate([smalls[0], *smalls[6:]]).reshape(-1, inner)
    select_rows = jnp.stack(
        [
            jnp.pad(jnp.concatenate([sel, stp], axis=1), ((0, 0), (0, 128 - sel_half - step_half)))
            for sel, stp in zip(jnp.split(grad_select, 2, axis=1), jnp.split(grad_step_w, 2, axis=1))
        ]
    )
    select_rows = select_rows.reshape(128, c_rows, 128)
    select_rows = after(select_rows, gate_up_sum, grad_down)
    totals, select_sum = sum_all(jnp.concatenate([gains, *channel_rows]), select_rows)
    grad_select, grad_step = select_sum[:, :sel_half], select_sum[:, sel_half : sel_half + step_half]
    gain_sums = totals[: gains.shape[0]].reshape(4, width)
    at, channel_sums = gains.shape[0], []
    for a in channel_rows:
        channel_sums.append(totals[at : at + a.shape[0]])
        at += a.shape[0]
    totals = [
        gain_sums[0],
        channel_sums[0],
        *(channel_sums[k][0] for k in (1, 2)),
        channel_sums[3],
        channel_sums[4][0],
        *gain_sums[1:],
    ]
    ring_a, ring_b, ring_c = together((ring_a, ring_b, ring_c, select_sum))[:3]
    sum_a, sum_b, sum_c = sum_planes(
        [jnp.concatenate([ring_a, rings[0]], axis=1), jnp.concatenate([ring_b, rings[1]], axis=1), ring_c], ORDERS
    )
    sum_a, out_sum_a = sum_a[:, :cut_a], sum_a[:, cut_a:]
    sum_b, grad_attn_out = sum_b[:, : cut_b - cut_a], sum_b[:, cut_b - cut_a :]
    grad_mamba_out = jnp.concatenate([out_sum_a[:, :half_width], out_sum_a[:, half_width:]], axis=0)
    grad_mamba_in = jnp.concatenate([sum_a, sum_b, sum_c[:, :mixed_c]], axis=1)
    grad_qkv = sum_c[:, mixed_c:]
    grad_query = grad_qkv[:, :q_cols]
    grad_key, grad_value = grad_qkv[:, q_cols : q_cols + k_cols], grad_qkv[:, q_cols + k_cols :]


    return (
        output,
        input_grad,
        totals[0],
        grad_query,
        grad_key,
        grad_value,
        grad_attn_out,
        grad_mamba_in,
        totals[1],
        totals[2],
        grad_select,
        grad_step,
        totals[3],
        totals[4],
        totals[5],
        grad_mamba_out,
        totals[6],
        totals[7],
        totals[8],
        grad_gate,
        grad_up,
        grad_down,
    )


def solution(mesh):
    torus = Mesh(
        mesh.devices.reshape(mesh.shape["head"], 2, 4, 4, mesh.shape["seq"]),
        ("head", "xh", "y", "z", "xl"),
    )
    weight = P(BLK_SEQ, "head")
    rows = P("xl", HEAD_BLK, None)
    in_specs = (rows, P("xl", None), rows, P()) + (weight,) * 5
    in_specs += (P(), P(), weight, weight, P(), P(), P(), weight, P(), P(), P()) + (weight,) * 3
    out_specs = (rows, rows, P()) + (weight,) * 5
    out_specs += (P(), P(), weight, weight, P(), P(), P(), weight, P(), P(), P()) + (weight,) * 3
    return jax.shard_map(
        shards, mesh=torus, in_specs=in_specs, out_specs=out_specs, check_vma=False
    )
```

```python
import functools
import math

import jax
import jax.numpy as jnp
import numpy as np
from jax import lax
from jax.experimental import pallas as pl
from jax.experimental.pallas import tpu as pltpu
from jax.sharding import Mesh
from jax.sharding import PartitionSpec as P

HEADS = 25
KV_HEADS = 5
HEAD_DIM = 64
WINDOW = 1024
RANK = 100
X_RING = ("xh", "xl")
ROWS = ("head", "xh", "y")
EVERY = ("head", "xh", "y", "z", "xl")
Y_RING = "y"
Z_RING = "z"
BLK_SEQ = ("xh", "y", "z", "xl")
HEAD_BLK = ("head", "xh", "y", "z")
EPSILON = 1e-06
LOG2_E = 1.0 / math.log(2.0)
FF_PAD = 88
WIDTH = HEADS * HEAD_DIM
LANES = -(-WIDTH // 128) * 128


def received(a, axis, d):
    n = lax.axis_size(axis)
    return lax.ppermute(a, axis, [((i + d) % n, i) for i in range(n)])


def other_core(a):
    return received(a, "head", 1)


def shifted(a, distance, axis=HEAD_BLK):
    n = lax.axis_size(axis)
    return lax.ppermute(a, axis, [(i - distance, i) for i in range(n) if 0 <= i - distance < n])


def after(value, *others):
    return lax.optimization_barrier((value, *others))[0]


def dealt(blocks, axis):
    return lax.all_to_all(blocks, axis, 0, 0, tiled=True)


def shown(a, axis):
    return dealt(jnp.broadcast_to(a[None], (lax.axis_size(axis), *a.shape)), axis)


def summed(blocks, axis):
    return jnp.sum(dealt(blocks, axis).astype(jnp.float32), axis=0)


ORDER_A = (("y", "z"), X_RING)
ORDER_B = (("xh", "z", "xl"), Y_RING)
ORDER_C = (("xh", "y", "xl"), Z_RING)
ORDERS = (ORDER_A, ORDER_B, ORDER_C)


def together(values):
    return lax.optimization_barrier(tuple(values))


def ring_pieces(a, axis):
    half = a.shape[0] // 2
    up, down = received(a, axis, 1), received(a, axis, -1)
    return [a, up, received(up[:half], axis, 1), received(down[half:], axis, -1), down]


def ring_whole(a, axis):
    return jnp.concatenate([a] + [received(a, axis, j) for j in (1, 2, 3)], axis=0)


def ring_in_order(a, axis):
    me = lax.axis_index(axis)
    out = jnp.zeros((4, *a.shape), a.dtype)
    for j, part in enumerate([a] + [received(a, axis, j) for j in (1, 2, 3)]):
        out = lax.dynamic_update_index_in_dim(out, part, lax.rem(me + j, 4), 0)
    return out.reshape(4 * a.shape[0], a.shape[1])


def gather_planes(shards, orders, last=()):
    planes = []
    for a, order in zip(shards, orders):
        planes.append(shown(after(a, *last), order[0]).reshape(16 * a.shape[0], a.shape[1]))
        last = planes[-1:]
    return planes


def ring_sum(pieces, axis):
    own, up, far_low, far_high, down = pieces
    half = far_low.shape[0]
    low = own.dtype
    from_down, from_up = received(far_low, axis, -1), received(far_high, axis, 1)
    to_up = jnp.concatenate(
        [(up[:half].astype(jnp.float32) + from_down.astype(jnp.float32)).astype(low), up[half:]]
    )
    to_down = jnp.concatenate(
        [down[:half], (down[half:].astype(jnp.float32) + from_up.astype(jnp.float32)).astype(low)]
    )
    return (
        own.astype(jnp.float32)
        + received(to_up, axis, -1).astype(jnp.float32)
        + received(to_down, axis, 1).astype(jnp.float32)
    )


def ring_sum_whole(whole, axis):
    rows = whole.shape[0] // 4
    total = whole[:rows].astype(jnp.float32)
    for j in (1, 2, 3):
        total = total + received(whole[j * rows : (j + 1) * rows], axis, -j).astype(jnp.float32)
    return total


def sum_rings(grads, orders):
    return [to_low(ring_sum(a, order[1])) for a, order in zip(grads, orders)]


def sum_planes(rings, orders):
    return [summed(a.reshape(16, a.shape[0] // 16, a.shape[1]), order[0]) for a, order in zip(rings, orders)]


def ring_sum_in_order(whole, axis):
    rows = whole.shape[0] // 4
    blocks = whole.reshape(4, rows, whole.shape[1])
    me = lax.axis_index(axis)
    total = 0.0
    for j in range(4):
        block = lax.dynamic_index_in_dim(blocks, lax.rem(me + j, 4), 0, keepdims=False)
        total = total + (received(block, axis, -j) if j else block).astype(jnp.float32)
    return total


def padded_index(index):
    return jnp.pad(index, (0, LANES - WIDTH), constant_values=-1)


def picker(order, rows, stride=None, offset=0):
    stride = stride or rows
    ring, inside = np.indices((4, 16 * rows))
    turned = lax.rem(lax.axis_index(order[1]) + jnp.asarray(ring, jnp.int32), 4)
    block, row = inside // rows, jnp.asarray(inside % rows, jnp.int32)
    if order is ORDER_A:
        xh, y, z, xl = turned // 2, block // 4, block % 4, turned % 2
    elif order is ORDER_B:
        xh, y, z, xl = block // 8, turned, block // 2 % 4, block % 2
    else:
        xh, y, z, xl = block // 8, block // 2 % 4, turned, block % 2
    return padded_index(((((xh * 4 + y) * 4 + z) * 2 + xl) * stride + offset + row).reshape(-1))


def ff_picker(rows):
    xh, y, xl, z, row = np.indices((2, 4, 2, 4, rows))
    index = (((((xh * 4 + y) * 4 + z) * 2 + xl) * rows + row)).reshape(16, 4 * rows)
    return jnp.asarray(np.pad(index, ((0, 0), (0, LANES // 16 - 4 * rows)), constant_values=-1).reshape(-1), jnp.int32)


def gathered(a, axes):
    return lax.all_gather(a, axes).reshape(-1, a.shape[1])


def scattered(a, axes):
    blocks = a.reshape(lax.axis_size(axes), -1, a.shape[1])
    return lax.optimization_barrier(lax.psum_scatter(blocks, axes, scatter_dimension=0))


HALVES = (WIDTH // 4, WIDTH // 4, WIDTH // 8, WIDTH // 8, WIDTH // 4)


def bounds(sizes):
    stops = np.cumsum(sizes)
    return [(int(stop - size), int(stop)) for size, stop in zip(sizes, stops)]


def rows_of(pieces):
    return bounds([a.shape[0] for a in pieces])


def dot_nn(a, b):
    return jnp.dot(a, b, preferred_element_type=jnp.float32)


def dot_nt(a, b):
    return lax.dot_general(a, b, (((1,), (1,)), ((), ())), preferred_element_type=jnp.float32)


def dot_tn(a, b):
    return lax.dot_general(a, b, (((0,), (0,)), ((), ())), preferred_element_type=jnp.float32)


def whole_call(kernel, operands, outs, flops):
    sizes = sum(a.size * a.dtype.itemsize for a in (*operands, *outs))
    return pl.pallas_call(
        kernel,
        out_shape=outs,
        in_specs=[pl.BlockSpec(memory_space=pltpu.VMEM)] * len(operands),
        out_specs=[pl.BlockSpec(memory_space=pltpu.VMEM)] * len(outs),
        compiler_params=pltpu.CompilerParams(vmem_limit_bytes=40 * 2**20),
        cost_estimate=pl.CostEstimate(flops=flops, bytes_accessed=sizes, transcendentals=0),
    )(*operands)


def out_array(rows, cols, low=True):
    return jax.ShapeDtypeStruct((rows, cols), jnp.bfloat16 if low else jnp.float32)


def clear_rest(ref, start):
    if start < ref.shape[1]:
        ref[:, start:] = jnp.zeros((ref.shape[0], ref.shape[1] - start), ref.dtype)


def nn_kernel(windows, *refs):
    count = len(windows)
    lefts, pieces, y_ref = refs[:count], refs[count:-1], refs[-1]
    width = windows[0][1] - windows[0][0]
    for at in range(0, width, 512):
        stop = min(at + 512, width)
        total = 0.0
        for left, (low, _) in zip(lefts, windows):
            for (start, end), piece in zip(rows_of(pieces), pieces):
                total = total + dot_nn(left[:, start:end], piece[:, low + at : low + stop])
        y_ref[:, at:stop] = total.astype(y_ref.dtype)
    clear_rest(y_ref, width)


def by_pieces(lefts, pieces, windows, low=True):
    rows, width = lefts[0].shape[0], windows[0][1] - windows[0][0]
    flops = 2 * rows * width * sum(a.shape[1] for a in lefts)
    return whole_call(
        functools.partial(nn_kernel, windows), (*lefts, *pieces), [out_array(rows, -(-width // 128) * 128 if low else width, low)], flops
    )[0]


def nt_kernel(windows, *refs):
    count = len(windows)
    grads, pieces, outs = refs[:count], refs[count:-count], refs[-count:]
    for grad, (low, high), out in zip(grads, windows, outs):
        for (start, end), piece in zip(rows_of(pieces), pieces):
            out[:, start:end] = dot_nt(grad[:, : high - low], piece[:, low:high]).astype(out.dtype)
        clear_rest(out, rows_of(pieces)[-1][1])


def by_pieces_nt(grads, pieces, windows):
    rows, depth = grads[0].shape[0], sum(a.shape[0] for a in pieces)
    flops = 2 * rows * depth * sum(a.shape[1] for a in grads)
    return whole_call(
        functools.partial(nt_kernel, windows), (*grads, *pieces), [out_array(rows, -(-depth // 128) * 128)] * len(grads), flops
    )


def tn_kernel(sizes, right, *refs):
    lefts, outs = refs[: -len(sizes)], refs[-len(sizes) :]
    width = right.shape[1]
    for k, left in enumerate(lefts):
        for (start, end), out in zip(bounds(sizes), outs):
            out[:, k * width : (k + 1) * width] = dot_tn(left[:, start:end], right[...]).astype(out.dtype)


def grad_pieces(lefts, right, sizes):
    outs = [out_array(size, right.shape[1] * len(lefts)) for size in sizes]
    flops = 2 * right.size * sum(sizes) * len(lefts)
    return whole_call(functools.partial(tn_kernel, sizes), (right, *lefts), outs, flops)


def feed_kernel(x_ref, g_ref, up_ref, down_ref, act_ref, d_ref, y_ref, dx_ref):
    units = down_ref.shape[0]
    both = dot_nn(x_ref[...], up_ref[...])
    gate, up = both[:, :units], both[:, units:]
    sig = 1.0 / (1.0 + jnp.exp(-gate))
    silu = gate * sig
    act = (silu * up).astype(jnp.bfloat16)
    act_ref[...] = act
    y_ref[:, :WIDTH] = dot_nn(act, down_ref[...]).astype(y_ref.dtype)
    clear_rest(y_ref, WIDTH)
    d_act = dot_nt(g_ref[:, :WIDTH], down_ref[...])
    d_ref[:, :units] = (d_act * up * (sig * (1.0 + gate * (1.0 - sig)))).astype(d_ref.dtype)
    d_ref[:, units:] = (d_act * silu).astype(d_ref.dtype)
    dx_ref[...] = dot_nt(d_ref[...], up_ref[...]).astype(dx_ref.dtype)


def feed_forward(x, g, gate_up, down):
    tokens, width = x.shape
    units = down.shape[0]
    block = 256

    def rows(cols):
        return pl.BlockSpec((block, cols), lambda i: (i, 0))

    def fixed(a):
        return pl.BlockSpec(a.shape, lambda i: (0, 0))

    return pl.pallas_call(
        feed_kernel,
        grid=(tokens // block,),
        in_specs=[rows(width), rows(width), fixed(gate_up), fixed(down)],
        out_specs=[rows(units), rows(2 * units), rows(width), rows(width)],
        out_shape=[out_array(tokens, c) for c in (units, 2 * units, width, width)],
        compiler_params=pltpu.CompilerParams(
            dimension_semantics=("arbitrary",), vmem_limit_bytes=48 * 2**20
        ),
        cost_estimate=pl.CostEstimate(
            flops=2 * tokens * width * units * 6, bytes_accessed=2 * tokens * (4 * width + 3 * units), transcendentals=tokens * units
        ),
    )(x, g, gate_up, down)


def feed_grads_kernel(x_ref, d_ref, act_ref, g_ref, up_ref, down_ref):
    up_ref[...] = dot_tn(x_ref[...], d_ref[...]).astype(up_ref.dtype)
    down_ref[...] = dot_tn(act_ref[...], g_ref[:, :WIDTH]).astype(down_ref.dtype)


def feed_grads(x, d, act, g):
    outs = [out_array(x.shape[1], d.shape[1]), out_array(act.shape[1], WIDTH)]
    flops = 2 * x.shape[0] * x.shape[1] * (d.shape[1] + act.shape[1])
    return whole_call(feed_grads_kernel, (x, d, act, g), outs, flops)


def one_hot(index_ref, start, stop):
    width = index_ref.shape[1]
    rows = lax.broadcasted_iota(jnp.int32, (stop - start, width), 0) + start
    return jnp.where(rows == index_ref[...], 1.0, 0.0).astype(jnp.bfloat16)


def turn_kernel(count, *refs):
    lefts, indices, outs = refs[:count], refs[count : 2 * count], refs[2 * count :]
    for left, index, out in zip(lefts, indices, outs):
        total = 0.0
        for start in range(0, left.shape[1], 400):
            total = total + dot_nn(left[:, start : start + 400], one_hot(index, start, start + 400))
        out[...] = total.astype(out.dtype)


def turned(lefts, indices):
    outs = [out_array(a.shape[0], index.shape[0]) for a, index in zip(lefts, indices)]
    rows = [index.reshape(1, -1) for index in indices]
    flops = sum(2 * a.size * a.shape[1] for a in lefts)
    return whole_call(functools.partial(turn_kernel, len(lefts)), (*lefts, *rows), outs, flops)


def turn_back_kernel(count, *refs):
    lefts, indices, outs = refs[:count], refs[count : 2 * count], refs[2 * count :]
    for start in range(0, outs[0].shape[1], 400):
        total = 0.0
        for k, (left, index) in enumerate(zip(lefts, indices)):
            hot = one_hot(index, start, start + 400)
            if left.dtype == jnp.float32:
                high = left[...].astype(jnp.bfloat16)
                rest = (left[...] - high.astype(jnp.float32)).astype(jnp.bfloat16)
                part = dot_nt(high, hot) + dot_nt(rest, hot)
            else:
                part = dot_nt(left[...], hot)
            if len(outs) > 1:
                outs[k][:, start : start + 400] = part.astype(outs[k].dtype)
            total = total + part
        if len(outs) == 1:
            outs[0][:, start : start + 400] = total.astype(outs[0].dtype)


def turned_back(lefts, indices, low, summed=False, width=WIDTH):
    rows = lefts[0].shape[0]
    outs = [out_array(rows, width, low)] * (1 if summed else len(lefts))
    hots = [index.reshape(1, -1) for index in indices]
    flops = sum(2 * a.size * width for a in lefts)
    return whole_call(functools.partial(turn_back_kernel, len(lefts)), (*lefts, *hots), outs, flops)


def join_columns(mine, got):
    first = lax.axis_index("head") == 0
    return jnp.concatenate([jnp.where(first, mine, got), jnp.where(first, got, mine)], axis=1)


def own_tokens(both):
    rows = both.shape[0] // 2
    return join_columns(both[:rows], other_core(both[rows:]))


def own_columns(a):
    first = lax.axis_index("head") == 0
    low, high = jnp.split(a, 2, axis=1)
    mine, theirs = jnp.where(first, low, high), jnp.where(first, high, low)
    return jnp.concatenate([mine, other_core(theirs)], axis=0)


def both_tokens(a):
    return jnp.concatenate([a, other_core(a)], axis=0)


def sum_cores(both):
    rows = both.shape[0] // 2
    return both[:rows].astype(jnp.float32) + other_core(to_low(both[rows:])).astype(jnp.float32)


def chain_kernel(reverse, packed_ref, rate_ref, out_ref):
    rate = rate_ref[...] * LOG2_E
    count, states = packed_ref.shape[0], rate.shape[0]

    def one(k, state):
        p = count - 1 - k if reverse else k
        out_ref[p] = state
        packed = packed_ref[p].astype(jnp.float32)
        total = packed[states : states + 1] + packed[states + 1 : states + 2]
        return jnp.exp2(total * rate) * state + packed[:states]

    lax.fori_loop(0, count, one, jnp.zeros(rate.shape, jnp.float32))


def chain_carry(total_step, state, decay_rate, reverse):
    count = lax.axis_size(HEAD_BLK)
    states, channels = state.shape
    high = lax.reduce_precision(total_step, 8, 7)
    packed = jnp.concatenate([state, high[None], (total_step - high)[None]]).astype(jnp.bfloat16)

    def tiles(a):
        padded = jnp.pad(a, ((0, 0), (0, count * 128 - channels)))
        return padded.reshape(a.shape[0], count, 128).transpose(1, 0, 2)

    rate = lax.dynamic_index_in_dim(tiles(decay_rate), lax.axis_index(HEAD_BLK), 0, keepdims=False)
    chained = pl.pallas_call(
        functools.partial(chain_kernel, reverse),
        out_shape=jax.ShapeDtypeStruct((count, states, 128), jnp.float32),
    )(dealt(tiles(packed), HEAD_BLK), rate)
    got = dealt(to_low(chained), HEAD_BLK)[: channels // 128]
    return got.transpose(1, 0, 2).reshape(states, channels).astype(jnp.float32)


def sum_parts(values, owned):
    count = lax.axis_size(EVERY)
    lines = values.reshape(-1, 128)
    each = -(-lines.shape[0] // count)
    padded = jnp.pad(lines, ((0, count * each - lines.shape[0]), (0, 0))).reshape(count, each, 128)
    mine = summed(jnp.concatenate([to_low(owned), to_low(padded)], axis=1), EVERY)
    return mine[owned.shape[1] :], mine[: owned.shape[1]]


def show_parts(mine, shape, local):
    rows = -(-local.shape[0] // 128)
    lines = jnp.pad(local, (0, rows * 128 - local.shape[0])).reshape(rows, 128)
    got = shown(jnp.concatenate([mine, lines], axis=0), EVERY)
    each = mine.shape[0]
    totals = got[:, :each].reshape(-1, 128)[: shape[0] * shape[1] // 128].reshape(shape)
    return totals, jnp.sum(got[:, each:], axis=0).reshape(-1)[: local.shape[0]]


def rms_scale(values, gain):
    return values * lax.rsqrt(jnp.mean(values * values, axis=-1, keepdims=True) + EPSILON) * gain


def to_low(values):
    return values.astype(jnp.bfloat16)


def product(left, right):
    return jnp.dot(left, right, preferred_element_type=jnp.float32)


def product_tn(left, right):
    return lax.dot_general(
        left, right, (((0,), (0,)), ((), ())), preferred_element_type=jnp.float32
    )


def product_nt(left, right):
    return lax.dot_general(
        left, right, (((1,), (1,)), ((), ())), preferred_element_type=jnp.float32
    )


def chain_combine(earlier, later):
    return (earlier[0] * later[0], later[0] * earlier[1] + later[1])


def conv_silu(padded, conv_weight, conv_bias):
    tap_count = conv_weight.shape[0]
    length = padded.shape[0] - tap_count + 1
    total_sum = conv_bias
    for tap_index in range(tap_count):
        total_sum = total_sum + conv_weight[tap_index] * padded[tap_index : tap_index + length]
    return jax.nn.silu(total_sum)


def rate_piece(step_pre, step_bias, log_decay):
    return (jax.nn.softplus(step_pre + step_bias), -jnp.exp(log_decay))


def gate_piece(scan_out, conv_values, gate_z, skip_gain):
    return (scan_out + skip_gain * conv_values) * jax.nn.silu(gate_z)


def merge_piece(tokens, attn_out, mamba_out, attn_gain, mamba_gain):
    return tokens + 0.5 * (rms_scale(attn_out, attn_gain) + rms_scale(mamba_out, mamba_gain))


def swiglu(gate_val, up_val):
    return jax.nn.silu(gate_val) * up_val


SCAN_TILE = 640


def scan_state_kernel(step_ref, drive_ref, in_ref, rate_ref, end_ref):
    rate = rate_ref[...] * LOG2_E
    width = rate.shape[1]

    def eight(k, state):
        base = pl.multiple_of(k * 8, 8)
        step, drive = step_ref[pl.ds(base, 8), :], drive_ref[pl.ds(base, 8), :]
        for i in range(8):
            decay = jnp.exp2(step[i : i + 1] * rate)
            in_now = jnp.tile(in_ref[base + i], (1, width // 128))
            state = decay * state + in_now * drive[i : i + 1]
        return state

    end_ref[...] = lax.fori_loop(0, step_ref.shape[0] // 8, eight, jnp.zeros(rate.shape, jnp.float32))


def scan_full_kernel(step_ref, drive_ref, in_ref, out_ref, rate_ref, start_ref, y_ref):
    rate = rate_ref[...] * LOG2_E
    width = rate.shape[1]

    def eight(k, state):
        base = pl.multiple_of(k * 8, 8)
        step, drive = step_ref[pl.ds(base, 8), :], drive_ref[pl.ds(base, 8), :]
        rows = []
        for i in range(8):
            decay = jnp.exp2(step[i : i + 1] * rate)
            in_now = jnp.tile(in_ref[base + i], (1, width // 128))
            out_now = jnp.tile(out_ref[base + i], (1, width // 128))
            state = decay * state + in_now * drive[i : i + 1]
            rows.append(jnp.sum(out_now * state, axis=0, keepdims=True))
        y_ref[pl.ds(base, 8), :] = jnp.concatenate(rows, axis=0)
        return state

    lax.fori_loop(0, step_ref.shape[0] // 8, eight, start_ref[...])


def adjoint_state_kernel(step_ref, d_scan_ref, out_ref, rate_ref, d_start_ref):
    rate = rate_ref[...] * LOG2_E
    width = rate.shape[1]
    blocks = step_ref.shape[0] // 8

    def eight(k, carry):
        base = pl.multiple_of((blocks - 1 - k) * 8, 8)
        step, d_scan = step_ref[pl.ds(base, 8), :], d_scan_ref[pl.ds(base, 8), :]
        for i in range(7, -1, -1):
            out_now = jnp.tile(out_ref[base + i], (1, width // 128))
            carry = jnp.exp2(step[i : i + 1] * rate) * (out_now * d_scan[i : i + 1] + carry)
        return carry

    d_start_ref[...] = lax.fori_loop(0, blocks, eight, jnp.zeros(rate.shape, jnp.float32))


def scan_back_kernel(
    step_ref,
    conv_ref,
    d_scan_ref,
    in_ref,
    out_ref,
    rate_ref,
    start_ref,
    d_end_ref,
    d_step_ref,
    d_conv_ref,
    d_rate_ref,
    d_in_ref,
    d_out_ref,
    states_ref,
    decays_ref,
):
    true_rate = rate_ref[...]
    rate = true_rate * LOG2_E
    width = rate.shape[1]
    tiles = width // 128
    blocks = step_ref.shape[0] // 8

    @pl.when(pl.program_id(0) == 0)
    def _():
        d_in_ref[...] = jnp.zeros(d_in_ref.shape, jnp.float32)
        d_out_ref[...] = jnp.zeros(d_out_ref.shape, jnp.float32)

    def folded(a):
        total = a[:, :128]
        for j in range(1, tiles):
            total = total + a[:, j * 128 : (j + 1) * 128]
        return total

    states_ref[0] = start_ref[...]

    def forward(k, state):
        base = pl.multiple_of(k * 8, 8)
        step, conv = step_ref[pl.ds(base, 8), :], conv_ref[pl.ds(base, 8), :]
        d_scan = d_scan_ref[pl.ds(base, 8), :]
        drive = step * conv
        for i in range(8):
            decay = jnp.exp2(step[i : i + 1] * rate)
            in_now = jnp.tile(in_ref[base + i], (1, tiles))
            state = decay * state + in_now * drive[i : i + 1]
            decays_ref[base + i] = decay
            states_ref[base + i + 1] = state
            d_out_ref[base + i] += folded(d_scan[i : i + 1] * state)
        return state

    lax.fori_loop(0, blocks, forward, start_ref[...])

    def backward(k, carried):
        carry, d_rate = carried
        base = pl.multiple_of((blocks - 1 - k) * 8, 8)
        step, conv = step_ref[pl.ds(base, 8), :], conv_ref[pl.ds(base, 8), :]
        d_scan = d_scan_ref[pl.ds(base, 8), :]
        drive = step * conv
        through_rate, through_drive = [], []
        for i in range(7, -1, -1):
            in_now = jnp.tile(in_ref[base + i], (1, tiles))
            out_now = jnp.tile(out_ref[base + i], (1, tiles))
            adjoint = out_now * d_scan[i : i + 1] + carry
            carry = decays_ref[base + i] * adjoint
            before = carry * states_ref[base + i]
            d_rate = d_rate + before * step[i : i + 1]
            through_rate.append(jnp.sum(true_rate * before, axis=0, keepdims=True))
            through_drive.append(jnp.sum(adjoint * in_now, axis=0, keepdims=True))
            d_in_ref[base + i] += folded(adjoint * drive[i : i + 1])
        by_rate = jnp.concatenate(through_rate[::-1], axis=0)
        by_drive = jnp.concatenate(through_drive[::-1], axis=0)
        d_step_ref[pl.ds(base, 8), :] = by_rate + by_drive * conv
        d_conv_ref[pl.ds(base, 8), :] = by_drive * step
        return carry, d_rate

    zero = jnp.zeros(rate.shape, jnp.float32)
    d_rate_ref[...] = lax.fori_loop(0, blocks, backward, (d_end_ref[...], zero))[1]


def scan_specs(rows, states):
    tokens = pl.BlockSpec((rows, SCAN_TILE), lambda i: (0, i))
    maps = pl.BlockSpec((rows, states, 128), lambda i: (0, 0, 0))
    state = pl.BlockSpec((states, SCAN_TILE), lambda i: (0, i))
    return tokens, maps, state


def scan_call(kernel, operands, in_kinds, outs, out_kinds, scratch=(), flops=8, exps=1):
    rows, channels = operands[0].shape
    states = 16
    kinds = dict(zip("tms", scan_specs(rows, states)))
    shapes = {"t": (rows, channels), "m": (rows, states, 128), "s": (states, channels)}
    work = rows * states * channels
    return pl.pallas_call(
        kernel,
        grid=(channels // SCAN_TILE,),
        in_specs=[kinds[k] for k in in_kinds],
        out_specs=[kinds[k] for k in out_kinds],
        out_shape=[jax.ShapeDtypeStruct(shapes[k], jnp.float32) for k in out_kinds],
        scratch_shapes=scratch,
        compiler_params=pltpu.CompilerParams(
            dimension_semantics=("arbitrary",), vmem_limit_bytes=(36 if scratch else 16) * 2**20
        ),
        cost_estimate=pl.CostEstimate(
            flops=work * flops, bytes_accessed=4 * rows * channels * 4, transcendentals=work * exps
        ),
    )(*operands)


def lanes(a):
    return jnp.broadcast_to(a[:, :, None], (*a.shape, 128))


def scan_state(step_size, drive, in_lanes, decay_rate):
    return scan_call(scan_state_kernel, (step_size, drive, in_lanes, decay_rate), "ttms", 1, "s")[0]


def scan_full(step_size, drive, in_lanes, out_lanes, decay_rate, state_in):
    operands = (step_size, drive, in_lanes, out_lanes, decay_rate, state_in)
    return scan_call(scan_full_kernel, operands, "ttmmss", 1, "t")[0]


def adjoint_state(step_size, d_scan, out_lanes, decay_rate):
    return scan_call(adjoint_state_kernel, (step_size, d_scan, out_lanes, decay_rate), "ttms", 1, "s")[0]


def scan_back(step_size, conv_values, d_scan, in_lanes, out_lanes, decay_rate, state_in, d_end):
    rows, states = step_size.shape[0], decay_rate.shape[0]
    scratch = (
        pltpu.VMEM((rows + 1, states, SCAN_TILE), jnp.float32),
        pltpu.VMEM((rows, states, SCAN_TILE), jnp.float32),
    )
    operands = (step_size, conv_values, d_scan, in_lanes, out_lanes, decay_rate, state_in, d_end)
    d_step, d_conv, d_rate, d_in, d_out = scan_call(
        scan_back_kernel, operands, "tttmmsss", 5, "ttsmm", scratch, flops=24
    )
    return d_step, d_conv, d_rate, jnp.sum(d_in, axis=-1), jnp.sum(d_out, axis=-1)


SCORE_SCALE = 1.0 / math.sqrt(HEAD_DIM)
GROUP = HEADS // KV_HEADS


def attend_kernel(q_ref, window_ref, bias_ref, out_ref, total_ref):
    keys, values = window_ref[:, :HEAD_DIM], window_ref[:, HEAD_DIM:]
    for h in range(GROUP):
        lanes = slice(h * HEAD_DIM, (h + 1) * HEAD_DIM)
        scores = dot_nt(q_ref[0, :, lanes], keys) * SCORE_SCALE + bias_ref[...]
        top = jnp.max(scores, axis=1, keepdims=True)
        weights = jnp.exp(scores - top)
        total = jnp.sum(weights, axis=1, keepdims=True)
        low = (weights * (1.0 / total)).astype(jnp.bfloat16)
        out_ref[0, :, lanes] = dot_nn(low, values).astype(out_ref.dtype)
        total_ref[0, :, h : h + 1] = top + jnp.log(total)


def attend_back_kernel(q_ref, window_ref, bias_ref, total_ref, d_ref, dq_ref, d_window_ref):
    keys, values = window_ref[:, :HEAD_DIM], window_ref[:, HEAD_DIM:]
    d_keys = d_values = 0.0
    for h in range(GROUP):
        lanes = slice(h * HEAD_DIM, (h + 1) * HEAD_DIM)
        queries, d_heads = q_ref[0, :, lanes], d_ref[0, :, lanes]
        weights = jnp.exp(dot_nt(keys, queries) * SCORE_SCALE + bias_ref[...] - total_ref[0, h : h + 1, :])
        d_weights = dot_nt(values, d_heads)
        through = jnp.sum(weights * d_weights, axis=0, keepdims=True)
        d_scores = (weights * (d_weights - through)).astype(jnp.bfloat16)
        d_values = d_values + dot_nn(weights.astype(jnp.bfloat16), d_heads)
        d_keys = d_keys + dot_nn(d_scores, queries)
        dq_ref[0, :, lanes] = (dot_tn(d_scores, keys) * SCORE_SCALE).astype(dq_ref.dtype)
    d_window_ref[:, :HEAD_DIM] = (d_keys * SCORE_SCALE).astype(d_window_ref.dtype)
    d_window_ref[:, HEAD_DIM:] = d_values.astype(d_window_ref.dtype)


def attend_call(kernel, operands, kinds, outs, out_kinds, rows, span, products):
    groups = pl.BlockSpec((1, rows, GROUP * HEAD_DIM), lambda i: (i, 0, 0))
    window = pl.BlockSpec((span, 2 * HEAD_DIM), lambda i: (0, i))
    specs = {"q": groups, "w": window}
    for a in (*operands, *outs):
        specs[a.shape] = pl.BlockSpec(a.shape, lambda i: (0, 0)) if len(a.shape) == 2 else pl.BlockSpec((1, *a.shape[1:]), lambda i: (i, 0, 0))
    return pl.pallas_call(
        kernel,
        grid=(KV_HEADS,),
        in_specs=[specs[k if k in specs else a.shape] for k, a in zip(kinds, operands)],
        out_specs=[specs[k if k in specs else a.shape] for k, a in zip(out_kinds, outs)],
        out_shape=outs,
        compiler_params=pltpu.CompilerParams(
            dimension_semantics=("arbitrary",), vmem_limit_bytes=24 * 2**20
        ),
        cost_estimate=pl.CostEstimate(
            flops=2 * products * HEADS * rows * span * HEAD_DIM, bytes_accessed=4 * rows * span, transcendentals=HEADS * rows * span
        ),
    )(*operands)


def by_groups(a):
    return a.reshape(a.shape[0], KV_HEADS, GROUP * HEAD_DIM).transpose(1, 0, 2)


def from_groups(a):
    return a.transpose(1, 0, 2).reshape(a.shape[1], HEADS * HEAD_DIM)


def attend(queries, window, bias):
    rows, span = queries.shape[1], window.shape[0]
    outs = [
        jax.ShapeDtypeStruct(queries.shape, jnp.bfloat16),
        jax.ShapeDtypeStruct((KV_HEADS, rows, 8), jnp.float32),
    ]
    return attend_call(attend_kernel, (queries, window, bias), "qwb", outs, "qt", rows, span, 2)


def attend_back(queries, window, bias_t, totals, d_heads):
    rows, span = queries.shape[1], window.shape[0]
    outs = [
        jax.ShapeDtypeStruct(queries.shape, jnp.bfloat16),
        jax.ShapeDtypeStruct(window.shape, jnp.bfloat16),
    ]
    operands = (queries, window, bias_t, totals.transpose(0, 2, 1), d_heads)
    return attend_call(attend_back_kernel, operands, "qwbtq", outs, "qw", rows, span, 5)


def shards(
    inputs,
    segment_ids,
    out_grad,
    norm_gain,
    w_query,
    w_key,
    w_value,
    w_attn_out,
    w_mamba_in,
    conv_weight,
    conv_bias,
    w_select,
    w_step,
    step_bias,
    log_decay,
    skip_gain,
    w_mamba_out,
    attn_gain,
    mamba_gain,
    ffn_norm_gain,
    w_gate,
    w_up,
    w_down,
):
    rows_dev, width = inputs.shape[1:]
    inner = conv_weight.shape[1]
    edge_count = conv_weight.shape[0] - 1
    rank_width = RANK
    state_width = log_decay.shape[0]
    reach_blocks = WINDOW // rows_dev
    group_size = HEADS // KV_HEADS
    score_scale = 1.0 / math.sqrt(HEAD_DIM)
    position = lax.axis_index(HEAD_BLK)
    core = lax.axis_index("head")
    first_core = core == 0
    tokens = inputs[0].astype(jnp.float32)

    d_rows = w_query.shape[0]
    c_rows = w_select.shape[0]
    sel_half, step_half = w_select.shape[1], w_step.shape[1]
    mamba_in = w_mamba_in
    cut_a, cut_b = 1408, 2816
    mixed_c = inner - cut_b
    planes = gather_planes(
        (
            mamba_in[:, :cut_a],
            mamba_in[:, cut_a:cut_b],
            jnp.concatenate([mamba_in[:, cut_b:], w_query, w_key, w_value], axis=1),
        ),
        ORDERS,
    )
    parts = [ring_pieces(a, order[1]) for a, order in zip(planes, ORDERS)]
    half_width = width // 2
    windows_in = [(0, a[0].shape[1]) for a in parts]
    windows_out_a, window_out_b = ((0, half_width), (half_width, 2 * half_width)), (0, half_width)
    select_step = jnp.pad(
        jnp.concatenate([w_select, w_step], axis=1), ((0, 0), (0, 128 - sel_half - step_half))
    )
    select_mine = shown(after(select_step, planes[2]), BLK_SEQ).reshape(inner, 128)
    select_got = other_core(select_mine)
    select_full = join_columns(select_mine[:, :sel_half], select_got[:, :sel_half])
    step_full = join_columns(
        select_mine[:, sel_half : sel_half + step_half], select_got[:, sel_half : sel_half + step_half]
    )

    out_shards = (jnp.concatenate([w_mamba_out[:d_rows], w_mamba_out[d_rows:]], axis=1), w_attn_out)
    out_planes = [
        gathered(after(out_shards[0], planes[0]), ORDER_A[0]),
        *gather_planes(out_shards[1:], ORDERS[1:2], (select_mine,)),
    ]

    ff_rows = w_down.shape[0]

    def to_units(w):
        split = w.reshape(d_rows, 4, 4, 2, ff_rows).transpose(2, 0, 1, 3, 4)
        return jnp.pad(split, ((0, 0),) * 4 + ((0, FF_PAD - ff_rows),)).reshape(4, d_rows, 8 * FF_PAD)

    def from_units(g):
        split = g.reshape(4, d_rows, 4, 2, FF_PAD)[..., :ff_rows]
        return split.transpose(1, 2, 0, 3, 4).reshape(d_rows, 32 * ff_rows)

    units = 8 * FF_PAD
    gate_up = jnp.concatenate([to_units(w_gate), to_units(w_up)], axis=2)
    gate_up_dealt = dealt(after(gate_up, out_planes[1]), Z_RING).reshape(4 * d_rows, 2 * units)
    gate_up = gathered(jnp.pad(gate_up_dealt, ((0, LANES // 16 - 4 * d_rows), (0, 0))), ("xh", "y", "xl"))

    here = lax.axis_index("xh") == core
    down = jnp.pad(w_down, ((0, FF_PAD - ff_rows), (0, 0)))
    down = join_columns(down, other_core(down))
    down = jnp.where(here, down, received(down, "xh", 1))
    down_shard = down
    down = gathered(down, ("y", "xl"))

    def group_tokens(a):
        return both_tokens(ring_whole(a, Z_RING))

    def group_sum(both):
        return ring_sum_whole(to_low(sum_cores(both)), Z_RING)

    grad_out = out_grad[0]

    pick_a, pick_b, pick_c = (picker(order, d_rows) for order in ORDERS)
    pick_ff = ff_picker(d_rows)
    pick_out = [picker(ORDER_A, d_rows, c_rows, k * d_rows) for k in (0, 1)]

    normed, norm_back = jax.vjp(rms_scale, tokens, norm_gain)
    normed_chip = both_tokens(to_low(normed))
    normed_a, normed_b, normed_c = turned((normed_chip,) * 3, (pick_a, pick_b, pick_c))
    normed_c = after(normed_c, gate_up_dealt, down_shard)

    q_cols, k_cols = w_query.shape[1], w_key.shape[1]
    projected = [
        by_pieces((left,), pieces, (window,))
        for left, pieces, window in zip((normed_a, normed_b, normed_c), parts, windows_in)
    ]
    mixed_mine = jnp.concatenate([a[:rows_dev] for a in projected], axis=1)
    mixed_got = other_core(jnp.concatenate([a[rows_dev:] for a in projected], axis=1))
    conv_in = jnp.where(first_core, mixed_mine[:, :inner], mixed_got[:, :inner])
    gate_z = jnp.where(first_core, mixed_got[:, :inner], mixed_mine[:, :inner]).astype(jnp.float32)
    qkv_cols = q_cols + 2 * k_cols
    qkv_mine, qkv_got = (a[:, inner : inner + qkv_cols] for a in (mixed_mine, mixed_got))
    queries = join_columns(qkv_mine[:, :q_cols], qkv_got[:, :q_cols])
    keys_low = join_columns(qkv_mine[:, q_cols : q_cols + k_cols], qkv_got[:, q_cols : q_cols + k_cols])
    values_low = join_columns(qkv_mine[:, q_cols + k_cols :], qkv_got[:, q_cols + k_cols :])
    key_value = jnp.stack([a.reshape(rows_dev, KV_HEADS, HEAD_DIM) for a in (keys_low, values_low)], axis=2)
    key_value = key_value.reshape(rows_dev, 2 * KV_HEADS * HEAD_DIM)

    mamba_out_a, attn_out_b = (
        ring_pieces(after(a, conv_in), order[1]) for a, order in zip(out_planes, ORDERS)
    )
    grad_out_group = group_tokens(jnp.pad(after(grad_out, conv_in), ((0, 0), (0, LANES - width))))

    along_z = lax.axis_index(Z_RING)
    kv_cols = KV_HEADS * HEAD_DIM
    row = ring_in_order(key_value, Z_RING).reshape(4, rows_dev, 2 * kv_cols)
    edge_rows = after(shifted(conv_in[rows_dev - edge_count :], 1), row)
    window = jnp.concatenate([shifted(row, 2, ROWS), shifted(row, 1, ROWS), row])
    window = lax.dynamic_slice_in_dim(window, along_z, reach_blocks + 1).reshape(-1, key_value.shape[1])

    padded_in = jnp.concatenate([edge_rows, conv_in], axis=0).astype(jnp.float32)
    conved, conv_back = jax.vjp(conv_silu, padded_in, conv_weight, conv_bias)
    conved_low = to_low(conved)
    conv_values = conved_low.astype(jnp.float32)
    selected = product(conved_low, select_full)
    step_raw = to_low(selected[:, :rank_width])
    in_mat = selected[:, rank_width : rank_width + state_width]
    out_mat = selected[:, rank_width + state_width :]
    step_pre = product_nt(step_raw, step_full)
    (step_size, decay_rate), rate_back = jax.vjp(rate_piece, step_pre, step_bias, log_decay)
    total_step = jnp.sum(step_size, axis=0)
    drive = step_size * conv_values
    in_lanes, out_lanes = lanes(in_mat), lanes(out_mat)
    end_state = scan_state(step_size, drive, in_lanes, decay_rate)
    queries = after(queries, end_state)
    state_in = chain_carry(total_step, end_state, decay_rate, False)
    scan_out = scan_full(step_size, drive, in_lanes, out_lanes, decay_rate, state_in)
    gated, gate_back = jax.vjp(gate_piece, scan_out, conv_values, gate_z, skip_gain)
    gated_low = after(to_low(gated), grad_out_group)

    span_keys = (reach_blocks + 1) * rows_dev
    segment_row = segment_ids[0]
    padded_segs = jnp.concatenate(
        [jnp.full((reach_blocks * rows_dev,), -1, jnp.int32), segment_row]
    )
    key_segs = lax.dynamic_slice_in_dim(padded_segs, position * rows_dev, span_keys)
    query_segs = lax.dynamic_slice_in_dim(segment_row, position * rows_dev, rows_dev)
    gaps = (reach_blocks * rows_dev + jnp.arange(rows_dev, dtype=jnp.int32))[:, None] - jnp.arange(
        span_keys, dtype=jnp.int32
    )[None, :]
    allowed = (gaps >= 0) & (gaps < WINDOW) & (query_segs[:, None] == key_segs[None, :])
    queries_by_group = by_groups(queries)
    heads_by_group, score_totals = attend(queries_by_group, window, jnp.where(allowed, 0.0, -1e30))
    heads_low = from_groups(heads_by_group)

    heads_b, *gated_a = (
        both_tokens(a) for a in turned((heads_low, gated_low, gated_low), (pick_b, *pick_out))
    )
    branch_out = jnp.concatenate(
        [
            by_pieces((heads_b,), attn_out_b, (window_out_b,), False),
            by_pieces(gated_a, mamba_out_a, windows_out_a, False),
        ],
        axis=1,
    )
    out_mine, out_got = branch_out[:rows_dev], other_core(branch_out[rows_dev:])
    attn_out = join_columns(out_mine[:, :half_width], out_got[:, :half_width])
    mamba_out = join_columns(out_mine[:, half_width:], out_got[:, half_width:])
    hidden_mid, merge_back = jax.vjp(
        merge_piece, tokens, attn_out, mamba_out, attn_gain, mamba_gain
    )
    normed_two, norm_two_back = jax.vjp(rms_scale, hidden_mid, ffn_norm_gain)
    normed_two_ff = group_tokens(turned((to_low(normed_two),), (pick_ff,))[0])
    act_low, d_gate_up, down_part, d_part = feed_forward(normed_two_ff, grad_out_group, gate_up, down)
    d_cores = to_low(sum_cores(d_part))
    d_normed_two = ring_sum_whole(d_cores, Z_RING)
    act_low, d_gate_up = together((act_low, d_gate_up, d_cores))[:2]
    grad_gate_up, grad_down = feed_grads(normed_two_ff, d_gate_up, act_low, grad_out_group)

    gate_up_sum = scattered(grad_gate_up, ("xh", "y", "xl"))[: 4 * d_rows].reshape(4, d_rows, 2 * units)
    gate_up_sum = dealt(gate_up_sum, Z_RING).astype(jnp.float32)
    grad_gate, grad_up = from_units(gate_up_sum[..., :units]), from_units(gate_up_sum[..., units:])
    grad_down = scattered(grad_down, ("y", "xl")).astype(jnp.float32)
    grad_down = grad_down + received(to_low(grad_down), "xh", 1).astype(jnp.float32)
    down_l, down_r = grad_down[:ff_rows, :half_width], grad_down[:ff_rows, half_width:]
    down_got = other_core(to_low(jnp.where(first_core, down_r, down_l))).astype(jnp.float32)
    grad_down = jnp.where(here, jnp.where(first_core, down_l, down_r), down_got)

    d_mid_norm, grad_ffn_norm = norm_two_back(turned_back((d_normed_two,), (pick_ff,), False)[0])
    d_mid = grad_out.astype(jnp.float32) + d_mid_norm
    d_tokens_res, d_attn_out, d_mamba_out, grad_attn_gain, grad_mamba_gain = merge_back(d_mid)
    d_attn_low, d_mamba_low = to_low(d_attn_out), to_low(d_mamba_out)
    d_branch = jnp.concatenate(
        [d_attn_low[:, :half_width], d_mamba_low[:, :half_width], d_attn_low[:, half_width:], d_mamba_low[:, half_width:]],
        axis=1,
    )
    d_branch_half = own_columns(d_branch)
    d_attn_half, d_mamba_half = d_branch_half[:, :half_width], d_branch_half[:, half_width:]
    d_gated_a = by_pieces_nt((d_mamba_half, d_mamba_half), mamba_out_a, windows_out_a)
    d_heads_b = by_pieces_nt((d_attn_half,), attn_out_b, (window_out_b,))
    d_branch = to_low(sum_cores(jnp.concatenate([*d_gated_a, *d_heads_b], axis=1)))
    d_gated_a, d_heads_b = [d_branch[:, k * LANES : (k + 1) * LANES] for k in (0, 1)], d_branch[:, 2 * LANES :]
    d_gated = turned_back(d_gated_a, pick_out, False, True, inner)[0]
    d_heads = turned_back((d_heads_b,), (pick_b,), True)[0]

    d_scan, d_conv_gate, d_gate_z, grad_skip = gate_back(d_gated)
    d_state_in = adjoint_state(step_size, d_scan, out_lanes, decay_rate)
    d_heads, d_attn_half, d_mamba_half, down_part = together(
        (d_heads, d_attn_half, d_mamba_half, down_part, d_state_in)
    )[:4]
    output = to_low(hidden_mid + group_sum(down_part)[:, :width])[None]

    d_queries, d_window = attend_back(
        queries_by_group, window, jnp.where(allowed.T, 0.0, -1e30), score_totals, by_groups(d_heads)
    )
    d_queries = from_groups(d_queries)
    d_rows_z = jnp.zeros((12, rows_dev, d_window.shape[1]), jnp.bfloat16)
    d_rows_z = lax.dynamic_update_slice_in_dim(
        d_rows_z, d_window.reshape(reach_blocks + 1, rows_dev, -1), along_z, 0
    )
    d_row = (
        d_rows_z[8:].astype(jnp.float32)
        + shifted(d_rows_z[4:8], -1, ROWS).astype(jnp.float32)
        + shifted(d_rows_z[:4], -2, ROWS).astype(jnp.float32)
    )
    d_key_value = ring_sum_in_order(to_low(d_row).reshape(4 * rows_dev, 2 * kv_cols), Z_RING)
    d_key_value = to_low(d_key_value).reshape(rows_dev, KV_HEADS, 2, HEAD_DIM)
    d_keys, d_values = (d_key_value[:, :, k].reshape(rows_dev, kv_cols) for k in (0, 1))

    kv_half = kv_cols // 2
    d_qkv_half = own_columns(
        jnp.concatenate(
            [
                d_queries[:, :q_cols],
                d_keys[:, :kv_half],
                d_values[:, :kv_half],
                d_queries[:, q_cols:],
                d_keys[:, kv_half:],
                d_values[:, kv_half:],
            ],
            axis=1,
        )
    )
    rings = sum_rings(
        (grad_pieces(gated_a, d_mamba_half, HALVES), grad_pieces((heads_b,), d_attn_half, HALVES)), ORDERS[:2]
    )

    d_end = chain_carry(total_step, d_state_in, decay_rate, True)
    d_step, d_conv_scan, d_rate, d_in_mat, d_out_mat = scan_back(
        step_size, conv_values, d_scan, in_lanes, out_lanes, decay_rate, state_in, d_end
    )
    d_step_pre, grad_step_bias, grad_log_decay = rate_back((d_step, d_rate))
    d_step_low = to_low(d_step_pre)
    grad_step_w = product_tn(d_step_low, step_raw)
    d_step_raw = product(d_step_low, step_full)
    d_selected = to_low(jnp.concatenate([d_step_raw, d_in_mat, d_out_mat], axis=1))
    grad_select = product_tn(conved_low, d_selected)
    d_conved = product_nt(d_selected, select_full) + d_conv_gate + d_conv_scan
    d_padded, grad_conv_w, grad_conv_b = conv_back(d_conved)
    edge_back = shifted(to_low(d_padded[:edge_count]), -1).astype(jnp.float32)
    d_conv_in = d_padded[edge_count:] + jnp.concatenate(
        [jnp.zeros((rows_dev - edge_count, inner), jnp.float32), edge_back], axis=0
    )
    d_mixed_half = own_columns(to_low(jnp.concatenate([d_conv_in, d_gate_z], axis=1)))
    d_mixed_a, d_mixed_b, d_mixed_c = (
        d_mixed_half[:, :cut_a],
        d_mixed_half[:, cut_a:cut_b],
        jnp.concatenate([d_mixed_half[:, cut_b:], d_qkv_half], axis=1),
    )

    pieces = [
        grad_pieces((left,), grad, HALVES)
        for left, grad in ((normed_a, d_mixed_a), (normed_b, d_mixed_b), (normed_c, d_mixed_c))
    ]
    d_mixed_a, d_mixed_b, d_mixed_c = together((d_mixed_a, d_mixed_b, d_mixed_c, *(p[0] for p in pieces)))[:3]
    ring_a, ring_b, ring_c = sum_rings(pieces, ORDERS)
    d_normed = turned_back(
        [
            by_pieces_nt((grad,), pieces, (window,))[0]
            for grad, pieces, window in zip((d_mixed_a, d_mixed_b, d_mixed_c), parts, windows_in)
        ],
        (pick_a, pick_b, pick_c),
        False,
        True,
    )[0]
    d_tokens_norm, grad_norm = norm_back(sum_cores(d_normed))
    input_grad = to_low(d_tokens_res + d_tokens_norm)[None]

    smalls = (
        grad_norm,
        grad_conv_w,
        grad_conv_b,
        grad_step_bias,
        grad_log_decay,
        grad_skip,
        grad_attn_gain,
        grad_mamba_gain,
        grad_ffn_norm,
    )
    channel_rows = [a.reshape(-1, inner) for a in smalls[1:6]]
    gains = jnp.concatenate([*smalls[6:], jnp.zeros((width,), jnp.float32)]).reshape(-1, inner)
    select_rows = jnp.stack(
        [
            jnp.pad(jnp.concatenate([sel, stp], axis=1), ((0, 0), (0, 128 - sel_half - step_half)))
            for sel, stp in zip(jnp.split(grad_select, 2, axis=1), jnp.split(grad_step_w, 2, axis=1))
        ]
    )
    select_rows = select_rows.reshape(128, c_rows, 128)
    small_rows = jnp.concatenate([gains, *channel_rows])
    small_part, select_sum = sum_parts(small_rows, select_rows)
    totals, norm_sum = show_parts(small_part, small_rows.shape, grad_norm)
    gain_sums = totals[: gains.shape[0]].reshape(4, width)
    at, channel_sums = gains.shape[0], []
    for a in channel_rows:
        channel_sums.append(totals[at : at + a.shape[0]])
        at += a.shape[0]
    totals = [
        norm_sum,
        channel_sums[0],
        *(channel_sums[k][0] for k in (1, 2)),
        channel_sums[3],
        channel_sums[4][0],
        *gain_sums[:3],
    ]
    ring_a, ring_b, ring_c, select_sum = together((ring_a, ring_b, ring_c, select_sum))
    grad_select, grad_step = select_sum[:, :sel_half], select_sum[:, sel_half : sel_half + step_half]
    sum_a, sum_b, sum_c = sum_planes(
        [jnp.concatenate([ring_a, rings[0]], axis=1), jnp.concatenate([ring_b, rings[1]], axis=1), ring_c], ORDERS
    )
    sum_a, out_sum_a = sum_a[:, :cut_a], sum_a[:, cut_a:]
    sum_b, grad_attn_out = sum_b[:, : cut_b - cut_a], sum_b[:, cut_b - cut_a :]
    grad_mamba_out = jnp.concatenate([out_sum_a[:, :half_width], out_sum_a[:, half_width:]], axis=0)
    grad_mamba_in = jnp.concatenate([sum_a, sum_b, sum_c[:, :mixed_c]], axis=1)
    grad_qkv = sum_c[:, mixed_c:]
    grad_query = grad_qkv[:, :q_cols]
    grad_key, grad_value = grad_qkv[:, q_cols : q_cols + k_cols], grad_qkv[:, q_cols + k_cols :]


    return (
        output,
        input_grad,
        totals[0],
        grad_query,
        grad_key,
        grad_value,
        grad_attn_out,
        grad_mamba_in,
        totals[1],
        totals[2],
        grad_select,
        grad_step,
        totals[3],
        totals[4],
        totals[5],
        grad_mamba_out,
        totals[6],
        totals[7],
        totals[8],
        grad_gate,
        grad_up,
        grad_down,
    )


def solution(mesh):
    torus = Mesh(
        mesh.devices.reshape(mesh.shape["head"], 2, 4, 4, mesh.shape["seq"]),
        ("head", "xh", "y", "z", "xl"),
    )
    weight = P(BLK_SEQ, "head")
    rows = P("xl", HEAD_BLK, None)
    in_specs = (rows, P("xl", None), rows, P()) + (weight,) * 5
    in_specs += (P(), P(), weight, weight, P(), P(), P(), weight, P(), P(), P()) + (weight,) * 3
    out_specs = (rows, rows, P()) + (weight,) * 5
    out_specs += (P(), P(), weight, weight, P(), P(), P(), weight, P(), P(), P()) + (weight,) * 3
    return jax.shard_map(
        shards, mesh=torus, in_specs=in_specs, out_specs=out_specs, check_vma=False
    )
```
